256 devices in a mesh: orb: 64 (over z, x, core), grp: 4 (over y).
Axes of the slice: x: 4, y: 4, z: 8, core: 2. Of those that a mesh axis runs over, the one named last changes fastest.
Arguments:
- orbitals: float32 [256, 262144], P(('orb', 'grp')), may hold values from -10 to 10
- potential: float32 [4096, 64], replicated, may hold values from -2 to 2
- occupation: float32 [256], replicated, may hold values from 0.5 to 2
- region_bounds: int32 [256, 2], replicated, may hold values from 0 to 64, as said below
Outputs:
- orthonormal: float32 [256, 262144], P(('orb', 'grp'))
- gradient: float32 [256, 262144], P(('orb', 'grp'))
- subspace: float32 [256, 256], replicated
- density: float32 [4096, 64], P(('orb', 'grp'))
The draws below stay inside these ranges and needn't reach their ends.
Inputs may be any that keep to these rules, and one draw needn't show every extreme that they name: Orbital i's region is planes region_bounds[i,0] to region_bounds[i,1] - 1, at least 16 planes.
All inputs are finite; a program needn't handle non-finite values.
Results may differ from the reference program's by a relative error of at most 0.0003.
Values sent between devices are 32-bit elements; how exact they have to be, the bound alone decides.
No kernel may reach another device: no remote copies, remote signals or barrier semaphores. Data moves between devices by JAX's collectives and lax.ppermute only.
A program may use at most 128 MiB of HBM per device.

```python
import math
import jax
import jax.numpy as jnp
from jax import lax

G = 64
NORB = 256
CELLS = 262144


def draw_orbitals(key, part):
    key = jax.random.fold_in(key, 5)
    first_key, second_key = jax.random.split(key)
    independent = jnp.clip(jax.random.normal(first_key, (NORB, CELLS), jnp.float32), -6.0, 6.0)
    coupling = jax.random.uniform(second_key, (NORB, 1), jnp.float32, -0.6, 0.6)
    return independent + coupling * jnp.roll(independent, -1, axis=0)


def draw_region_bounds(key, part):
    key = jax.random.fold_in(key, 11)
    first_key, second_key = jax.random.split(key)
    length = jax.random.randint(first_key, (NORB,), G // 4, G + 1).astype(jnp.int32)
    length = length.at[0].set(G).at[1].set(G // 4)
    lowest = jax.random.randint(second_key, (NORB,), 0, 4 * G).astype(jnp.int32) % (G - length + 1)
    return jnp.stack([lowest, lowest + length], axis=1).astype(jnp.int32)


def setup_inputs(seed: int = 0) -> dict:
    key_list = jax.random.split(jax.random.key(seed), 5)
    orbitals = draw_orbitals(jax.random.fold_in(key_list[4], 71), 0)
    potential = jnp.clip(jax.random.uniform(key_list[1], (G * G, G), jnp.float32, -2.0, 2.0), -2.0, 2.0)
    occupation = jnp.clip(jnp.exp(jax.random.uniform(key_list[2], (NORB,), jnp.float32, math.log(0.5), math.log(2.0))), 0.5, 2.0)
    region_bounds = draw_region_bounds(jax.random.fold_in(key_list[4], 71), 0)
    return {"orbitals": orbitals, "potential": potential, "occupation": occupation, "region_bounds": region_bounds}


magic_taps = (0.0028, -0.0236, 0.1026, 0.8364, 0.1026, -0.0236, 0.0028)
kinetic_taps = (-1.0 / 560.0, 8.0 / 315.0, -0.2, 1.6, -205.0 / 72.0, 1.6, -0.2, 8.0 / 315.0, -1.0 / 560.0)
precise = lax.Precision.HIGHEST

def solve_triangular(factor, rhs):
    return lax.linalg.triangular_solve(factor, rhs, left_side=True, lower=True)

def banded(extent, taps):
    radius = len(taps) // 2
    offset = jnp.arange(extent, dtype=jnp.int32)[None, :] - jnp.arange(extent, dtype=jnp.int32)[:, None]
    matrix = jnp.zeros((extent, extent), jnp.float32)
    for position, weight in enumerate(taps):
        matrix = matrix + jnp.where(offset == position - radius, jnp.float32(weight), jnp.float32(0.0))
    return matrix

def along_axis(values, matrix, which):
    if which == 1:
        return jnp.einsum('rc,ncyz->nryz', matrix, values, precision=precise)
    if which == 2:
        return jnp.einsum('rc,nxcz->nxrz', matrix, values, precision=precise)
    return jnp.einsum('rc,nxyc->nxyr', matrix, values, precision=precise)

def separable(values, matrix):
    return along_axis(along_axis(along_axis(values, matrix, 1), matrix, 2), matrix, 3)

def hamiltonian(values, grid_potential, magic_matrix, kinetic_matrix):
    realspace = separable(values, magic_matrix)
    weighted = separable(realspace * grid_potential[None], magic_matrix)
    laplace = along_axis(values, kinetic_matrix, 1) + along_axis(values, kinetic_matrix, 2) + along_axis(values, kinetic_matrix, 3)
    return (weighted - 0.5 * laplace, realspace)

def reference(orbitals, potential, occupation, region_bounds):
    orbital_total = orbitals.shape[0]
    cell_total = orbitals.shape[1]
    width_block = 8
    magic_matrix = banded(G, magic_taps)
    kinetic_matrix = banded(G, kinetic_taps)
    grid_potential = potential.reshape(G, G, G)
    planes = jnp.arange(G, dtype=jnp.int32)
    region_mask = ((planes[None, :] >= region_bounds[:, 0:1]) & (planes[None, :] < region_bounds[:, 1:2])).astype(jnp.float32)

    def accumulate(density_sum, pieces):
        orbital_block, mask_block, occupation_block = pieces
        values = orbital_block.reshape(width_block, G, G, G) * mask_block[:, :, None, None]
        applied, realspace = hamiltonian(values, grid_potential, magic_matrix, kinetic_matrix)
        density_sum = density_sum + jnp.sum(occupation_block[:, None, None, None] * realspace * realspace, axis=0)
        return (density_sum, (values.reshape(width_block, cell_total), applied.reshape(width_block, cell_total)))
    steps_count = orbital_total // width_block
    density_sum, (masked, images) = lax.scan(accumulate, jnp.zeros((G, G, G), jnp.float32), (orbitals.reshape(steps_count, width_block, cell_total), region_mask.reshape(steps_count, width_block, G), occupation.reshape(steps_count, width_block)))
    masked = masked.reshape(orbital_total, cell_total)
    images = images.reshape(orbital_total, cell_total)
    density = (density_sum / orbital_total).reshape(G * G, G)
    intersection = jnp.dot(masked.astype(jnp.float32), masked.T.astype(jnp.float32), precision=precise, preferred_element_type=jnp.float32) / cell_total
    hamilton_matrix = jnp.dot(masked.astype(jnp.float32), images.T.astype(jnp.float32), precision=precise, preferred_element_type=jnp.float32) / cell_total
    factor = jnp.linalg.cholesky(intersection)
    orthonormal = solve_triangular(factor, masked)
    ortho_images = solve_triangular(factor, images)
    half_solved = solve_triangular(factor, hamilton_matrix)
    subspace = solve_triangular(factor, half_solved.T).T
    gradient = ortho_images - jnp.dot(subspace.astype(jnp.float32), orthonormal.astype(jnp.float32), precision=precise, preferred_element_type=jnp.float32)
    return (orthonormal, gradient, subspace, density)
```

```python
import jax
import jax.numpy as jnp
from jax import lax
from jax.sharding import PartitionSpec as P

G = 64


magic_taps = (0.0028, -0.0236, 0.1026, 0.8364, 0.1026, -0.0236, 0.0028)
kinetic_taps = (
    -1.0 / 560.0,
    8.0 / 315.0,
    -0.2,
    1.6,
    -205.0 / 72.0,
    1.6,
    -0.2,
    8.0 / 315.0,
    -1.0 / 560.0,
)
precise = lax.Precision.HIGHEST


def solve_triangular(factor, rhs):
    return lax.linalg.triangular_solve(factor, rhs, left_side=True, lower=True)


def banded(extent, taps):
    radius = len(taps) // 2
    offset = (
        jnp.arange(extent, dtype=jnp.int32)[None, :] - jnp.arange(extent, dtype=jnp.int32)[:, None]
    )
    matrix = jnp.zeros((extent, extent), jnp.float32)
    for position, weight in enumerate(taps):
        matrix = matrix + jnp.where(
            offset == position - radius, jnp.float32(weight), jnp.float32(0.0)
        )
    return matrix


def along_axis(values, matrix, which):
    if which == 1:
        return jnp.einsum("rc,ncyz->nryz", matrix, values, precision=precise)
    if which == 2:
        return jnp.einsum("rc,nxcz->nxrz", matrix, values, precision=precise)
    return jnp.einsum("rc,nxyc->nxyr", matrix, values, precision=precise)


def separable(values, matrix):
    return along_axis(along_axis(along_axis(values, matrix, 1), matrix, 2), matrix, 3)


def hamiltonian(values, grid_potential, magic_matrix, kinetic_matrix):
    realspace = separable(values, magic_matrix)
    weighted = separable(realspace * grid_potential[None], magic_matrix)
    laplace = (
        along_axis(values, kinetic_matrix, 1)
        + along_axis(values, kinetic_matrix, 2)
        + along_axis(values, kinetic_matrix, 3)
    )
    return (weighted - 0.5 * laplace, realspace)


def on_device(orbitals, potential, occupation, region_bounds):
    orbitals_here = orbitals.shape[0]
    cell_total = orbitals.shape[1]
    orb_count = lax.axis_size("orb")
    grp_count = lax.axis_size("grp")
    device_total = orb_count * grp_count
    orbital_total = orbitals_here * device_total
    segment = cell_total // device_total
    position = lax.axis_index("orb") * grp_count + lax.axis_index("grp")
    first_orbital = position * orbitals_here
    my_bounds = lax.dynamic_slice_in_dim(region_bounds, first_orbital, orbitals_here, 0)
    my_occupation = lax.dynamic_slice_in_dim(occupation, first_orbital, orbitals_here, 0)
    planes = jnp.arange(G, dtype=jnp.int32)
    region_mask = (
        (planes[None, :] >= my_bounds[:, 0:1]) & (planes[None, :] < my_bounds[:, 1:2])
    ).astype(jnp.float32)
    magic_matrix = banded(G, magic_taps)
    kinetic_matrix = banded(G, kinetic_taps)
    values = orbitals.reshape(orbitals_here, G, G, G) * region_mask[:, :, None, None]
    applied, realspace = hamiltonian(
        values, potential.reshape(G, G, G), magic_matrix, kinetic_matrix
    )
    masked = values.reshape(orbitals_here, cell_total)
    images = applied.reshape(orbitals_here, cell_total)

    axes = ("orb", "grp")
    lanes = 128
    tile = (device_total, segment // lanes, lanes)

    def exchange(blocks):
        return lax.all_to_all(blocks, axes, split_axis=0, concat_axis=0, tiled=True)

    def sum_everywhere(matrix):
        rows = orbital_total // device_total
        parts = exchange(matrix.reshape(device_total, rows * orbital_total // lanes, lanes))
        own = jnp.sum(parts, axis=0, keepdims=True)
        spread = exchange(jnp.broadcast_to(own, parts.shape))
        return spread.reshape(orbital_total, orbital_total)

    partial_value = jnp.sum(my_occupation[:, None, None, None] * realspace * realspace, axis=0) / (
        orbital_total
    )
    density = jnp.sum(exchange(partial_value.reshape(tile)), axis=0).reshape(-1, G)
    seg_psi = exchange(masked.reshape(tile)).reshape(orbital_total, segment)
    seg_images = exchange(images.reshape(tile)).reshape(orbital_total, segment)
    intersection = (
        sum_everywhere(
            jnp.dot(seg_psi, seg_psi.T, precision=precise, preferred_element_type=jnp.float32)
        )
        / cell_total
    )
    hamilton_matrix = (
        sum_everywhere(
            jnp.dot(seg_psi, seg_images.T, precision=precise, preferred_element_type=jnp.float32)
        )
        / cell_total
    )
    factor = jnp.linalg.cholesky(intersection)
    orthonormal = solve_triangular(factor, seg_psi)
    back_psi = exchange(orthonormal.reshape(tile))
    ortho_images = solve_triangular(factor, seg_images)
    half_solved = solve_triangular(factor, hamilton_matrix)
    subspace = solve_triangular(factor, half_solved.T).T
    gradient = ortho_images - jnp.dot(
        subspace, orthonormal, precision=precise, preferred_element_type=jnp.float32
    )
    back_gradient = exchange(gradient.reshape(tile))
    return (
        back_psi.reshape(orbitals_here, cell_total),
        back_gradient.reshape(orbitals_here, cell_total),
        subspace,
        density,
    )


def solution(mesh):
    in_specs = (P(("orb", "grp"), None), P(), P(), P())
    out_specs = (P(("orb", "grp"), None), P(("orb", "grp"), None), P(), P(("orb", "grp"), None))
    return jax.shard_map(
        on_device, mesh=mesh, in_specs=in_specs, out_specs=out_specs, check_vma=False
    )
```

```python
import functools

import jax
import jax.numpy as jnp
import ml_dtypes
import numpy as np
from jax import lax
from jax.experimental import pallas as pl
from jax.experimental.pallas import tpu as pltpu
from jax.sharding import PartitionSpec as P

G = 64
LANES = 128
PAIRS = G * G // LANES
PAD = 8
SHIFT = 2
STRIP = 16

magic_taps = (0.0028, -0.0236, 0.1026, 0.8364, 0.1026, -0.0236, 0.0028)
kinetic_taps = (
    -1.0 / 560.0,
    8.0 / 315.0,
    -0.2,
    1.6,
    -205.0 / 72.0,
    1.6,
    -0.2,
    8.0 / 315.0,
    -1.0 / 560.0,
)
precise = lax.Precision.HIGHEST
AXES = ("orb", "grp")


def banded(extent, taps):
    radius = len(taps) // 2
    matrix = np.zeros((extent, extent))
    for position, weight in enumerate(taps):
        matrix += weight * np.eye(extent, k=position - radius)
    return matrix


def shifted_blocks(along_y, along_z):
    radius = len(along_y) // 2
    blocks = np.zeros((2 * SHIFT + 1, 2, G, 2, G))
    for shift in range(-SHIFT, SHIFT + 1):
        for source in range(2):
            for target in range(2):
                offset = 2 * shift + source - target
                if abs(offset) <= radius:
                    blocks[shift + SHIFT, source, :, target, :] = (
                        along_y[offset + radius] * along_z.T
                    )
    return blocks.reshape((2 * SHIFT + 1) * LANES, LANES)


def split_constant(matrix):
    high = matrix.astype(ml_dtypes.bfloat16)
    low = (matrix - high.astype(np.float64)).astype(ml_dtypes.bfloat16)
    return high, low


def filter_constants():
    magic = shifted_blocks(magic_taps, banded(G, magic_taps))
    kinetic = shifted_blocks(kinetic_taps, np.eye(G)) + shifted_blocks(
        (1.0,), banded(G, kinetic_taps)
    )
    return (
        split_constant(np.concatenate([magic, kinetic], axis=1)),
        split_constant(magic),
    )


def plane_filter(read, first, taps):
    radius = len(taps) // 2
    total = taps[radius] * read(first)
    for step in range(1, radius + 1):
        total += taps[radius + step] * (read(first + step) + read(first - step))
    return total


def hamiltonian_kernel(
    occupation_ref,
    values_ref,
    potential_ref,
    both_high_ref,
    both_low_ref,
    magic_high_ref,
    magic_low_ref,
    images_ref,
    density_ref,
    source,
    filtered,
    kinetic,
):
    margin = len(kinetic_taps) // 2

    def clear_margins():
        zeros = jnp.zeros((margin, PAIRS + 2 * PAD, LANES), jnp.float32)
        source[:margin] = zeros
        source[margin + G :] = zeros
        edge = jnp.zeros((G + 2 * margin, PAD, LANES), jnp.float32)
        source[:, :PAD] = edge
        source[:, PAD + PAIRS :] = edge
        zeros = jnp.zeros((margin, PAIRS, LANES), jnp.float32)
        filtered[:margin] = zeros
        filtered[margin + G :] = zeros

    def product(x, high_ref, low_ref):
        shifted = jnp.concatenate(
            [
                source[pl.ds(margin + x, STRIP), PAD + s : PAD + s + PAIRS].reshape(
                    STRIP * PAIRS, LANES
                )
                for s in range(-SHIFT, SHIFT + 1)
            ],
            axis=1,
        )
        high = shifted.astype(jnp.bfloat16)
        low = (shifted - high.astype(jnp.float32)).astype(jnp.bfloat16)
        dot = functools.partial(jnp.dot, preferred_element_type=jnp.float32)
        return dot(high, high_ref[...]) + (dot(low, high_ref[...]) + dot(high, low_ref[...]))

    def own(x):
        return source[pl.ds(margin + x, STRIP), PAD : PAD + PAIRS]

    def half(x):
        return filtered[pl.ds(margin + x, STRIP)]

    clear_margins()
    source[margin : margin + G, PAD : PAD + PAIRS] = values_ref[...]

    @pl.loop(0, G, step=STRIP)
    def _(x):
        both = product(x, both_high_ref, both_low_ref)
        filtered[pl.ds(margin + x, STRIP)] = both[:, :LANES].reshape(STRIP, PAIRS, LANES)
        kinetic[pl.ds(x, STRIP)] = both[:, LANES:].reshape(STRIP, PAIRS, LANES) + plane_filter(
            own, x, kinetic_taps
        )

    scale = occupation_ref[0]

    @pl.loop(0, G, step=STRIP)
    def _(x):
        realspace = plane_filter(half, x, magic_taps)
        density_ref[pl.ds(x, STRIP)] = scale * realspace * realspace
        source[pl.ds(margin + x, STRIP), PAD : PAD + PAIRS] = (
            realspace * potential_ref[pl.ds(x, STRIP)]
        )

    @pl.loop(0, G, step=STRIP)
    def _(x):
        filtered[pl.ds(margin + x, STRIP)] = product(x, magic_high_ref, magic_low_ref).reshape(
            STRIP, PAIRS, LANES
        )

    @pl.loop(0, G, step=STRIP)
    def _(x):
        images_ref[pl.ds(x, STRIP)] = (
            plane_filter(half, x, magic_taps) - 0.5 * kinetic[pl.ds(x, STRIP)]
        )


def vmem():
    return pl.BlockSpec(memory_space=pltpu.VMEM)


def smem():
    return pl.BlockSpec(memory_space=pltpu.SMEM)


def apply_hamiltonian(values, potential, scale):
    (both_high, both_low), (magic_high, magic_low) = filter_constants()
    margin = len(kinetic_taps) // 2
    grid = jax.ShapeDtypeStruct((G, PAIRS, LANES), jnp.float32)
    return pl.pallas_call(
        hamiltonian_kernel,
        out_shape=(grid, grid),
        in_specs=[smem()] + [vmem()] * 6,
        out_specs=(vmem(), vmem()),
        scratch_shapes=[
            pltpu.VMEM((G + 2 * margin, PAIRS + 2 * PAD, LANES), jnp.float32),
            pltpu.VMEM((G + 2 * margin, PAIRS, LANES), jnp.float32),
            pltpu.VMEM((G, PAIRS, LANES), jnp.float32),
        ],
        compiler_params=pltpu.CompilerParams(vmem_limit_bytes=40 * 2**20),
        cost_estimate=pl.CostEstimate(
            flops=6 * 2048 * 640 * 384, bytes_accessed=5 * 2**20, transcendentals=0
        ),
        name="hamiltonian",
    )(
        scale,
        values,
        potential,
        jnp.asarray(both_high),
        jnp.asarray(both_low),
        jnp.asarray(magic_high),
        jnp.asarray(magic_low),
    )


def transposed_dot(a, b):
    return lax.dot_general(
        a, b, (((1,), (1,)), ((), ())), precision=precise, preferred_element_type=jnp.float32
    )


def overlap_kernel(left_ref, right_ref, out_ref):
    total = None
    for row in range(left_ref.shape[1]):
        term = transposed_dot(left_ref[:, row, :], right_ref[:, row, :])
        total = term if total is None else total + term
    out_ref[...] = total


def overlap(left, right):
    orbitals = left.shape[0]
    return pl.pallas_call(
        overlap_kernel,
        out_shape=jax.ShapeDtypeStruct((orbitals, orbitals), jnp.float32),
        in_specs=[vmem(), vmem()],
        out_specs=vmem(),
        compiler_params=pltpu.CompilerParams(vmem_limit_bytes=32 * 2**20),
        cost_estimate=pl.CostEstimate(
            flops=12 * 256 * 256 * 1024, bytes_accessed=2 * 2**20, transcendentals=0
        ),
        name="overlap",
    )(left, right)


BLOCK = 32
ROWS = 8


def factor_kernel(cells, matrix_ref, inverse_ref, work):
    size = matrix_ref.shape[0]
    work[:, :size] = matrix_ref[...] * (1.0 / cells)
    row = lax.broadcasted_iota(jnp.int32, (size, size), 0)
    column = lax.broadcasted_iota(jnp.int32, (size, size), 1)
    work[:, size:] = jnp.where(row == column, 1.0, 0.0)
    sub = lax.broadcasted_iota(jnp.int32, (ROWS, LANES), 0)

    def row_of(tile, j):
        return jnp.broadcast_to(tile[j : j + 1, :], tile.shape)

    for start in range(0, size, BLOCK):
        stop = start + BLOCK
        first = start // LANES * LANES
        last = size + (stop + LANES - 1) // LANES * LANES
        lanes = range(first, last, LANES)
        groups = BLOCK // ROWS
        tiles = [
            {c: work[start + g * ROWS : start + (g + 1) * ROWS, c : c + LANES] for c in lanes}
            for g in range(groups)
        ]
        for q in range(groups):
            base = start + q * ROWS
            home, at = base // LANES * LANES, base % LANES
            spread = [
                [
                    jnp.broadcast_to(tiles[g][home][:, at + m : at + m + 1], (ROWS, LANES))
                    for m in range(ROWS)
                ]
                if g >= q
                else None
                for g in range(groups)
            ]
            scales = jnp.ones((ROWS, LANES), jnp.float32)
            for j in range(ROWS):
                pivot = row_of(spread[q][j], j)
                root = lax.rsqrt(pivot)
                root = root * (1.5 - 0.5 * pivot * root * root)
                scales = jnp.where(sub == j, root, scales)
                weight = {}
                for g in range(q, groups):
                    weight[g] = spread[g][j] * root
                weight[q] = jnp.where(sub > j, weight[q], 0.0)
                for m in range(j + 1, ROWS):
                    top = row_of(spread[q][m], j) * root
                    for g in range(q, groups):
                        spread[g][m] = spread[g][m] - weight[g] * top
                for c in lanes:
                    top = row_of(tiles[q][c], j) * root
                    for g in range(q, groups):
                        tiles[g][c] = tiles[g][c] - weight[g] * top
            for c in lanes:
                tiles[q][c] = tiles[q][c] * scales
        for g in range(groups):
            for c in lanes:
                work[start + g * ROWS : start + (g + 1) * ROWS, c : c + LANES] = tiles[g][c]
        if stop < size:
            low = stop // LANES * LANES
            done = work[start:stop, :]
            update = lax.dot_general(
                done[:, low:size],
                done[:, low:last],
                (((0,), (0,)), ((), ())),
                precision=precise,
                preferred_element_type=jnp.float32,
            )
            work[stop:, low:last] = work[stop:, low:last] - update[stop - low :, :]
    inverse_ref[...] = jnp.where(row >= column, work[:, size:], 0.0)


def inverse_factor(matrix, cells):
    size = matrix.shape[0]
    return pl.pallas_call(
        functools.partial(factor_kernel, cells),
        out_shape=jax.ShapeDtypeStruct((size, size), jnp.float32),
        in_specs=[vmem()],
        out_specs=vmem(),
        scratch_shapes=[pltpu.VMEM((size, 2 * size), jnp.float32)],
        compiler_params=pltpu.CompilerParams(vmem_limit_bytes=32 * 2**20),
        cost_estimate=pl.CostEstimate(
            flops=20_000_000_000, bytes_accessed=2**19, transcendentals=256
        ),
        name="inverse_factor",
    )(matrix)


def mix_kernel(cells, inverse_ref, hamilton_ref, psi_ref, images_ref, out_ref, subspace_ref):
    def dot(a, b):
        return jnp.dot(a, b, precision=precise, preferred_element_type=jnp.float32)

    inverse = inverse_ref[...]
    subspace = transposed_dot(dot(inverse, hamilton_ref[...] * (1.0 / cells)), inverse)
    subspace_ref[...] = subspace
    rows = psi_ref.shape[1]
    for row in range(rows):
        orthonormal = dot(inverse, psi_ref[:, row, :])
        out_ref[:, row, :] = orthonormal
        out_ref[:, rows + row, :] = dot(inverse, images_ref[:, row, :]) - dot(
            subspace, orthonormal
        )


def mix(inverse, hamilton_matrix, psi, images, cells):
    size = inverse.shape[0]
    orbitals, rows, lanes = psi.shape
    return pl.pallas_call(
        functools.partial(mix_kernel, cells),
        out_shape=(
            jax.ShapeDtypeStruct((orbitals, 2 * rows, lanes), jnp.float32),
            jax.ShapeDtypeStruct((size, size), jnp.float32),
        ),
        in_specs=[vmem()] * 4,
        out_specs=(vmem(), vmem()),
        compiler_params=pltpu.CompilerParams(vmem_limit_bytes=32 * 2**20),
        cost_estimate=pl.CostEstimate(
            flops=36 * 256 * 256 * 1024, bytes_accessed=5 * 2**20, transcendentals=0
        ),
        name="mix",
    )(inverse, hamilton_matrix, psi, images)


def exchange(blocks):
    return lax.all_to_all(blocks, AXES, split_axis=0, concat_axis=0, tiled=True)


def reduce_slab(partial, mesh_shape):
    orb, grp = mesh_shape
    core_count, x_count = 2, 4
    z_count = orb // (core_count * x_count)
    me = lax.axis_index("orb")
    core, x, z = me % core_count, me // core_count % x_count, me // (core_count * x_count)
    y = lax.axis_index("grp")

    def flat(z, x, core):
        return ((z % z_count) * x_count + x % x_count) * core_count + core % core_count

    places = [
        (a, b, c) for a in range(z_count) for b in range(x_count) for c in range(core_count)
    ]

    def stage(values, dim, count, index, axis, pairs):
        total = lax.dynamic_index_in_dim(values, index, dim, keepdims=False)
        arrived = [
            lax.ppermute(
                lax.dynamic_index_in_dim(values, (index + k) % count, dim, keepdims=False),
                axis,
                pairs(k),
            )
            for k in range(1, count)
        ]
        for term in arrived:
            total = total + term
        return total

    values = partial.reshape(z_count, x_count, core_count, grp, -1, LANES)
    values = stage(
        values, 2, core_count, core, "orb",
        lambda k: [(flat(a, b, c), flat(a, b, c + k)) for a, b, c in places],
    )
    values = stage(
        values, 2, grp, y, "grp", lambda k: [(i, (i + k) % grp) for i in range(grp)]
    )
    values = stage(
        values, 1, x_count, x, "orb",
        lambda k: [(flat(a, b, c), flat(a, b + k, c)) for a, b, c in places],
    )
    return stage(
        values, 0, z_count, z, "orb",
        lambda k: [(flat(a, b, c), flat(a + k, b, c)) for a, b, c in places],
    )


def on_device(mesh_shape, orbitals, potential, occupation, region_bounds):
    cell_total = orbitals.shape[1]
    device_total = mesh_shape[0] * mesh_shape[1]
    orbital_total = device_total
    segment = cell_total // device_total
    position = lax.axis_index("orb") * mesh_shape[1] + lax.axis_index("grp")
    bounds = lax.dynamic_slice_in_dim(region_bounds, position, 1, 0)
    scale = lax.dynamic_slice_in_dim(occupation, position, 1, 0) / orbital_total
    planes = lax.broadcasted_iota(jnp.int32, (G, PAIRS, LANES), 0)
    inside = (planes >= bounds[0, 0]) & (planes < bounds[0, 1])
    masked = jnp.where(inside, orbitals.reshape(G, PAIRS, LANES), 0.0)

    tile = (device_total, segment // LANES, LANES)
    seg_psi = exchange(masked.reshape(tile))
    images, density_part = apply_hamiltonian(masked, potential.reshape(G, PAIRS, LANES), scale)
    density = reduce_slab(density_part, mesh_shape).reshape(-1, G)

    row = (device_total, orbital_total // LANES, LANES)

    def own_row(parts):
        return jnp.broadcast_to(jnp.sum(parts, axis=0, keepdims=True), row)

    def square(rows):
        return rows.reshape(orbital_total, orbital_total)

    seg_images = exchange(images.reshape(tile))
    intersection = square(exchange(own_row(exchange(overlap(seg_psi, seg_psi).reshape(row)))))
    inverse = inverse_factor(intersection, cell_total)
    hamilton_matrix = square(
        exchange(own_row(exchange(overlap(seg_psi, seg_images).reshape(row))))
    )
    mixed, subspace = mix(inverse, hamilton_matrix, seg_psi, seg_images, cell_total)
    back = exchange(mixed)
    rows = segment // LANES
    return (
        back[:, :rows].reshape(1, cell_total),
        back[:, rows:].reshape(1, cell_total),
        subspace,
        density,
    )


def solution(mesh):
    in_specs = (P(AXES, None), P(), P(), P())
    out_specs = (P(AXES, None), P(AXES, None), P(), P(AXES, None))
    step = functools.partial(on_device, (mesh.shape["orb"], mesh.shape["grp"]))
    return jax.shard_map(
        step, mesh=mesh, in_specs=in_specs, out_specs=out_specs, check_vma=False
    )
```

```python
import functools

import jax
import jax.numpy as jnp
import ml_dtypes
import numpy as np
from jax import lax
from jax.experimental import pallas as pl
from jax.experimental.pallas import tpu as pltpu
from jax.sharding import PartitionSpec as P

G = 64
LANES = 128
PAIRS = G * G // LANES
PAD = 8
SHIFT = 2
STRIP = 16
ROWS = 8
BLOCK = 32

magic_taps = (0.0028, -0.0236, 0.1026, 0.8364, 0.1026, -0.0236, 0.0028)
kinetic_taps = (
    -1.0 / 560.0,
    8.0 / 315.0,
    -0.2,
    1.6,
    -205.0 / 72.0,
    1.6,
    -0.2,
    8.0 / 315.0,
    -1.0 / 560.0,
)
precise = lax.Precision.HIGHEST
AXES = ("orb", "grp")


def banded(extent, taps):
    radius = len(taps) // 2
    matrix = np.zeros((extent, extent))
    for position, weight in enumerate(taps):
        matrix += weight * np.eye(extent, k=position - radius)
    return matrix


def shifted_blocks(along_y, along_z):
    radius = len(along_y) // 2
    blocks = np.zeros((2 * SHIFT + 1, 2, G, 2, G))
    for shift in range(-SHIFT, SHIFT + 1):
        for source in range(2):
            for target in range(2):
                offset = 2 * shift + source - target
                if abs(offset) <= radius:
                    blocks[shift + SHIFT, source, :, target, :] = (
                        along_y[offset + radius] * along_z.T
                    )
    return blocks.reshape((2 * SHIFT + 1) * LANES, LANES)


def split_constant(matrix):
    high = matrix.astype(ml_dtypes.bfloat16)
    low = (matrix - high.astype(np.float64)).astype(ml_dtypes.bfloat16)
    return high, low


def filter_constants():
    magic = shifted_blocks(magic_taps, banded(G, magic_taps))
    kinetic = shifted_blocks(kinetic_taps, np.eye(G)) + shifted_blocks(
        (1.0,), banded(G, kinetic_taps)
    )
    return (
        split_constant(np.concatenate([magic, kinetic], axis=1)),
        split_constant(magic),
    )


def plane_filter(read, first, taps):
    radius = len(taps) // 2
    total = taps[radius] * read(first)
    for step in range(1, radius + 1):
        total += taps[radius + step] * (read(first + step) + read(first - step))
    return total


def hamiltonian_kernel(
    place_ref,
    bounds_ref,
    occupation_ref,
    orbital_ref,
    potential_ref,
    both_high_ref,
    both_low_ref,
    magic_high_ref,
    magic_low_ref,
    keep_ref,
    give_ref,
    density_ref,
    source,
    filtered,
    kinetic,
):
    margin = len(kinetic_taps) // 2
    position, core = place_ref[0], place_ref[1]

    zeros = jnp.zeros((margin, PAIRS + 2 * PAD, LANES), jnp.float32)
    source[:margin] = zeros
    source[margin + G :] = zeros
    edge = jnp.zeros((G + 2 * margin, PAD, LANES), jnp.float32)
    source[:, :PAD] = edge
    source[:, PAD + PAIRS :] = edge
    zeros = jnp.zeros((margin, PAIRS, LANES), jnp.float32)
    filtered[:margin] = zeros
    filtered[margin + G :] = zeros

    def product(x, high_ref, low_ref):
        shifted = jnp.concatenate(
            [
                source[pl.ds(margin + x, STRIP), PAD + s : PAD + s + PAIRS].reshape(
                    STRIP * PAIRS, LANES
                )
                for s in range(-SHIFT, SHIFT + 1)
            ],
            axis=1,
        )
        high = shifted.astype(jnp.bfloat16)
        low = (shifted - high.astype(jnp.float32)).astype(jnp.bfloat16)
        dot = functools.partial(jnp.dot, preferred_element_type=jnp.float32)
        return dot(high, high_ref[...]) + (dot(low, high_ref[...]) + dot(high, low_ref[...]))

    def own(x):
        return source[pl.ds(margin + x, STRIP), PAD : PAD + PAIRS]

    def half(x):
        return filtered[pl.ds(margin + x, STRIP)]

    planes = lax.broadcasted_iota(jnp.int32, (STRIP, PAIRS, LANES), 0)
    begin, end = bounds_ref[position, 0], bounds_ref[position, 1]
    blocks = STRIP * PAIRS // ROWS
    half_planes = G // 2

    def tiled(strip):
        return strip.reshape(blocks, ROWS, LANES)

    for side, out_ref in ((core, keep_ref), (1 - core, give_ref)):
        for strip in range(0, half_planes, STRIP):
            x = half_planes * side + strip
            inside = (planes + x >= begin) & (planes + x < end)
            masked = jnp.where(inside, orbital_ref[pl.ds(x, STRIP)], 0.0)
            source[pl.ds(margin + x, STRIP), PAD : PAD + PAIRS] = masked
            first = strip * PAIRS // ROWS
            out_ref[first : first + blocks, :ROWS, :] = tiled(masked)

    @pl.loop(0, G, step=STRIP)
    def _(x):
        both = product(x, both_high_ref, both_low_ref)
        filtered[pl.ds(margin + x, STRIP)] = both[:, :LANES].reshape(STRIP, PAIRS, LANES)
        kinetic[pl.ds(x, STRIP)] = both[:, LANES:].reshape(STRIP, PAIRS, LANES) + plane_filter(
            own, x, kinetic_taps
        )

    scale = occupation_ref[position] * (1.0 / occupation_ref.shape[0])
    lines = STRIP * G // 2

    @pl.loop(0, G, step=STRIP)
    def _(x):
        realspace = plane_filter(half, x, magic_taps)
        density_ref[pl.ds(x, STRIP)] = scale * realspace * realspace
        potential = jnp.concatenate(
            [potential_ref[pl.ds(x * G + odd, lines, stride=2), :] for odd in range(2)], axis=1
        ).reshape(STRIP, PAIRS, LANES)
        source[pl.ds(margin + x, STRIP), PAD : PAD + PAIRS] = realspace * potential

    @pl.loop(0, G, step=STRIP)
    def _(x):
        filtered[pl.ds(margin + x, STRIP)] = product(x, magic_high_ref, magic_low_ref).reshape(
            STRIP, PAIRS, LANES
        )

    for side, out_ref in ((core, keep_ref), (1 - core, give_ref)):
        for strip in range(0, half_planes, STRIP):
            x = half_planes * side + strip
            images = plane_filter(half, x, magic_taps) - 0.5 * kinetic[pl.ds(x, STRIP)]
            first = strip * PAIRS // ROWS
            out_ref[first : first + blocks, ROWS:, :] = tiled(images)


def vmem():
    return pl.BlockSpec(memory_space=pltpu.VMEM)


def smem():
    return pl.BlockSpec(memory_space=pltpu.SMEM)


def apply_hamiltonian(place, region_bounds, occupation, orbital, potential):
    (both_high, both_low), (magic_high, magic_low) = filter_constants()
    margin = len(kinetic_taps) // 2
    side = jax.ShapeDtypeStruct((G * PAIRS // ROWS // 2, 2 * ROWS, LANES), jnp.float32)
    grid = jax.ShapeDtypeStruct((G, PAIRS, LANES), jnp.float32)
    return pl.pallas_call(
        hamiltonian_kernel,
        out_shape=(side, side, grid),
        in_specs=[smem()] * 3 + [vmem()] * 6,
        out_specs=(vmem(),) * 3,
        scratch_shapes=[
            pltpu.VMEM((G + 2 * margin, PAIRS + 2 * PAD, LANES), jnp.float32),
            pltpu.VMEM((G + 2 * margin, PAIRS, LANES), jnp.float32),
            pltpu.VMEM((G, PAIRS, LANES), jnp.float32),
        ],
        compiler_params=pltpu.CompilerParams(vmem_limit_bytes=40 * 2**20),
        cost_estimate=pl.CostEstimate(
            flops=6 * 2048 * 640 * 384, bytes_accessed=5 * 2**20, transcendentals=0
        ),
        name="hamiltonian",
    )(
        place,
        region_bounds,
        occupation,
        orbital,
        potential,
        jnp.asarray(both_high),
        jnp.asarray(both_low),
        jnp.asarray(magic_high),
        jnp.asarray(magic_low),
    )


def transposed_dot(a, b):
    return lax.dot_general(
        a, b, (((1,), (1,)), ((), ())), precision=precise, preferred_element_type=jnp.float32
    )


CORES = 2
LINES = 4


def natural_rows(flat_ref, natural_ref, core, gather):
    planes, orbitals, _ = natural_ref.shape
    groups = orbitals // (CORES * LINES)
    stride = CORES * LINES * planes
    for slot in range(CORES):
        for line in range(LINES):
            for plane in range(planes):
                inner = pl.ds((line * CORES + slot) * planes + plane, groups, stride=stride)
                outer = pl.ds((slot ^ core) * LINES + line, groups, stride=CORES * LINES)
                if gather:
                    natural_ref[plane, outer, :] = flat_ref[inner, :]
                else:
                    flat_ref[inner, :] = natural_ref[plane, outer, :]


def overlap_kernel(core_ref, flat_ref, natural_ref, packed_ref):
    for core in range(CORES):

        @pl.when(core_ref[0] == core)
        def _(core=core):
            natural_rows(flat_ref, natural_ref, core, True)

    planes, size, _ = natural_ref.shape
    half = planes // 2
    total = None
    for plane in range(0, half, 2):
        psi = jnp.concatenate([natural_ref[plane], natural_ref[plane + 1]], axis=1)
        images = jnp.concatenate(
            [natural_ref[half + plane], natural_ref[half + plane + 1]], axis=1
        )
        term = transposed_dot(psi, jnp.concatenate([psi, images], axis=0))
        total = term if total is None else total + term
    row = lax.broadcasted_iota(jnp.int32, (size, size), 0)
    column = lax.broadcasted_iota(jnp.int32, (size, size), 1)
    hamilton = total[:, size:]
    packed = jnp.where(row <= column, total[:, :size], hamilton)
    diagonal = jnp.sum(jnp.where(row == column, hamilton, 0.0), axis=1, keepdims=True)
    chunks = size // ROWS
    for part in range(size // LANES):
        packed_ref[:, part * ROWS : (part + 1) * ROWS, :] = packed[
            :, part * LANES : (part + 1) * LANES
        ].reshape(chunks, ROWS, LANES)
    packed_ref[:, size // LANES * ROWS :, :] = jnp.broadcast_to(
        diagonal, (size, LANES)
    ).reshape(chunks, ROWS, LANES)


def overlap(core, arrived):
    rows, lanes = arrived.shape
    planes = 2 * ROWS
    size = rows // planes
    return pl.pallas_call(
        overlap_kernel,
        out_shape=(
            jax.ShapeDtypeStruct((planes, size, lanes), jnp.float32),
            jax.ShapeDtypeStruct((size // ROWS, (size // LANES + 1) * ROWS, LANES), jnp.float32),
        ),
        in_specs=[smem(), vmem()],
        out_specs=(vmem(), vmem()),
        compiler_params=pltpu.CompilerParams(vmem_limit_bytes=40 * 2**20),
        cost_estimate=pl.CostEstimate(
            flops=24 * 256 * 256 * 1024, bytes_accessed=4 * 2**20, transcendentals=0
        ),
        name="overlap",
    )(core, arrived)


def eliminate(work):
    size = work.shape[0]
    sub = lax.broadcasted_iota(jnp.int32, (ROWS, LANES), 0)

    def row_of(tile, j):
        return jnp.broadcast_to(tile[j : j + 1, :], tile.shape)

    for start in range(0, size, BLOCK):
        stop = start + BLOCK
        first = start // LANES * LANES
        last = size + (stop + LANES - 1) // LANES * LANES
        lanes = range(first, last, LANES)
        groups = BLOCK // ROWS
        tiles = [
            {c: work[start + g * ROWS : start + (g + 1) * ROWS, c : c + LANES] for c in lanes}
            for g in range(groups)
        ]
        for q in range(groups):
            base = start + q * ROWS
            home, at = base // LANES * LANES, base % LANES
            spread = [
                [
                    jnp.broadcast_to(tiles[g][home][:, at + m : at + m + 1], (ROWS, LANES))
                    for m in range(ROWS)
                ]
                if g >= q
                else None
                for g in range(groups)
            ]
            scales = jnp.ones((ROWS, LANES), jnp.float32)
            for j in range(ROWS):
                pivot = row_of(spread[q][j], j)
                root = lax.rsqrt(pivot)
                root = root * (1.5 - 0.5 * pivot * root * root)
                scales = jnp.where(sub == j, root, scales)
                weight = {}
                for g in range(q, groups):
                    weight[g] = spread[g][j] * root
                weight[q] = jnp.where(sub > j, weight[q], 0.0)
                for m in range(j + 1, ROWS):
                    top = row_of(spread[q][m], j) * root
                    for g in range(q, groups):
                        spread[g][m] = spread[g][m] - weight[g] * top
                for c in lanes:
                    top = row_of(tiles[q][c], j) * root
                    for g in range(q, groups):
                        tiles[g][c] = tiles[g][c] - weight[g] * top
            for c in lanes:
                tiles[q][c] = tiles[q][c] * scales
        for g in range(groups):
            for c in lanes:
                work[start + g * ROWS : start + (g + 1) * ROWS, c : c + LANES] = tiles[g][c]
        if stop < size:
            low = stop // LANES * LANES
            done = work[start:stop, :]
            update = lax.dot_general(
                done[:, low:size],
                done[:, low:last],
                (((0,), (0,)), ((), ())),
                precision=precise,
                preferred_element_type=jnp.float32,
            )
            work[stop:, low:last] = work[stop:, low:last] - update[stop - low :, :]


def solve_kernel(cells, summed_ref, natural_ref, flat_ref, subspace_ref, work, mixed):
    def dot(a, b):
        return jnp.dot(a, b, precision=precise, preferred_element_type=jnp.float32)

    size = work.shape[0]
    parts = size // LANES
    tiles = [
        summed_ref[:, part * ROWS : (part + 1) * ROWS, :].reshape(size, LANES)
        for part in range(parts + 1)
    ]
    packed = jnp.concatenate(tiles[:parts], axis=1) * (1.0 / cells)
    diagonal = jnp.concatenate(tiles[parts:] * parts, axis=1) * (1.0 / cells)
    row = lax.broadcasted_iota(jnp.int32, (size, size), 0)
    column = lax.broadcasted_iota(jnp.int32, (size, size), 1)
    turned = packed.T
    work[:, :size] = jnp.where(row <= column, packed, turned)
    work[:, size:] = jnp.where(row == column, 1.0, 0.0)
    hamilton = jnp.where(row > column, packed, jnp.where(row == column, diagonal, turned))
    eliminate(work)
    inverse = jnp.where(row >= column, work[:, size:], 0.0)
    subspace = transposed_dot(dot(inverse, hamilton), inverse)
    subspace_ref[...] = subspace
    planes = natural_ref.shape[0]
    half = planes // 2
    for plane in range(0, half, 2):
        both = [
            dot(
                inverse,
                jnp.concatenate([natural_ref[plane + k], natural_ref[half + plane + k]], axis=1),
            )
            for k in range(2)
        ]
        product = dot(subspace, jnp.concatenate([part[:, :LANES] for part in both], axis=1))
        for k, part in enumerate(both):
            mixed[plane + k] = part[:, :LANES]
            mixed[half + plane + k] = part[:, LANES:] - product[:, k * LANES : (k + 1) * LANES]
    natural_rows(flat_ref, mixed, 0, False)


def solve(summed, natural, cells):
    planes, size, lanes = natural.shape
    return pl.pallas_call(
        functools.partial(solve_kernel, cells),
        out_shape=(
            jax.ShapeDtypeStruct((planes * size, lanes), jnp.float32),
            jax.ShapeDtypeStruct((size, size), jnp.float32),
        ),
        in_specs=[vmem()] * 2,
        out_specs=(vmem(), vmem()),
        scratch_shapes=[
            pltpu.VMEM((size, 2 * size), jnp.float32),
            pltpu.VMEM(natural.shape, jnp.float32),
        ],
        compiler_params=pltpu.CompilerParams(vmem_limit_bytes=48 * 2**20),
        cost_estimate=pl.CostEstimate(
            flops=20_000_000_000, bytes_accessed=6 * 2**20, transcendentals=256
        ),
        name="solve",
    )(summed, natural)


def assemble_kernel(core_ref, arrived_ref, received_ref, first_ref, second_ref, sems):
    core = core_ref[0]
    blocks = received_ref.shape[0]
    copies = []
    for which, out_ref in enumerate((first_ref, second_ref)):
        rows = pl.ds(which * ROWS, ROWS)
        copies.append(
            pltpu.make_async_copy(
                arrived_ref.at[:, pl.ds((core * 2 + which) * ROWS, ROWS)],
                out_ref.at[pl.ds(core * blocks, blocks)],
                sems.at[2 * which],
            )
        )
        copies.append(
            pltpu.make_async_copy(
                received_ref.at[:, rows],
                out_ref.at[pl.ds((1 - core) * blocks, blocks)],
                sems.at[2 * which + 1],
            )
        )
    for copy in copies:
        copy.start()
    for copy in copies:
        copy.wait()


def assemble(core, arrived, received):
    blocks, _, lanes = received.shape
    out = jax.ShapeDtypeStruct((CORES * blocks, ROWS, lanes), jnp.float32)
    anywhere = pl.BlockSpec(memory_space=pl.ANY)
    return pl.pallas_call(
        assemble_kernel,
        out_shape=(out, out),
        in_specs=[smem(), anywhere, anywhere],
        out_specs=(anywhere, anywhere),
        scratch_shapes=[pltpu.SemaphoreType.DMA((4,))],
        cost_estimate=pl.CostEstimate(flops=0, bytes_accessed=4 * 2**20, transcendentals=0),
        name="assemble",
    )(core, arrived, received)


def exchange(blocks, groups, axes=AXES):
    return lax.all_to_all(
        blocks, axes, split_axis=0, concat_axis=0, tiled=True, axis_index_groups=groups
    )


class Layout:
    def __init__(self, orb, grp):
        self.x, self.core, self.y = 4, CORES, grp
        self.z = orb // (self.x * self.core)
        self.total = orb * grp

    def orb(self, z, x, core):
        return ((z % self.z) * self.x + x % self.x) * self.core + core % self.core

    def device(self, z, x, core, y):
        return self.orb(z, x, core) * self.y + y

    def places(self):
        return [
            (z, x, core)
            for z in range(self.z)
            for x in range(self.x)
            for core in range(self.core)
        ]

    def chips(self):
        return [
            [
                self.device(z, x, core, y)
                for z in range(self.z)
                for x in range(self.x)
                for y in range(self.y)
            ]
            for core in range(self.core)
        ]

    def planes(self):
        return [
            [
                self.device(z, x, core, y)
                for x in range(self.x)
                for core in range(self.core)
                for y in range(self.y)
            ]
            for z in range(self.z)
        ]

    def columns(self):
        return [
            [self.orb(z, x, core) for z in range(self.z)]
            for x in range(self.x)
            for core in range(self.core)
        ]

    def swap_cores(self, values):
        pairs = [(self.orb(z, x, c), self.orb(z, x, c + 1)) for z, x, c in self.places()]
        return lax.ppermute(values, "orb", pairs)


def reduce_slab(partial, layout):
    me = lax.axis_index("orb")
    core = me % layout.core
    x = me // layout.core % layout.x
    z = me // (layout.core * layout.x)
    y = lax.axis_index("grp")

    def stage(values, dim, count, index, axis, pairs):
        total = lax.dynamic_index_in_dim(values, index, dim, keepdims=False)
        arrived = [
            lax.ppermute(
                lax.dynamic_index_in_dim(values, (index + k) % count, dim, keepdims=False),
                axis,
                pairs(k),
            )
            for k in range(1, count)
        ]
        for term in arrived:
            total = total + term
        return total

    def along(dz, dx, dc):
        return lambda k: [
            (layout.orb(a, b, c), layout.orb(a + dz * k, b + dx * k, c + dc * k))
            for a, b, c in layout.places()
        ]

    def lines(k):
        return [(i, (i + k) % layout.y) for i in range(layout.y)]

    values = partial.reshape(layout.z, layout.x, layout.core, layout.y, -1, LANES)
    values = stage(values, 2, layout.core, core, "orb", along(0, 0, 1))
    values = stage(values, 2, layout.y, y, "grp", lines)
    values = stage(values, 1, layout.x, x, "orb", along(0, 1, 0))
    return stage(values, 0, layout.z, z, "orb", along(1, 0, 0))


def sum_everywhere(chunks, layout):
    count, rows, lanes = chunks.shape

    def spread(values, copies):
        return jnp.broadcast_to(jnp.sum(values, axis=0, keepdims=True), (copies, rows, lanes))

    part = spread(exchange(chunks, layout.planes()), layout.z)
    part = spread(exchange(part, layout.columns(), "orb"), count)
    return exchange(part, layout.planes())


def on_device(layout, orbitals, potential, occupation, region_bounds):
    cell_total = orbitals.shape[1]
    orb, grp = lax.axis_index("orb"), lax.axis_index("grp")
    position = orb * layout.y + grp
    core = orb % layout.core
    place = jnp.stack([position, core]).astype(jnp.int32)
    core = core.reshape(1).astype(jnp.int32)
    keep, give, density_part = apply_hamiltonian(
        place, region_bounds, occupation, orbitals.reshape(G, PAIRS, LANES), potential
    )
    sent = jnp.concatenate([keep, layout.swap_cores(give)], axis=1)
    density = reduce_slab(density_part, layout)
    arrived = exchange(sent, layout.chips())
    arrived, density = lax.optimization_barrier((arrived, density))
    natural, packed = overlap(core, arrived.reshape(-1, LANES))
    summed = sum_everywhere(packed, layout)
    mixed, subspace = solve(summed, natural, cell_total)
    back = exchange(mixed.reshape(-1, 4 * ROWS, LANES), layout.chips())
    other = lax.dynamic_slice_in_dim(back, (1 - core[0]) * 2 * ROWS, 2 * ROWS, 1)
    orthonormal, gradient = assemble(core, back, layout.swap_cores(other))
    return (
        orthonormal.reshape(1, cell_total),
        gradient.reshape(1, cell_total),
        subspace,
        density.reshape(-1, G),
    )


def solution(mesh):
    in_specs = (P(AXES, None), P(), P(), P())
    out_specs = (P(AXES, None), P(AXES, None), P(), P(AXES, None))
    step = functools.partial(on_device, Layout(mesh.shape["orb"], mesh.shape["grp"]))
    return jax.shard_map(
        step, mesh=mesh, in_specs=in_specs, out_specs=out_specs, check_vma=False
    )
```

```python
import functools

import jax
import jax.numpy as jnp
import ml_dtypes
import numpy as np
from jax import lax
from jax.experimental import pallas as pl
from jax.experimental.pallas import tpu as pltpu
from jax.sharding import PartitionSpec as P

G = 64
LANES = 128
PAIRS = G * G // LANES
PAD = 8
SHIFT = 2
STRIP = 16
ROWS = 8
BLOCK = 32

magic_taps = (0.0028, -0.0236, 0.1026, 0.8364, 0.1026, -0.0236, 0.0028)
kinetic_taps = (
    -1.0 / 560.0,
    8.0 / 315.0,
    -0.2,
    1.6,
    -205.0 / 72.0,
    1.6,
    -0.2,
    8.0 / 315.0,
    -1.0 / 560.0,
)
precise = lax.Precision.HIGHEST
AXES = ("orb", "grp")


def banded(extent, taps):
    radius = len(taps) // 2
    matrix = np.zeros((extent, extent))
    for position, weight in enumerate(taps):
        matrix += weight * np.eye(extent, k=position - radius)
    return matrix


def shifted_blocks(along_y, along_z):
    radius = len(along_y) // 2
    blocks = np.zeros((2 * SHIFT + 1, 2, G, 2, G))
    for shift in range(-SHIFT, SHIFT + 1):
        for source in range(2):
            for target in range(2):
                offset = 2 * shift + source - target
                if abs(offset) <= radius:
                    blocks[shift + SHIFT, source, :, target, :] = (
                        along_y[offset + radius] * along_z.T
                    )
    return blocks.reshape((2 * SHIFT + 1) * LANES, LANES)


def split_constant(matrix):
    high = matrix.astype(ml_dtypes.bfloat16)
    low = (matrix - high.astype(np.float64)).astype(ml_dtypes.bfloat16)
    return high, low


def filter_constants():
    magic = shifted_blocks(magic_taps, banded(G, magic_taps))
    kinetic = shifted_blocks(kinetic_taps, np.eye(G)) + shifted_blocks(
        (1.0,), banded(G, kinetic_taps)
    )
    return (
        split_constant(np.concatenate([magic, kinetic], axis=1)),
        split_constant(magic),
    )


def plane_filter(read, first, taps):
    radius = len(taps) // 2
    total = taps[radius] * read(first)
    for step in range(1, radius + 1):
        total += taps[radius + step] * (read(first + step) + read(first - step))
    return total


def hamiltonian_kernel(
    place_ref,
    bounds_ref,
    occupation_ref,
    orbital_ref,
    potential_ref,
    both_high_ref,
    both_low_ref,
    magic_high_ref,
    magic_low_ref,
    keep_ref,
    give_ref,
    density_ref,
    source,
    filtered,
    kinetic,
):
    margin = len(kinetic_taps) // 2
    position, core = place_ref[0], place_ref[1]

    zeros = jnp.zeros((margin, PAIRS + 2 * PAD, LANES), jnp.float32)
    source[:margin] = zeros
    source[margin + G :] = zeros
    edge = jnp.zeros((G + 2 * margin, PAD, LANES), jnp.float32)
    source[:, :PAD] = edge
    source[:, PAD + PAIRS :] = edge
    zeros = jnp.zeros((margin, PAIRS, LANES), jnp.float32)
    filtered[:margin] = zeros
    filtered[margin + G :] = zeros

    def product(x, high_ref, low_ref):
        shifted = jnp.concatenate(
            [
                source[pl.ds(margin + x, STRIP), PAD + s : PAD + s + PAIRS].reshape(
                    STRIP * PAIRS, LANES
                )
                for s in range(-SHIFT, SHIFT + 1)
            ],
            axis=1,
        )
        high = shifted.astype(jnp.bfloat16)
        low = (shifted - high.astype(jnp.float32)).astype(jnp.bfloat16)
        dot = functools.partial(jnp.dot, preferred_element_type=jnp.float32)
        return dot(high, high_ref[...]) + (dot(low, high_ref[...]) + dot(high, low_ref[...]))

    def own(x):
        return source[pl.ds(margin + x, STRIP), PAD : PAD + PAIRS]

    def half(x):
        return filtered[pl.ds(margin + x, STRIP)]

    planes = lax.broadcasted_iota(jnp.int32, (STRIP, PAIRS, LANES), 0)
    begin, end = bounds_ref[position, 0], bounds_ref[position, 1]
    blocks = STRIP * PAIRS // ROWS
    half_planes = G // 2

    def tiled(strip):
        return strip.reshape(blocks, ROWS, LANES)

    for side, out_ref in ((core, keep_ref), (1 - core, give_ref)):
        for strip in range(0, half_planes, STRIP):
            x = half_planes * side + strip
            inside = (planes + x >= begin) & (planes + x < end)
            masked = jnp.where(inside, orbital_ref[pl.ds(x, STRIP)], 0.0)
            source[pl.ds(margin + x, STRIP), PAD : PAD + PAIRS] = masked
            first = strip * PAIRS // ROWS
            out_ref[first : first + blocks, :ROWS, :] = tiled(masked)

    @pl.loop(0, G, step=STRIP)
    def _(x):
        both = product(x, both_high_ref, both_low_ref)
        filtered[pl.ds(margin + x, STRIP)] = both[:, :LANES].reshape(STRIP, PAIRS, LANES)
        kinetic[pl.ds(x, STRIP)] = both[:, LANES:].reshape(STRIP, PAIRS, LANES) + plane_filter(
            own, x, kinetic_taps
        )

    scale = occupation_ref[position] * (1.0 / occupation_ref.shape[0])
    lines = STRIP * G // 2

    @pl.loop(0, G, step=STRIP)
    def _(x):
        realspace = plane_filter(half, x, magic_taps)
        density_ref[pl.ds(x, STRIP)] = scale * realspace * realspace
        potential = jnp.concatenate(
            [potential_ref[pl.ds(x * G + odd, lines, stride=2), :] for odd in range(2)], axis=1
        ).reshape(STRIP, PAIRS, LANES)
        source[pl.ds(margin + x, STRIP), PAD : PAD + PAIRS] = realspace * potential

    @pl.loop(0, G, step=STRIP)
    def _(x):
        filtered[pl.ds(margin + x, STRIP)] = product(x, magic_high_ref, magic_low_ref).reshape(
            STRIP, PAIRS, LANES
        )

    for side, out_ref in ((core, keep_ref), (1 - core, give_ref)):
        for strip in range(0, half_planes, STRIP):
            x = half_planes * side + strip
            images = plane_filter(half, x, magic_taps) - 0.5 * kinetic[pl.ds(x, STRIP)]
            first = strip * PAIRS // ROWS
            out_ref[first : first + blocks, ROWS:, :] = tiled(images)


def vmem():
    return pl.BlockSpec(memory_space=pltpu.VMEM)


def smem():
    return pl.BlockSpec(memory_space=pltpu.SMEM)


def apply_hamiltonian(place, region_bounds, occupation, orbital, potential):
    (both_high, both_low), (magic_high, magic_low) = filter_constants()
    margin = len(kinetic_taps) // 2
    side = jax.ShapeDtypeStruct((G * PAIRS // ROWS // 2, 2 * ROWS, LANES), jnp.float32)
    grid = jax.ShapeDtypeStruct((G, PAIRS, LANES), jnp.float32)
    return pl.pallas_call(
        hamiltonian_kernel,
        out_shape=(side, side, grid),
        in_specs=[smem()] * 3 + [vmem()] * 6,
        out_specs=(vmem(),) * 3,
        scratch_shapes=[
            pltpu.VMEM((G + 2 * margin, PAIRS + 2 * PAD, LANES), jnp.float32),
            pltpu.VMEM((G + 2 * margin, PAIRS, LANES), jnp.float32),
            pltpu.VMEM((G, PAIRS, LANES), jnp.float32),
        ],
        compiler_params=pltpu.CompilerParams(vmem_limit_bytes=40 * 2**20),
        cost_estimate=pl.CostEstimate(
            flops=6 * 2048 * 640 * 384, bytes_accessed=5 * 2**20, transcendentals=0
        ),
        name="hamiltonian",
    )(
        place,
        region_bounds,
        occupation,
        orbital,
        potential,
        jnp.asarray(both_high),
        jnp.asarray(both_low),
        jnp.asarray(magic_high),
        jnp.asarray(magic_low),
    )


def transposed_dot(a, b):
    return lax.dot_general(
        a, b, (((1,), (1,)), ((), ())), precision=precise, preferred_element_type=jnp.float32
    )


CORES = 2
LINES = 4


def natural_rows(flat_ref, natural_ref, core, gather):
    planes, orbitals, _ = natural_ref.shape
    groups = orbitals // (CORES * LINES)
    stride = CORES * LINES * planes
    for slot in range(CORES):
        for line in range(LINES):
            for plane in range(planes):
                inner = pl.ds((line * CORES + slot) * planes + plane, groups, stride=stride)
                outer = pl.ds((slot ^ core) * LINES + line, groups, stride=CORES * LINES)
                if gather:
                    natural_ref[plane, outer, :] = flat_ref[inner, :]
                else:
                    flat_ref[inner, :] = natural_ref[plane, outer, :]


def overlap_kernel(core_ref, flat_ref, natural_ref, packed_ref):
    for core in range(CORES):

        @pl.when(core_ref[0] == core)
        def _(core=core):
            natural_rows(flat_ref, natural_ref, core, True)

    planes, size, _ = natural_ref.shape
    half = planes // 2
    total = None
    for plane in range(0, half, 2):
        psi = jnp.concatenate([natural_ref[plane], natural_ref[plane + 1]], axis=1)
        images = jnp.concatenate(
            [natural_ref[half + plane], natural_ref[half + plane + 1]], axis=1
        )
        term = transposed_dot(psi, jnp.concatenate([psi, images], axis=0))
        total = term if total is None else total + term
    row = lax.broadcasted_iota(jnp.int32, (size, size), 0)
    column = lax.broadcasted_iota(jnp.int32, (size, size), 1)
    hamilton = total[:, size:]
    packed = jnp.where(row <= column, total[:, :size], hamilton)
    diagonal = jnp.sum(jnp.where(row == column, hamilton, 0.0), axis=1, keepdims=True)
    chunks = size // ROWS
    for part in range(size // LANES):
        packed_ref[:, part * ROWS : (part + 1) * ROWS, :] = packed[
            :, part * LANES : (part + 1) * LANES
        ].reshape(chunks, ROWS, LANES)
    packed_ref[:, size // LANES * ROWS :, :] = jnp.broadcast_to(
        diagonal, (size, LANES)
    ).reshape(chunks, ROWS, LANES)


def overlap(core, arrived):
    rows, lanes = arrived.shape
    planes = 2 * ROWS
    size = rows // planes
    return pl.pallas_call(
        overlap_kernel,
        out_shape=(
            jax.ShapeDtypeStruct((planes, size, lanes), jnp.float32),
            jax.ShapeDtypeStruct((size // ROWS, (size // LANES + 1) * ROWS, LANES), jnp.float32),
        ),
        in_specs=[smem(), vmem()],
        out_specs=(vmem(), vmem()),
        compiler_params=pltpu.CompilerParams(vmem_limit_bytes=40 * 2**20),
        cost_estimate=pl.CostEstimate(
            flops=24 * 256 * 256 * 1024, bytes_accessed=4 * 2**20, transcendentals=0
        ),
        name="overlap",
    )(core, arrived)


def eliminate(work):
    size = work.shape[0]
    sub = lax.broadcasted_iota(jnp.int32, (ROWS, LANES), 0)

    def row_of(tile, j):
        return jnp.broadcast_to(tile[j : j + 1, :], tile.shape)

    for start in range(0, size, BLOCK):
        stop = start + BLOCK
        first = start // LANES * LANES
        last = size + (stop + LANES - 1) // LANES * LANES
        lanes = range(first, last, LANES)
        groups = BLOCK // ROWS
        tiles = [
            {c: work[start + g * ROWS : start + (g + 1) * ROWS, c : c + LANES] for c in lanes}
            for g in range(groups)
        ]
        for q in range(groups):
            base = start + q * ROWS
            home, at = base // LANES * LANES, base % LANES
            spread = [
                [
                    jnp.broadcast_to(tiles[g][home][:, at + m : at + m + 1], (ROWS, LANES))
                    for m in range(ROWS)
                ]
                if g >= q
                else None
                for g in range(groups)
            ]
            scales = jnp.ones((ROWS, LANES), jnp.float32)
            for j in range(ROWS):
                pivot = row_of(spread[q][j], j)
                root = lax.rsqrt(pivot)
                root = root * (1.5 - 0.5 * pivot * root * root)
                scales = jnp.where(sub == j, root, scales)
                weight = {}
                for g in range(q, groups):
                    weight[g] = spread[g][j] * root
                weight[q] = jnp.where(sub > j, weight[q], 0.0)
                for m in range(j + 1, ROWS):
                    top = row_of(spread[q][m], j) * root
                    for g in range(q, groups):
                        spread[g][m] = spread[g][m] - weight[g] * top
                for c in lanes:
                    top = row_of(tiles[q][c], j) * root
                    for g in range(q, groups):
                        tiles[g][c] = tiles[g][c] - weight[g] * top
            for c in lanes:
                tiles[q][c] = tiles[q][c] * scales
        for g in range(groups):
            for c in lanes:
                work[start + g * ROWS : start + (g + 1) * ROWS, c : c + LANES] = tiles[g][c]
        if stop < size:
            low = stop // LANES * LANES
            done = work[start:stop, :]
            update = lax.dot_general(
                done[:, low:size],
                done[:, low:last],
                (((0,), (0,)), ((), ())),
                precision=precise,
                preferred_element_type=jnp.float32,
            )
            work[stop:, low:last] = work[stop:, low:last] - update[stop - low :, :]


def solve_kernel(cells, summed_ref, natural_ref, flat_ref, subspace_ref, work, mixed):
    def dot(a, b):
        return jnp.dot(a, b, precision=precise, preferred_element_type=jnp.float32)

    size = work.shape[0]
    parts = size // LANES
    tiles = [
        summed_ref[:, part * ROWS : (part + 1) * ROWS, :].reshape(size, LANES)
        for part in range(parts + 1)
    ]
    packed = jnp.concatenate(tiles[:parts], axis=1) * (1.0 / cells)
    diagonal = jnp.concatenate(tiles[parts:] * parts, axis=1) * (1.0 / cells)
    row = lax.broadcasted_iota(jnp.int32, (size, size), 0)
    column = lax.broadcasted_iota(jnp.int32, (size, size), 1)
    turned = packed.T
    work[:, :size] = jnp.where(row <= column, packed, turned)
    work[:, size:] = jnp.where(row == column, 1.0, 0.0)
    hamilton = jnp.where(row > column, packed, jnp.where(row == column, diagonal, turned))
    eliminate(work)
    inverse = jnp.where(row >= column, work[:, size:], 0.0)
    subspace = transposed_dot(dot(inverse, hamilton), inverse)
    subspace_ref[...] = subspace
    planes = natural_ref.shape[0]
    half = planes // 2
    for plane in range(0, half, 2):
        both = [
            dot(
                inverse,
                jnp.concatenate([natural_ref[plane + k], natural_ref[half + plane + k]], axis=1),
            )
            for k in range(2)
        ]
        product = dot(subspace, jnp.concatenate([part[:, :LANES] for part in both], axis=1))
        for k, part in enumerate(both):
            mixed[plane + k] = part[:, :LANES]
            mixed[half + plane + k] = part[:, LANES:] - product[:, k * LANES : (k + 1) * LANES]
    natural_rows(flat_ref, mixed, 0, False)


def solve(summed, natural, cells):
    planes, size, lanes = natural.shape
    return pl.pallas_call(
        functools.partial(solve_kernel, cells),
        out_shape=(
            jax.ShapeDtypeStruct((planes * size, lanes), jnp.float32),
            jax.ShapeDtypeStruct((size, size), jnp.float32),
        ),
        in_specs=[vmem()] * 2,
        out_specs=(vmem(), vmem()),
        scratch_shapes=[
            pltpu.VMEM((size, 2 * size), jnp.float32),
            pltpu.VMEM(natural.shape, jnp.float32),
        ],
        compiler_params=pltpu.CompilerParams(vmem_limit_bytes=48 * 2**20),
        cost_estimate=pl.CostEstimate(
            flops=20_000_000_000, bytes_accessed=6 * 2**20, transcendentals=256
        ),
        name="solve",
    )(summed, natural)


def assemble_kernel(core_ref, arrived_ref, received_ref, first_ref, second_ref, staged, sems):
    core = core_ref[0]
    blocks = received_ref.shape[0]
    copies = []
    for which, out_ref in enumerate((first_ref, second_ref)):
        for own in range(2):
            slot = 2 * which + own
            if own:
                staged[slot] = arrived_ref[:, pl.ds((core * 2 + which) * ROWS, ROWS), :]
            else:
                staged[slot] = received_ref[:, which * ROWS : (which + 1) * ROWS, :]
            side = core if own else 1 - core
            copy = pltpu.make_async_copy(
                staged.at[slot], out_ref.at[pl.ds(side * blocks, blocks)], sems.at[slot]
            )
            copy.start()
            copies.append(copy)
    for copy in copies:
        copy.wait()


def assemble(core, arrived, received):
    blocks, _, lanes = received.shape
    out = jax.ShapeDtypeStruct((CORES * blocks, ROWS, lanes), jnp.float32)
    anywhere = pl.BlockSpec(memory_space=pl.ANY)
    return pl.pallas_call(
        assemble_kernel,
        out_shape=(out, out),
        in_specs=[smem(), vmem(), vmem()],
        out_specs=(anywhere, anywhere),
        scratch_shapes=[
            pltpu.VMEM((4, blocks, ROWS, lanes), jnp.float32),
            pltpu.SemaphoreType.DMA((4,)),
        ],
        compiler_params=pltpu.CompilerParams(vmem_limit_bytes=32 * 2**20),
        cost_estimate=pl.CostEstimate(flops=0, bytes_accessed=4 * 2**20, transcendentals=0),
        name="assemble",
    )(core, arrived, received)


def exchange(blocks, groups, axes=AXES):
    return lax.all_to_all(
        blocks, axes, split_axis=0, concat_axis=0, tiled=True, axis_index_groups=groups
    )


class Layout:
    def __init__(self, orb, grp):
        self.x, self.core, self.y = 4, CORES, grp
        self.z = orb // (self.x * self.core)
        self.total = orb * grp

    def orb(self, z, x, core):
        return ((z % self.z) * self.x + x % self.x) * self.core + core % self.core

    def device(self, z, x, core, y):
        return self.orb(z, x, core) * self.y + y

    def places(self):
        return [
            (z, x, core)
            for z in range(self.z)
            for x in range(self.x)
            for core in range(self.core)
        ]

    def chips(self):
        return [
            [
                self.device(z, x, core, y)
                for z in range(self.z)
                for x in range(self.x)
                for y in range(self.y)
            ]
            for core in range(self.core)
        ]

    def planes(self):
        return [
            [
                self.device(z, x, core, y)
                for x in range(self.x)
                for core in range(self.core)
                for y in range(self.y)
            ]
            for z in range(self.z)
        ]

    def columns(self):
        return [
            [self.orb(z, x, core) for z in range(self.z)]
            for x in range(self.x)
            for core in range(self.core)
        ]

    def swap_cores(self, values):
        pairs = [(self.orb(z, x, c), self.orb(z, x, c + 1)) for z, x, c in self.places()]
        return lax.ppermute(values, "orb", pairs)


def reduce_slab(partial, layout):
    me = lax.axis_index("orb")
    core = me % layout.core
    x = me // layout.core % layout.x
    z = me // (layout.core * layout.x)
    y = lax.axis_index("grp")

    def stage(values, dim, count, index, axis, pairs):
        total = lax.dynamic_index_in_dim(values, index, dim, keepdims=False)
        arrived = [
            lax.ppermute(
                lax.dynamic_index_in_dim(values, (index + k) % count, dim, keepdims=False),
                axis,
                pairs(k),
            )
            for k in range(1, count)
        ]
        for term in arrived:
            total = total + term
        return total

    def along(dz, dx, dc):
        return lambda k: [
            (layout.orb(a, b, c), layout.orb(a + dz * k, b + dx * k, c + dc * k))
            for a, b, c in layout.places()
        ]

    def lines(k):
        return [(i, (i + k) % layout.y) for i in range(layout.y)]

    values = partial.reshape(layout.z, layout.x, layout.core, layout.y, -1, LANES)
    values = stage(values, 2, layout.core, core, "orb", along(0, 0, 1))
    values = stage(values, 2, layout.y, y, "grp", lines)
    values = stage(values, 1, layout.x, x, "orb", along(0, 1, 0))
    return values, lambda values: stage(values, 0, layout.z, z, "orb", along(1, 0, 0))


def sum_everywhere(chunks, layout):
    count, rows, lanes = chunks.shape

    def spread(values, copies):
        return jnp.broadcast_to(jnp.sum(values, axis=0, keepdims=True), (copies, rows, lanes))

    part = spread(exchange(chunks, layout.planes()), layout.z)
    part = spread(exchange(part, layout.columns(), "orb"), count)
    return exchange(part, layout.planes())


def on_device(layout, orbitals, potential, occupation, region_bounds):
    cell_total = orbitals.shape[1]
    orb, grp = lax.axis_index("orb"), lax.axis_index("grp")
    position = orb * layout.y + grp
    core = orb % layout.core
    place = jnp.stack([position, core]).astype(jnp.int32)
    core = core.reshape(1).astype(jnp.int32)
    keep, give, density_part = apply_hamiltonian(
        place, region_bounds, occupation, orbitals.reshape(G, PAIRS, LANES), potential
    )
    sent = jnp.concatenate([keep, layout.swap_cores(give)], axis=1)
    plane_density, along_z = reduce_slab(density_part, layout)
    arrived = exchange(sent, layout.chips())
    arrived, plane_density = lax.optimization_barrier((arrived, plane_density))
    natural, packed = overlap(core, arrived.reshape(-1, LANES))
    summed = sum_everywhere(packed, layout)
    mixed, subspace = solve(summed, natural, cell_total)
    mixed, plane_density = lax.optimization_barrier((mixed, plane_density))
    density = along_z(plane_density)
    back = exchange(mixed.reshape(-1, 4 * ROWS, LANES), layout.chips())
    other = lax.dynamic_slice_in_dim(back, (1 - core[0]) * 2 * ROWS, 2 * ROWS, 1)
    orthonormal, gradient = assemble(core, back, layout.swap_cores(other))
    return (
        orthonormal.reshape(1, cell_total),
        gradient.reshape(1, cell_total),
        subspace,
        density.reshape(-1, G),
    )


def solution(mesh):
    in_specs = (P(AXES, None), P(), P(), P())
    out_specs = (P(AXES, None), P(AXES, None), P(), P(AXES, None))
    step = functools.partial(on_device, Layout(mesh.shape["orb"], mesh.shape["grp"]))
    return jax.shard_map(
        step, mesh=mesh, in_specs=in_specs, out_specs=out_specs, check_vma=False
    )
```

```python
import functools

import jax
import jax.numpy as jnp
import ml_dtypes
import numpy as np
from jax import lax
from jax.experimental import pallas as pl
from jax.experimental.pallas import tpu as pltpu
from jax.sharding import PartitionSpec as P

G = 64
LANES = 128
PAIRS = G * G // LANES
PAD = 8
SHIFT = 2
STRIP = 16
ROWS = 8
BLOCK = 64

magic_taps = (0.0028, -0.0236, 0.1026, 0.8364, 0.1026, -0.0236, 0.0028)
kinetic_taps = (
    -1.0 / 560.0,
    8.0 / 315.0,
    -0.2,
    1.6,
    -205.0 / 72.0,
    1.6,
    -0.2,
    8.0 / 315.0,
    -1.0 / 560.0,
)
precise = lax.Precision.HIGHEST
AXES = ("orb", "grp")


def banded(extent, taps):
    radius = len(taps) // 2
    matrix = np.zeros((extent, extent))
    for position, weight in enumerate(taps):
        matrix += weight * np.eye(extent, k=position - radius)
    return matrix


def shifted_blocks(along_y, along_z):
    radius = len(along_y) // 2
    blocks = np.zeros((2 * SHIFT + 1, 2, G, 2, G))
    for shift in range(-SHIFT, SHIFT + 1):
        for source in range(2):
            for target in range(2):
                offset = 2 * shift + source - target
                if abs(offset) <= radius:
                    blocks[shift + SHIFT, source, :, target, :] = (
                        along_y[offset + radius] * along_z.T
                    )
    return blocks.reshape((2 * SHIFT + 1) * LANES, LANES)


def split_constant(matrix):
    high = matrix.astype(ml_dtypes.bfloat16)
    low = (matrix - high.astype(np.float64)).astype(ml_dtypes.bfloat16)
    return high, low


def filter_constants():
    magic = shifted_blocks(magic_taps, banded(G, magic_taps))
    kinetic = shifted_blocks(kinetic_taps, np.eye(G)) + shifted_blocks(
        (1.0,), banded(G, kinetic_taps)
    )
    return (
        split_constant(np.concatenate([magic, kinetic], axis=1)),
        split_constant(magic),
    )


def plane_filter(read, first, taps):
    radius = len(taps) // 2
    total = taps[radius] * read(first)
    for step in range(1, radius + 1):
        total += taps[radius + step] * (read(first + step) + read(first - step))
    return total


def hamiltonian_kernel(
    place_ref,
    occupation_ref,
    bounds_hbm,
    orbital_hbm,
    both_high_hbm,
    both_low_hbm,
    potential_hbm,
    magic_high_hbm,
    magic_low_hbm,
    keep_ref,
    give_ref,
    density_ref,
    bounds_ref,
    orbital_ref,
    both_high_ref,
    both_low_ref,
    potential_ref,
    magic_high_ref,
    magic_low_ref,
    source,
    filtered,
    kinetic,
    sems,
):
    margin = len(kinetic_taps) // 2
    position, core = place_ref[0], place_ref[1]
    copies = [
        pltpu.make_async_copy(far, near, sems.at[k])
        for k, (far, near) in enumerate(
            (
                (bounds_hbm, bounds_ref),
                (orbital_hbm, orbital_ref),
                (both_high_hbm, both_high_ref),
                (both_low_hbm, both_low_ref),
                (potential_hbm, potential_ref),
                (magic_high_hbm, magic_high_ref),
                (magic_low_hbm, magic_low_ref),
            )
        )
    ]
    for copy in copies:
        copy.start()

    zeros = jnp.zeros((margin, PAIRS + 2 * PAD, LANES), jnp.float32)
    source[:margin] = zeros
    source[margin + G :] = zeros
    edge = jnp.zeros((G + 2 * margin, PAD, LANES), jnp.float32)
    source[:, :PAD] = edge
    source[:, PAD + PAIRS :] = edge
    zeros = jnp.zeros((margin, PAIRS, LANES), jnp.float32)
    filtered[:margin] = zeros
    filtered[margin + G :] = zeros

    def product(x, high_ref, low_ref):
        shifted = jnp.concatenate(
            [
                source[pl.ds(margin + x, STRIP), PAD + s : PAD + s + PAIRS].reshape(
                    STRIP * PAIRS, LANES
                )
                for s in range(-SHIFT, SHIFT + 1)
            ],
            axis=1,
        )
        high = shifted.astype(jnp.bfloat16)
        low = (shifted - high.astype(jnp.float32)).astype(jnp.bfloat16)
        dot = functools.partial(jnp.dot, preferred_element_type=jnp.float32)
        return dot(high, high_ref[...]) + (dot(low, high_ref[...]) + dot(high, low_ref[...]))

    def own(x):
        return source[pl.ds(margin + x, STRIP), PAD : PAD + PAIRS]

    def half(x):
        return filtered[pl.ds(margin + x, STRIP)]

    copies[0].wait()
    copies[1].wait()
    planes = lax.broadcasted_iota(jnp.int32, (STRIP * PAIRS, LANES), 0) // PAIRS
    bounds = bounds_ref[pl.ds(position, 1), :]
    begin, end = bounds[:, 0:1], bounds[:, 1:2]
    blocks = STRIP * PAIRS // ROWS
    half_planes = G // 2

    def tiled(strip):
        return strip.reshape(blocks, ROWS, LANES)

    for side, out_ref in ((core, keep_ref), (1 - core, give_ref)):
        for strip in range(0, half_planes, STRIP):
            x = half_planes * side + strip
            inside = (planes + x >= begin) & (planes + x < end)
            orbital = orbital_ref[pl.ds(x, STRIP)].reshape(STRIP * PAIRS, LANES)
            masked = jnp.where(inside, orbital, 0.0).reshape(STRIP, PAIRS, LANES)
            source[pl.ds(margin + x, STRIP), PAD : PAD + PAIRS] = masked
            first = strip * PAIRS // ROWS
            out_ref[first : first + blocks, :ROWS, :] = tiled(masked)

    copies[2].wait()
    copies[3].wait()

    @pl.loop(0, G, step=STRIP)
    def _(x):
        both = product(x, both_high_ref, both_low_ref)
        filtered[pl.ds(margin + x, STRIP)] = both[:, :LANES].reshape(STRIP, PAIRS, LANES)
        kinetic[pl.ds(x, STRIP)] = both[:, LANES:].reshape(STRIP, PAIRS, LANES) + plane_filter(
            own, x, kinetic_taps
        )

    copies[4].wait()
    scale = occupation_ref[position] * (1.0 / occupation_ref.shape[0])
    lines = STRIP * G // 2

    @pl.loop(0, G, step=STRIP)
    def _(x):
        realspace = plane_filter(half, x, magic_taps)
        density_ref[pl.ds(x, STRIP)] = scale * realspace * realspace
        potential = jnp.concatenate(
            [potential_ref[pl.ds(x * G + odd, lines, stride=2), :] for odd in range(2)], axis=1
        ).reshape(STRIP, PAIRS, LANES)
        source[pl.ds(margin + x, STRIP), PAD : PAD + PAIRS] = realspace * potential

    copies[5].wait()
    copies[6].wait()

    @pl.loop(0, G, step=STRIP)
    def _(x):
        filtered[pl.ds(margin + x, STRIP)] = product(x, magic_high_ref, magic_low_ref).reshape(
            STRIP, PAIRS, LANES
        )

    for side, out_ref in ((core, keep_ref), (1 - core, give_ref)):
        for strip in range(0, half_planes, STRIP):
            x = half_planes * side + strip
            images = plane_filter(half, x, magic_taps) - 0.5 * kinetic[pl.ds(x, STRIP)]
            first = strip * PAIRS // ROWS
            out_ref[first : first + blocks, ROWS:, :] = tiled(images)


def vmem():
    return pl.BlockSpec(memory_space=pltpu.VMEM)


def smem():
    return pl.BlockSpec(memory_space=pltpu.SMEM)


def anywhere():
    return pl.BlockSpec(memory_space=pl.ANY)


def apply_hamiltonian(place, region_bounds, occupation, orbital, potential):
    (both_high, both_low), (magic_high, magic_low) = filter_constants()
    margin = len(kinetic_taps) // 2
    side = jax.ShapeDtypeStruct((G * PAIRS // ROWS // 2, 2 * ROWS, LANES), jnp.float32)
    grid = jax.ShapeDtypeStruct((G, PAIRS, LANES), jnp.float32)
    far = (region_bounds, orbital, both_high, both_low, potential, magic_high, magic_low)
    far = [jnp.asarray(values) for values in far]
    return pl.pallas_call(
        hamiltonian_kernel,
        out_shape=(side, side, grid),
        in_specs=[smem()] * 2 + [anywhere()] * len(far),
        out_specs=(vmem(),) * 3,
        scratch_shapes=[pltpu.VMEM(values.shape, values.dtype) for values in far]
        + [
            pltpu.VMEM((G + 2 * margin, PAIRS + 2 * PAD, LANES), jnp.float32),
            pltpu.VMEM((G + 2 * margin, PAIRS, LANES), jnp.float32),
            pltpu.VMEM((G, PAIRS, LANES), jnp.float32),
            pltpu.SemaphoreType.DMA((len(far),)),
        ],
        compiler_params=pltpu.CompilerParams(vmem_limit_bytes=40 * 2**20),
        cost_estimate=pl.CostEstimate(
            flops=6 * 2048 * 640 * 384, bytes_accessed=5 * 2**20, transcendentals=0
        ),
        name="hamiltonian",
    )(place, occupation, *far)


def transposed_dot(a, b):
    return lax.dot_general(
        a, b, (((1,), (1,)), ((), ())), precision=precise, preferred_element_type=jnp.float32
    )


CORES = 2
LINES = 4


def natural_rows(flat_ref, natural_ref, core, gather, part=0, parts=1):
    planes, orbitals, _ = natural_ref.shape
    groups = orbitals // (CORES * LINES * parts)
    stride = CORES * LINES * planes
    for slot in range(CORES):
        for line in range(LINES):
            for plane in range(planes):
                inner = (line * CORES + slot) * planes + plane + part * groups * stride
                inner = pl.ds(inner, groups, stride=stride)
                outer = (slot ^ core) * LINES + line + part * groups * CORES * LINES
                outer = pl.ds(outer, groups, stride=CORES * LINES)
                if gather:
                    natural_ref[plane, outer, :] = flat_ref[inner, :]
                else:
                    flat_ref[inner, :] = natural_ref[plane, outer, :]


def overlap_kernel(core_ref, flat_ref, natural_hbm, packed_ref, natural_ref, sem):
    for core in range(CORES):

        @pl.when(core_ref[0] == core)
        def _(core=core):
            natural_rows(flat_ref, natural_ref, core, True)

    copy = pltpu.make_async_copy(natural_ref, natural_hbm, sem)
    copy.start()
    planes, size, _ = natural_ref.shape
    half = planes // 2
    total = None
    for plane in range(0, half, 2):
        psi = jnp.concatenate([natural_ref[plane], natural_ref[plane + 1]], axis=1)
        images = jnp.concatenate(
            [natural_ref[half + plane], natural_ref[half + plane + 1]], axis=1
        )
        term = transposed_dot(psi, jnp.concatenate([psi, images], axis=0))
        total = term if total is None else total + term
    row = lax.broadcasted_iota(jnp.int32, (size, size), 0)
    column = lax.broadcasted_iota(jnp.int32, (size, size), 1)
    hamilton = total[:, size:]
    packed = jnp.where(row <= column, total[:, :size], hamilton)
    diagonal = jnp.sum(jnp.where(row == column, hamilton, 0.0), axis=1, keepdims=True)
    chunks = size // ROWS
    for part in range(size // LANES):
        packed_ref[:, part * ROWS : (part + 1) * ROWS, :] = packed[
            :, part * LANES : (part + 1) * LANES
        ].reshape(chunks, ROWS, LANES)
    packed_ref[:, size // LANES * ROWS :, :] = jnp.broadcast_to(
        diagonal, (size, LANES)
    ).reshape(chunks, ROWS, LANES)
    copy.wait()


def overlap(core, arrived):
    rows, lanes = arrived.shape
    planes = 2 * ROWS
    size = rows // planes
    return pl.pallas_call(
        overlap_kernel,
        out_shape=(
            jax.ShapeDtypeStruct((planes, size, lanes), jnp.float32),
            jax.ShapeDtypeStruct((size // ROWS, (size // LANES + 1) * ROWS, LANES), jnp.float32),
        ),
        in_specs=[smem(), vmem()],
        out_specs=(anywhere(), vmem()),
        scratch_shapes=[
            pltpu.VMEM((planes, size, lanes), jnp.float32),
            pltpu.SemaphoreType.DMA,
        ],
        compiler_params=pltpu.CompilerParams(vmem_limit_bytes=40 * 2**20),
        cost_estimate=pl.CostEstimate(
            flops=24 * 256 * 256 * 1024, bytes_accessed=4 * 2**20, transcendentals=0
        ),
        name="overlap",
    )(core, arrived)


def eliminate(work):
    size = work.shape[0]
    sub = lax.broadcasted_iota(jnp.int32, (ROWS, LANES), 0)

    def row_of(tile, j):
        return jnp.broadcast_to(tile[j : j + 1, :], tile.shape)

    for start in range(0, size, BLOCK):
        stop = start + BLOCK
        first = start // LANES * LANES
        last = size + (stop + LANES - 1) // LANES * LANES
        lanes = range(first, last, LANES)
        groups = BLOCK // ROWS
        tiles = [
            {c: work[start + g * ROWS : start + (g + 1) * ROWS, c : c + LANES] for c in lanes}
            for g in range(groups)
        ]
        for q in range(groups):
            base = start + q * ROWS
            home, at = base // LANES * LANES, base % LANES
            spread = [
                [
                    jnp.broadcast_to(tiles[g][home][:, at + m : at + m + 1], (ROWS, LANES))
                    for m in range(ROWS)
                ]
                if g >= q
                else None
                for g in range(groups)
            ]
            scales = jnp.ones((ROWS, LANES), jnp.float32)
            for j in range(ROWS):
                pivot = row_of(spread[q][j], j)
                root = lax.rsqrt(pivot)
                scales = jnp.where(sub == j, root, scales)
                weight = {}
                for g in range(q, groups):
                    below = spread[g][j]
                    if g == q:
                        below = jnp.where(sub > j, below, 0.0)
                    weight[g] = below * root
                for m in range(j + 1, ROWS):
                    top = row_of(spread[q][m], j) * root
                    for g in range(q, groups):
                        spread[g][m] = spread[g][m] - weight[g] * top
                for c in lanes:
                    top = row_of(tiles[q][c], j) * root
                    for g in range(q, groups):
                        tiles[g][c] = tiles[g][c] - weight[g] * top
            for c in lanes:
                tiles[q][c] = tiles[q][c] * scales
        for g in range(groups):
            for c in lanes:
                work[start + g * ROWS : start + (g + 1) * ROWS, c : c + LANES] = tiles[g][c]
        if stop < size:
            low = stop // LANES * LANES
            done = work[start:stop, :]
            update = lax.dot_general(
                done[:, low:size],
                done[:, low:last],
                (((0,), (0,)), ((), ())),
                precision=precise,
                preferred_element_type=jnp.float32,
            )
            work[stop:, low:last] = work[stop:, low:last] - update[stop - low :, :]


def solve_kernel(
    cells,
    summed_ref,
    natural_hbm,
    flat_hbm,
    subspace_ref,
    work,
    natural_ref,
    mixed,
    flat_ref,
    in_sem,
    out_sems,
):
    arrival = pltpu.make_async_copy(natural_hbm, natural_ref, in_sem)
    arrival.start()

    def dot(a, b):
        return jnp.dot(a, b, precision=precise, preferred_element_type=jnp.float32)

    size = work.shape[0]
    parts = size // LANES
    tiles = [
        summed_ref[:, part * ROWS : (part + 1) * ROWS, :].reshape(size, LANES)
        for part in range(parts + 1)
    ]
    packed = jnp.concatenate(tiles[:parts], axis=1) * (1.0 / cells)
    diagonal = jnp.concatenate(tiles[parts:] * parts, axis=1) * (1.0 / cells)
    row = lax.broadcasted_iota(jnp.int32, (size, size), 0)
    column = lax.broadcasted_iota(jnp.int32, (size, size), 1)
    turned = packed.T
    work[:, :size] = jnp.where(row <= column, packed, turned)
    work[:, size:] = jnp.where(row == column, 1.0, 0.0)
    hamilton = jnp.where(row > column, packed, jnp.where(row == column, diagonal, turned))
    eliminate(work)
    inverse = jnp.where(row >= column, work[:, size:], 0.0)
    subspace = transposed_dot(dot(inverse, hamilton), inverse)
    subspace_ref[...] = subspace
    planes = natural_ref.shape[0]
    half = planes // 2
    arrival.wait()
    for plane in range(0, half, 2):
        both = [
            dot(
                inverse,
                jnp.concatenate([natural_ref[plane + k], natural_ref[half + plane + k]], axis=1),
            )
            for k in range(2)
        ]
        product = dot(subspace, jnp.concatenate([part[:, :LANES] for part in both], axis=1))
        for k, part in enumerate(both):
            mixed[plane + k] = part[:, :LANES]
            mixed[half + plane + k] = part[:, LANES:] - product[:, k * LANES : (k + 1) * LANES]
    parts = 4
    rows = flat_ref.shape[0] // parts
    copies = []
    for part in range(parts):
        natural_rows(flat_ref, mixed, 0, False, part, parts)
        here = pl.ds(part * rows, rows)
        copy = pltpu.make_async_copy(flat_ref.at[here], flat_hbm.at[here], out_sems.at[part])
        copy.start()
        copies.append(copy)
    for copy in copies:
        copy.wait()


def solve(summed, natural, cells):
    planes, size, lanes = natural.shape
    return pl.pallas_call(
        functools.partial(solve_kernel, cells),
        out_shape=(
            jax.ShapeDtypeStruct((planes * size, lanes), jnp.float32),
            jax.ShapeDtypeStruct((size, size), jnp.float32),
        ),
        in_specs=[vmem(), anywhere()],
        out_specs=(anywhere(), vmem()),
        scratch_shapes=[
            pltpu.VMEM((size, 2 * size), jnp.float32),
            pltpu.VMEM(natural.shape, jnp.float32),
            pltpu.VMEM(natural.shape, jnp.float32),
            pltpu.VMEM((planes * size, lanes), jnp.float32),
            pltpu.SemaphoreType.DMA,
            pltpu.SemaphoreType.DMA((4,)),
        ],
        compiler_params=pltpu.CompilerParams(vmem_limit_bytes=48 * 2**20),
        cost_estimate=pl.CostEstimate(
            flops=20_000_000_000, bytes_accessed=6 * 2**20, transcendentals=256
        ),
        name="solve",
    )(summed, natural)


def assemble_kernel(core_ref, arrived_ref, received_ref, first_ref, second_ref, staged, sems):
    core = core_ref[0]
    blocks = received_ref.shape[0]
    copies = []
    for which, out_ref in enumerate((first_ref, second_ref)):
        for own in range(2):
            slot = 2 * which + own
            if own:
                staged[slot] = arrived_ref[:, pl.ds((core * 2 + which) * ROWS, ROWS), :]
            else:
                staged[slot] = received_ref[:, which * ROWS : (which + 1) * ROWS, :]
            side = core if own else 1 - core
            copy = pltpu.make_async_copy(
                staged.at[slot], out_ref.at[pl.ds(side * blocks, blocks)], sems.at[slot]
            )
            copy.start()
            copies.append(copy)
    for copy in copies:
        copy.wait()


def assemble(core, arrived, received):
    blocks, _, lanes = received.shape
    out = jax.ShapeDtypeStruct((CORES * blocks, ROWS, lanes), jnp.float32)
    return pl.pallas_call(
        assemble_kernel,
        out_shape=(out, out),
        in_specs=[smem(), vmem(), vmem()],
        out_specs=(anywhere(), anywhere()),
        scratch_shapes=[
            pltpu.VMEM((4, blocks, ROWS, lanes), jnp.float32),
            pltpu.SemaphoreType.DMA((4,)),
        ],
        compiler_params=pltpu.CompilerParams(vmem_limit_bytes=32 * 2**20),
        cost_estimate=pl.CostEstimate(flops=0, bytes_accessed=4 * 2**20, transcendentals=0),
        name="assemble",
    )(core, arrived, received)


def exchange(blocks, groups, axes=AXES):
    return lax.all_to_all(
        blocks, axes, split_axis=0, concat_axis=0, tiled=True, axis_index_groups=groups
    )


class Layout:
    def __init__(self, orb, grp):
        self.x, self.core, self.y = 4, CORES, grp
        self.z = orb // (self.x * self.core)
        self.total = orb * grp

    def orb(self, z, x, core):
        return ((z % self.z) * self.x + x % self.x) * self.core + core % self.core

    def device(self, z, x, core, y):
        return self.orb(z, x, core) * self.y + y

    def places(self):
        return [
            (z, x, core)
            for z in range(self.z)
            for x in range(self.x)
            for core in range(self.core)
        ]

    def chips(self):
        return [
            [
                self.device(z, x, core, y)
                for z in range(self.z)
                for x in range(self.x)
                for y in range(self.y)
            ]
            for core in range(self.core)
        ]

    def planes(self):
        return [
            [
                self.device(z, x, core, y)
                for x in range(self.x)
                for core in range(self.core)
                for y in range(self.y)
            ]
            for z in range(self.z)
        ]

    def columns(self):
        return [
            [self.orb(z, x, core) for z in range(self.z)]
            for x in range(self.x)
            for core in range(self.core)
        ]

    def swap_cores(self, values):
        pairs = [(self.orb(z, x, c), self.orb(z, x, c + 1)) for z, x, c in self.places()]
        return lax.ppermute(values, "orb", pairs)


def reduce_slab(partial, layout):
    me = lax.axis_index("orb")
    core = me % layout.core
    x = me // layout.core % layout.x
    y = lax.axis_index("grp")

    def stage(values, dim, count, index, axis, pairs):
        total = lax.dynamic_index_in_dim(values, index, dim, keepdims=False)
        arrived = [
            lax.ppermute(
                lax.dynamic_index_in_dim(values, (index + k) % count, dim, keepdims=False),
                axis,
                pairs(k),
            )
            for k in range(1, count)
        ]
        for term in arrived:
            total = total + term
        return total

    def along(dx, dc):
        return lambda k: [
            (layout.orb(a, b, c), layout.orb(a, b + dx * k, c + dc * k))
            for a, b, c in layout.places()
        ]

    def lines(k):
        return [(i, (i + k) % layout.y) for i in range(layout.y)]

    values = partial.reshape(layout.z, layout.x, layout.core, layout.y, -1, LANES)
    values = stage(values, 2, layout.core, core, "orb", along(0, 1))
    values = stage(values, 2, layout.y, y, "grp", lines)
    return stage(values, 1, layout.x, x, "orb", along(1, 0))


def sum_everywhere(chunks, slabs, layout):
    count, rows, lanes = chunks.shape
    part = jnp.sum(exchange(chunks, layout.planes()), axis=0, keepdims=True)
    part = jnp.broadcast_to(part, (layout.z, rows, lanes))
    part = exchange(jnp.concatenate([part, slabs], axis=1), layout.columns(), "orb")
    total = jnp.sum(part, axis=0)
    everywhere = jnp.broadcast_to(total[None, :rows], (count, rows, lanes))
    return exchange(everywhere, layout.planes()), total[rows:]


def on_device(layout, orbitals, potential, occupation, region_bounds):
    cell_total = orbitals.shape[1]
    orb, grp = lax.axis_index("orb"), lax.axis_index("grp")
    position = orb * layout.y + grp
    core = orb % layout.core
    place = jnp.stack([position, core]).astype(jnp.int32)
    core = core.reshape(1).astype(jnp.int32)
    keep, give, density_part = apply_hamiltonian(
        place, region_bounds, occupation, orbitals.reshape(G, PAIRS, LANES), potential
    )
    sent = jnp.concatenate([keep, layout.swap_cores(give)], axis=1)
    slabs = reduce_slab(density_part, layout)
    arrived = exchange(sent, layout.chips())
    arrived, slabs = lax.optimization_barrier((arrived, slabs))
    natural, packed = overlap(core, arrived.reshape(-1, LANES))
    summed, density = sum_everywhere(packed, slabs, layout)
    mixed, subspace = solve(summed, natural, cell_total)
    back = exchange(mixed.reshape(-1, 4 * ROWS, LANES), layout.chips())
    other = lax.dynamic_slice_in_dim(back, (1 - core[0]) * 2 * ROWS, 2 * ROWS, 1)
    orthonormal, gradient = assemble(core, back, layout.swap_cores(other))
    return (
        orthonormal.reshape(1, cell_total),
        gradient.reshape(1, cell_total),
        subspace,
        density.reshape(-1, G),
    )


def solution(mesh):
    in_specs = (P(AXES, None), P(), P(), P())
    out_specs = (P(AXES, None), P(AXES, None), P(), P(AXES, None))
    step = functools.partial(on_device, Layout(mesh.shape["orb"], mesh.shape["grp"]))
    return jax.shard_map(
        step, mesh=mesh, in_specs=in_specs, out_specs=out_specs, check_vma=False
    )
```

```python
import functools

import jax
import jax.numpy as jnp
import ml_dtypes
import numpy as np
from jax import lax
from jax.experimental import pallas as pl
from jax.experimental.pallas import tpu as pltpu
from jax.sharding import PartitionSpec as P

G = 64
LANES = 128
PAIRS = G * G // LANES
PAD = 8
SHIFT = 2
STRIP = 16
ROWS = 8
BLOCK = 64

magic_taps = (0.0028, -0.0236, 0.1026, 0.8364, 0.1026, -0.0236, 0.0028)
kinetic_taps = (
    -1.0 / 560.0,
    8.0 / 315.0,
    -0.2,
    1.6,
    -205.0 / 72.0,
    1.6,
    -0.2,
    8.0 / 315.0,
    -1.0 / 560.0,
)
precise = lax.Precision.HIGHEST
AXES = ("orb", "grp")


def banded(extent, taps):
    radius = len(taps) // 2
    matrix = np.zeros((extent, extent))
    for position, weight in enumerate(taps):
        matrix += weight * np.eye(extent, k=position - radius)
    return matrix


def shifted_blocks(along_y, along_z):
    radius = len(along_y) // 2
    blocks = np.zeros((2 * SHIFT + 1, 2, G, 2, G))
    for shift in range(-SHIFT, SHIFT + 1):
        for source in range(2):
            for target in range(2):
                offset = 2 * shift + source - target
                if abs(offset) <= radius:
                    blocks[shift + SHIFT, source, :, target, :] = (
                        along_y[offset + radius] * along_z.T
                    )
    return blocks.reshape((2 * SHIFT + 1) * LANES, LANES)


def split_constant(matrix):
    high = matrix.astype(ml_dtypes.bfloat16)
    low = (matrix - high.astype(np.float64)).astype(ml_dtypes.bfloat16)
    return high, low


def filter_constants():
    magic = shifted_blocks(magic_taps, banded(G, magic_taps))
    kinetic = shifted_blocks(kinetic_taps, np.eye(G)) + shifted_blocks(
        (1.0,), banded(G, kinetic_taps)
    )
    return (
        split_constant(np.concatenate([magic, kinetic], axis=1)),
        split_constant(magic),
    )


def plane_filter(read, first, taps):
    radius = len(taps) // 2
    total = taps[radius] * read(first)
    for step in range(1, radius + 1):
        total += taps[radius + step] * (read(first + step) + read(first - step))
    return total


def hamiltonian_kernel(
    place_ref,
    occupation_ref,
    bounds_hbm,
    orbital_hbm,
    both_high_hbm,
    both_low_hbm,
    potential_hbm,
    magic_high_hbm,
    magic_low_hbm,
    keep_ref,
    give_ref,
    density_ref,
    bounds_ref,
    orbital_ref,
    both_high_ref,
    both_low_ref,
    potential_ref,
    magic_high_ref,
    magic_low_ref,
    source,
    filtered,
    kinetic,
    sems,
):
    margin = len(kinetic_taps) // 2
    position, core = place_ref[0], place_ref[1]
    copies = [
        pltpu.make_async_copy(far, near, sems.at[k])
        for k, (far, near) in enumerate(
            (
                (bounds_hbm, bounds_ref),
                (orbital_hbm, orbital_ref),
                (both_high_hbm, both_high_ref),
                (both_low_hbm, both_low_ref),
                (potential_hbm, potential_ref),
                (magic_high_hbm, magic_high_ref),
                (magic_low_hbm, magic_low_ref),
            )
        )
    ]
    for copy in copies:
        copy.start()

    zeros = jnp.zeros((margin, PAIRS + 2 * PAD, LANES), jnp.float32)
    source[:margin] = zeros
    source[margin + G :] = zeros
    edge = jnp.zeros((G + 2 * margin, PAD, LANES), jnp.float32)
    source[:, :PAD] = edge
    source[:, PAD + PAIRS :] = edge
    zeros = jnp.zeros((margin, PAIRS, LANES), jnp.float32)
    filtered[:margin] = zeros
    filtered[margin + G :] = zeros

    def product(x, high_ref, low_ref):
        shifted = jnp.concatenate(
            [
                source[pl.ds(margin + x, STRIP), PAD + s : PAD + s + PAIRS].reshape(
                    STRIP * PAIRS, LANES
                )
                for s in range(-SHIFT, SHIFT + 1)
            ],
            axis=1,
        )
        high = shifted.astype(jnp.bfloat16)
        low = (shifted - high.astype(jnp.float32)).astype(jnp.bfloat16)
        dot = functools.partial(jnp.dot, preferred_element_type=jnp.float32)
        return dot(high, high_ref[...]) + (dot(low, high_ref[...]) + dot(high, low_ref[...]))

    def own(x):
        return source[pl.ds(margin + x, STRIP), PAD : PAD + PAIRS]

    def half(x):
        return filtered[pl.ds(margin + x, STRIP)]

    copies[0].wait()
    copies[1].wait()
    planes = lax.broadcasted_iota(jnp.int32, (STRIP * PAIRS, LANES), 0) // PAIRS
    bounds = bounds_ref[pl.ds(position, 1), :]
    begin, end = bounds[:, 0:1], bounds[:, 1:2]
    blocks = STRIP * PAIRS // ROWS
    half_planes = G // 2

    def tiled(strip):
        return strip.reshape(blocks, ROWS, LANES)

    for side, out_ref in ((core, keep_ref), (1 - core, give_ref)):
        for strip in range(0, half_planes, STRIP):
            x = half_planes * side + strip
            inside = (planes + x >= begin) & (planes + x < end)
            orbital = orbital_ref[pl.ds(x, STRIP)].reshape(STRIP * PAIRS, LANES)
            masked = jnp.where(inside, orbital, 0.0).reshape(STRIP, PAIRS, LANES)
            source[pl.ds(margin + x, STRIP), PAD : PAD + PAIRS] = masked
            first = strip * PAIRS // ROWS
            out_ref[first : first + blocks, :ROWS, :] = tiled(masked)

    copies[2].wait()
    copies[3].wait()

    @pl.loop(0, G, step=STRIP)
    def _(x):
        both = product(x, both_high_ref, both_low_ref)
        filtered[pl.ds(margin + x, STRIP)] = both[:, :LANES].reshape(STRIP, PAIRS, LANES)
        kinetic[pl.ds(x, STRIP)] = both[:, LANES:].reshape(STRIP, PAIRS, LANES) + plane_filter(
            own, x, kinetic_taps
        )

    copies[4].wait()
    scale = occupation_ref[position] * (1.0 / occupation_ref.shape[0])
    lines = STRIP * G // 2

    @pl.loop(0, G, step=STRIP)
    def _(x):
        realspace = plane_filter(half, x, magic_taps)
        density_ref[pl.ds(x, STRIP)] = scale * realspace * realspace
        potential = jnp.concatenate(
            [potential_ref[pl.ds(x * G + odd, lines, stride=2), :] for odd in range(2)], axis=1
        ).reshape(STRIP, PAIRS, LANES)
        source[pl.ds(margin + x, STRIP), PAD : PAD + PAIRS] = realspace * potential

    copies[5].wait()
    copies[6].wait()

    @pl.loop(0, G, step=STRIP)
    def _(x):
        filtered[pl.ds(margin + x, STRIP)] = product(x, magic_high_ref, magic_low_ref).reshape(
            STRIP, PAIRS, LANES
        )

    for side, out_ref in ((core, keep_ref), (1 - core, give_ref)):
        for strip in range(0, half_planes, STRIP):
            x = half_planes * side + strip
            images = plane_filter(half, x, magic_taps) - 0.5 * kinetic[pl.ds(x, STRIP)]
            first = strip * PAIRS // ROWS
            out_ref[first : first + blocks, ROWS:, :] = tiled(images)


def vmem():
    return pl.BlockSpec(memory_space=pltpu.VMEM)


def smem():
    return pl.BlockSpec(memory_space=pltpu.SMEM)


def far_away():
    return pl.BlockSpec(memory_space=pltpu.HBM)


def apply_hamiltonian(place, region_bounds, occupation, orbital, potential):
    (both_high, both_low), (magic_high, magic_low) = filter_constants()
    margin = len(kinetic_taps) // 2
    side = jax.ShapeDtypeStruct((G * PAIRS // ROWS // 2, 2 * ROWS, LANES), jnp.float32)
    grid = jax.ShapeDtypeStruct((G, PAIRS, LANES), jnp.float32)
    far = (region_bounds, orbital, both_high, both_low, potential, magic_high, magic_low)
    far = [jnp.asarray(values) for values in far]
    return pl.pallas_call(
        hamiltonian_kernel,
        out_shape=(side, side, grid),
        in_specs=[smem()] * 2 + [far_away()] * len(far),
        out_specs=(vmem(),) * 3,
        scratch_shapes=[pltpu.VMEM(values.shape, values.dtype) for values in far]
        + [
            pltpu.VMEM((G + 2 * margin, PAIRS + 2 * PAD, LANES), jnp.float32),
            pltpu.VMEM((G + 2 * margin, PAIRS, LANES), jnp.float32),
            pltpu.VMEM((G, PAIRS, LANES), jnp.float32),
            pltpu.SemaphoreType.DMA((len(far),)),
        ],
        compiler_params=pltpu.CompilerParams(vmem_limit_bytes=40 * 2**20),
        cost_estimate=pl.CostEstimate(
            flops=6 * 2048 * 640 * 384, bytes_accessed=5 * 2**20, transcendentals=0
        ),
        name="hamiltonian",
    )(place, occupation, *far)


def transposed_dot(a, b):
    return lax.dot_general(
        a, b, (((1,), (1,)), ((), ())), precision=precise, preferred_element_type=jnp.float32
    )


CORES = 2
LINES = 4


def natural_rows(flat_ref, natural_ref, core, gather, part=0, parts=1):
    planes, orbitals, _ = natural_ref.shape
    groups = orbitals // (CORES * LINES * parts)
    stride = CORES * LINES * planes
    for slot in range(CORES):
        for line in range(LINES):
            for plane in range(planes):
                inner = (line * CORES + slot) * planes + plane + part * groups * stride
                inner = pl.ds(inner, groups, stride=stride)
                outer = (slot ^ core) * LINES + line + part * groups * CORES * LINES
                outer = pl.ds(outer, groups, stride=CORES * LINES)
                if gather:
                    natural_ref[plane, outer, :] = flat_ref[inner, :]
                else:
                    flat_ref[inner, :] = natural_ref[plane, outer, :]


def overlap_kernel(core_ref, flat_ref, natural_hbm, packed_ref, natural_ref, sem):
    for core in range(CORES):

        @pl.when(core_ref[0] == core)
        def _(core=core):
            natural_rows(flat_ref, natural_ref, core, True)

    copy = pltpu.make_async_copy(natural_ref, natural_hbm, sem)
    copy.start()
    planes, size, _ = natural_ref.shape
    half = planes // 2
    total = None
    for plane in range(0, half, 2):
        psi = jnp.concatenate([natural_ref[plane], natural_ref[plane + 1]], axis=1)
        images = jnp.concatenate(
            [natural_ref[half + plane], natural_ref[half + plane + 1]], axis=1
        )
        term = transposed_dot(psi, jnp.concatenate([psi, images], axis=0))
        total = term if total is None else total + term
    row = lax.broadcasted_iota(jnp.int32, (size, size), 0)
    column = lax.broadcasted_iota(jnp.int32, (size, size), 1)
    hamilton = total[:, size:]
    packed = jnp.where(row <= column, total[:, :size], hamilton)
    diagonal = jnp.sum(jnp.where(row == column, hamilton, 0.0), axis=1, keepdims=True)
    chunks = size // ROWS
    for part in range(size // LANES):
        packed_ref[:, part * ROWS : (part + 1) * ROWS, :] = packed[
            :, part * LANES : (part + 1) * LANES
        ].reshape(chunks, ROWS, LANES)
    packed_ref[:, size // LANES * ROWS :, :] = jnp.broadcast_to(
        diagonal, (size, LANES)
    ).reshape(chunks, ROWS, LANES)
    copy.wait()


def overlap(core, arrived):
    rows, lanes = arrived.shape
    planes = 2 * ROWS
    size = rows // planes
    return pl.pallas_call(
        overlap_kernel,
        out_shape=(
            jax.ShapeDtypeStruct((planes, size, lanes), jnp.float32),
            jax.ShapeDtypeStruct((size // ROWS, (size // LANES + 1) * ROWS, LANES), jnp.float32),
        ),
        in_specs=[smem(), vmem()],
        out_specs=(far_away(), vmem()),
        scratch_shapes=[
            pltpu.VMEM((planes, size, lanes), jnp.float32),
            pltpu.SemaphoreType.DMA,
        ],
        compiler_params=pltpu.CompilerParams(vmem_limit_bytes=40 * 2**20),
        cost_estimate=pl.CostEstimate(
            flops=24 * 256 * 256 * 1024, bytes_accessed=4 * 2**20, transcendentals=0
        ),
        name="overlap",
    )(core, arrived)


def eliminate(work):
    size = work.shape[0]
    sub = lax.broadcasted_iota(jnp.int32, (ROWS, LANES), 0)

    def row_of(tile, j):
        return jnp.broadcast_to(tile[j : j + 1, :], tile.shape)

    for start in range(0, size, BLOCK):
        stop = start + BLOCK
        first = start // LANES * LANES
        last = size + (stop + LANES - 1) // LANES * LANES
        lanes = range(first, last, LANES)
        groups = BLOCK // ROWS
        tiles = [
            {c: work[start + g * ROWS : start + (g + 1) * ROWS, c : c + LANES] for c in lanes}
            for g in range(groups)
        ]
        for q in range(groups):
            base = start + q * ROWS
            home, at = base // LANES * LANES, base % LANES
            spread = [
                [
                    jnp.broadcast_to(tiles[g][home][:, at + m : at + m + 1], (ROWS, LANES))
                    for m in range(ROWS)
                ]
                if g >= q
                else None
                for g in range(groups)
            ]
            for j in range(0, ROWS, 2):
                first, second = spread[q][j], spread[q][j + 1]
                pivot, side, corner = row_of(first, j), row_of(first, j + 1), row_of(second, j + 1)
                root = lax.rsqrt(pivot)
                lower = side * root
                root2 = lax.rsqrt(pivot * corner - side * side) * (pivot * root)
                weight, weight2 = {}, {}
                for g in range(q, groups):
                    below, below2 = spread[g][j], spread[g][j + 1]
                    if g == q:
                        below = jnp.where(sub > j + 1, below, 0.0)
                        below2 = jnp.where(sub > j + 1, below2, 0.0)
                    weight[g] = below * root
                    weight2[g] = (below2 - weight[g] * lower) * root2

                def tops(tile):
                    top = row_of(tile, j) * root
                    return top, (row_of(tile, j + 1) - lower * top) * root2

                for m in range(j + 2, ROWS):
                    top, top2 = tops(spread[q][m])
                    for g in range(q, groups):
                        spread[g][m] = spread[g][m] - weight[g] * top - weight2[g] * top2
                for c in lanes:
                    top, top2 = tops(tiles[q][c])
                    for g in range(q, groups):
                        tiles[g][c] = tiles[g][c] - weight[g] * top - weight2[g] * top2
                    here = jnp.where(sub == j + 1, top2, tiles[q][c])
                    tiles[q][c] = jnp.where(sub == j, top, here)
        for g in range(groups):
            for c in lanes:
                work[start + g * ROWS : start + (g + 1) * ROWS, c : c + LANES] = tiles[g][c]
        if stop < size:
            low = stop // LANES * LANES
            done = work[start:stop, :]
            update = lax.dot_general(
                done[:, low:size],
                done[:, low:last],
                (((0,), (0,)), ((), ())),
                precision=precise,
                preferred_element_type=jnp.float32,
            )
            work[stop:, low:last] = work[stop:, low:last] - update[stop - low :, :]


def solve_kernel(
    cells,
    summed_ref,
    natural_hbm,
    flat_hbm,
    subspace_ref,
    work,
    natural_ref,
    mixed,
    flat_ref,
    in_sem,
    out_sems,
):
    arrival = pltpu.make_async_copy(natural_hbm, natural_ref, in_sem)
    arrival.start()

    def dot(a, b):
        return jnp.dot(a, b, precision=precise, preferred_element_type=jnp.float32)

    size = work.shape[0]
    parts = size // LANES
    tiles = [
        summed_ref[:, part * ROWS : (part + 1) * ROWS, :].reshape(size, LANES)
        for part in range(parts + 1)
    ]
    packed = jnp.concatenate(tiles[:parts], axis=1) * (1.0 / cells)
    diagonal = jnp.concatenate(tiles[parts:] * parts, axis=1) * (1.0 / cells)
    row = lax.broadcasted_iota(jnp.int32, (size, size), 0)
    column = lax.broadcasted_iota(jnp.int32, (size, size), 1)
    turned = packed.T
    on_diagonal = jnp.where(row == column, packed, 0.0)
    scale = lax.rsqrt(jnp.sum(on_diagonal, axis=0, keepdims=True))
    scale_down = lax.rsqrt(jnp.sum(on_diagonal, axis=1, keepdims=True))
    work[:, :size] = jnp.where(row <= column, packed, turned) * scale_down * scale
    work[:, size:] = jnp.where(row == column, scale, 0.0)
    hamilton = jnp.where(row > column, packed, jnp.where(row == column, diagonal, turned))
    eliminate(work)
    inverse = jnp.where(row >= column, work[:, size:], 0.0)
    subspace = transposed_dot(dot(inverse, hamilton), inverse)
    subspace_ref[...] = subspace
    planes = natural_ref.shape[0]
    half = planes // 2
    arrival.wait()
    for plane in range(0, half, 2):
        both = [
            dot(
                inverse,
                jnp.concatenate([natural_ref[plane + k], natural_ref[half + plane + k]], axis=1),
            )
            for k in range(2)
        ]
        product = dot(subspace, jnp.concatenate([part[:, :LANES] for part in both], axis=1))
        for k, part in enumerate(both):
            mixed[plane + k] = part[:, :LANES]
            mixed[half + plane + k] = part[:, LANES:] - product[:, k * LANES : (k + 1) * LANES]
    parts = 4
    rows = flat_ref.shape[0] // parts
    copies = []
    for part in range(parts):
        natural_rows(flat_ref, mixed, 0, False, part, parts)
        here = pl.ds(part * rows, rows)
        copy = pltpu.make_async_copy(flat_ref.at[here], flat_hbm.at[here], out_sems.at[part])
        copy.start()
        copies.append(copy)
    for copy in copies:
        copy.wait()


def solve(summed, natural, cells):
    planes, size, lanes = natural.shape
    return pl.pallas_call(
        functools.partial(solve_kernel, cells),
        out_shape=(
            jax.ShapeDtypeStruct((planes * size, lanes), jnp.float32),
            jax.ShapeDtypeStruct((size, size), jnp.float32),
        ),
        in_specs=[vmem(), far_away()],
        out_specs=(far_away(), vmem()),
        scratch_shapes=[
            pltpu.VMEM((size, 2 * size), jnp.float32),
            pltpu.VMEM(natural.shape, jnp.float32),
            pltpu.VMEM(natural.shape, jnp.float32),
            pltpu.VMEM((planes * size, lanes), jnp.float32),
            pltpu.SemaphoreType.DMA,
            pltpu.SemaphoreType.DMA((4,)),
        ],
        compiler_params=pltpu.CompilerParams(vmem_limit_bytes=48 * 2**20),
        cost_estimate=pl.CostEstimate(
            flops=20_000_000_000, bytes_accessed=6 * 2**20, transcendentals=256
        ),
        name="solve",
    )(summed, natural)


def assemble_kernel(core_ref, arrived_ref, received_ref, first_ref, second_ref, staged, sems):
    core = core_ref[0]
    blocks = received_ref.shape[0]
    copies = []
    for which, out_ref in enumerate((first_ref, second_ref)):
        for own in range(2):
            slot = 2 * which + own
            if own:
                staged[slot] = arrived_ref[:, pl.ds((core * 2 + which) * ROWS, ROWS), :]
            else:
                staged[slot] = received_ref[:, which * ROWS : (which + 1) * ROWS, :]
            side = core if own else 1 - core
            copy = pltpu.make_async_copy(
                staged.at[slot], out_ref.at[pl.ds(side * blocks, blocks)], sems.at[slot]
            )
            copy.start()
            copies.append(copy)
    for copy in copies:
        copy.wait()


def assemble(core, arrived, received):
    blocks, _, lanes = received.shape
    out = jax.ShapeDtypeStruct((CORES * blocks, ROWS, lanes), jnp.float32)
    return pl.pallas_call(
        assemble_kernel,
        out_shape=(out, out),
        in_specs=[smem(), vmem(), vmem()],
        out_specs=(far_away(), far_away()),
        scratch_shapes=[
            pltpu.VMEM((4, blocks, ROWS, lanes), jnp.float32),
            pltpu.SemaphoreType.DMA((4,)),
        ],
        compiler_params=pltpu.CompilerParams(vmem_limit_bytes=32 * 2**20),
        cost_estimate=pl.CostEstimate(flops=0, bytes_accessed=4 * 2**20, transcendentals=0),
        name="assemble",
    )(core, arrived, received)


def exchange(blocks, groups, axes=AXES):
    return lax.all_to_all(
        blocks, axes, split_axis=0, concat_axis=0, tiled=True, axis_index_groups=groups
    )


class Layout:
    def __init__(self, orb, grp):
        self.x, self.core, self.y = 4, CORES, grp
        self.z = orb // (self.x * self.core)
        self.total = orb * grp

    def orb(self, z, x, core):
        return ((z % self.z) * self.x + x % self.x) * self.core + core % self.core

    def device(self, z, x, core, y):
        return self.orb(z, x, core) * self.y + y

    def places(self):
        return [
            (z, x, core)
            for z in range(self.z)
            for x in range(self.x)
            for core in range(self.core)
        ]

    def chips(self):
        return [
            [
                self.device(z, x, core, y)
                for z in range(self.z)
                for x in range(self.x)
                for y in range(self.y)
            ]
            for core in range(self.core)
        ]

    def planes(self):
        return [
            [
                self.device(z, x, core, y)
                for x in range(self.x)
                for core in range(self.core)
                for y in range(self.y)
            ]
            for z in range(self.z)
        ]

    def columns(self):
        return [
            [self.orb(z, x, core) for z in range(self.z)]
            for x in range(self.x)
            for core in range(self.core)
        ]

    def swap_cores(self, values):
        pairs = [(self.orb(z, x, c), self.orb(z, x, c + 1)) for z, x, c in self.places()]
        return lax.ppermute(values, "orb", pairs)


def reduce_slab(partial, layout):
    me = lax.axis_index("orb")
    core = me % layout.core
    x = me // layout.core % layout.x
    y = lax.axis_index("grp")

    def stage(values, dim, count, index, axis, pairs):
        total = lax.dynamic_index_in_dim(values, index, dim, keepdims=False)
        arrived = [
            lax.ppermute(
                lax.dynamic_index_in_dim(values, (index + k) % count, dim, keepdims=False),
                axis,
                pairs(k),
            )
            for k in range(1, count)
        ]
        for term in arrived:
            total = total + term
        return total

    def along(dx, dc):
        return lambda k: [
            (layout.orb(a, b, c), layout.orb(a, b + dx * k, c + dc * k))
            for a, b, c in layout.places()
        ]

    def lines(k):
        return [(i, (i + k) % layout.y) for i in range(layout.y)]

    values = partial.reshape(layout.z, layout.x, layout.core, layout.y, -1, LANES)
    values = stage(values, 2, layout.core, core, "orb", along(0, 1))
    values = stage(values, 2, layout.y, y, "grp", lines)
    return stage(values, 1, layout.x, x, "orb", along(1, 0))


def sum_everywhere(chunks, slabs, layout):
    count, rows, lanes = chunks.shape
    part = jnp.sum(exchange(chunks, layout.planes()), axis=0, keepdims=True)
    part = jnp.broadcast_to(part, (layout.z, rows, lanes))
    part = exchange(jnp.concatenate([part, slabs], axis=1), layout.columns(), "orb")
    total = jnp.sum(part, axis=0)
    everywhere = jnp.broadcast_to(total[None, :rows], (count, rows, lanes))
    return exchange(everywhere, layout.planes()), total[rows:]


def on_device(layout, orbitals, potential, occupation, region_bounds):
    cell_total = orbitals.shape[1]
    orb, grp = lax.axis_index("orb"), lax.axis_index("grp")
    position = orb * layout.y + grp
    core = orb % layout.core
    place = jnp.stack([position, core]).astype(jnp.int32)
    core = core.reshape(1).astype(jnp.int32)
    keep, give, density_part = apply_hamiltonian(
        place, region_bounds, occupation, orbitals.reshape(G, PAIRS, LANES), potential
    )
    sent = jnp.concatenate([keep, layout.swap_cores(give)], axis=1)
    slabs = reduce_slab(density_part, layout)
    arrived = exchange(sent, layout.chips())
    arrived, slabs = lax.optimization_barrier((arrived, slabs))
    natural, packed = overlap(core, arrived.reshape(-1, LANES))
    summed, density = sum_everywhere(packed, slabs, layout)
    mixed, subspace = solve(summed, natural, cell_total)
    back = exchange(mixed.reshape(-1, 4 * ROWS, LANES), layout.chips())
    other = lax.dynamic_slice_in_dim(back, (1 - core[0]) * 2 * ROWS, 2 * ROWS, 1)
    orthonormal, gradient = assemble(core, back, layout.swap_cores(other))
    return (
        orthonormal.reshape(1, cell_total),
        gradient.reshape(1, cell_total),
        subspace,
        density.reshape(-1, G),
    )


def solution(mesh):
    in_specs = (P(AXES, None), P(), P(), P())
    out_specs = (P(AXES, None), P(AXES, None), P(), P(AXES, None))
    step = functools.partial(on_device, Layout(mesh.shape["orb"], mesh.shape["grp"]))
    return jax.shard_map(
        step, mesh=mesh, in_specs=in_specs, out_specs=out_specs, check_vma=False
    )
```

```python
import functools

import jax
import jax.numpy as jnp
import ml_dtypes
import numpy as np
from jax import lax
from jax.experimental import pallas as pl
from jax.experimental.pallas import tpu as pltpu
from jax.sharding import PartitionSpec as P

G = 64
LANES = 128
PAIRS = G * G // LANES
PAD = 8
SHIFT = 2
STRIP = 16
ROWS = 8
BLOCK = 64
MOST_VMEM = 60 * 2**20

magic_taps = (0.0028, -0.0236, 0.1026, 0.8364, 0.1026, -0.0236, 0.0028)
kinetic_taps = (
    -1.0 / 560.0,
    8.0 / 315.0,
    -0.2,
    1.6,
    -205.0 / 72.0,
    1.6,
    -0.2,
    8.0 / 315.0,
    -1.0 / 560.0,
)
precise = lax.Precision.HIGHEST
AXES = ("orb", "grp")


def banded(extent, taps):
    radius = len(taps) // 2
    matrix = np.zeros((extent, extent))
    for position, weight in enumerate(taps):
        matrix += weight * np.eye(extent, k=position - radius)
    return matrix


def shifted_blocks(along_y, along_z):
    radius = len(along_y) // 2
    blocks = np.zeros((2 * SHIFT + 1, 2, G, 2, G))
    for shift in range(-SHIFT, SHIFT + 1):
        for source in range(2):
            for target in range(2):
                offset = 2 * shift + source - target
                if abs(offset) <= radius:
                    blocks[shift + SHIFT, source, :, target, :] = (
                        along_y[offset + radius] * along_z.T
                    )
    return blocks.reshape((2 * SHIFT + 1) * LANES, LANES)


def split_constant(matrix):
    high = matrix.astype(ml_dtypes.bfloat16)
    low = (matrix - high.astype(np.float64)).astype(ml_dtypes.bfloat16)
    return high, low


def filter_constants():
    magic = shifted_blocks(magic_taps, banded(G, magic_taps))
    kinetic = shifted_blocks(kinetic_taps, np.eye(G)) + shifted_blocks(
        (1.0,), banded(G, kinetic_taps)
    )
    return (
        split_constant(np.concatenate([magic, kinetic], axis=1)),
        split_constant(magic),
    )


def plane_filter(read, first, taps):
    radius = len(taps) // 2
    total = taps[radius] * read(first)
    for step in range(1, radius + 1):
        total += taps[radius + step] * (read(first + step) + read(first - step))
    return total


def hamiltonian_kernel(
    place_ref,
    occupation_ref,
    bounds_hbm,
    orbital_hbm,
    both_high_hbm,
    both_low_hbm,
    potential_hbm,
    magic_high_hbm,
    magic_low_hbm,
    keep_hbm,
    give_hbm,
    density_hbm,
    bounds_ref,
    orbital_ref,
    both_high_ref,
    both_low_ref,
    potential_ref,
    magic_high_ref,
    magic_low_ref,
    source,
    filtered,
    kinetic,
    lines_ref,
    keep_ref,
    give_ref,
    density_ref,
    sems,
    out_sems,
):
    margin = len(kinetic_taps) // 2
    position, core = place_ref[0], place_ref[1]
    copies = [
        pltpu.make_async_copy(far, near, sems.at[k])
        for k, (far, near) in enumerate(
            (
                (bounds_hbm, bounds_ref),
                (orbital_hbm, orbital_ref),
                (both_high_hbm, both_high_ref),
                (both_low_hbm, both_low_ref),
                (potential_hbm, potential_ref),
                (magic_high_hbm, magic_high_ref),
                (magic_low_hbm, magic_low_ref),
            )
        )
    ]
    for copy in copies:
        copy.start()

    zeros = jnp.zeros((margin, PAIRS + 2 * PAD, LANES), jnp.float32)
    source[:margin] = zeros
    source[margin + G :] = zeros
    edge = jnp.zeros((G + 2 * margin, PAD, LANES), jnp.float32)
    source[:, :PAD] = edge
    source[:, PAD + PAIRS :] = edge
    zeros = jnp.zeros((margin, PAIRS, LANES), jnp.float32)
    filtered[:margin] = zeros
    filtered[margin + G :] = zeros

    def product(x, high_ref, low_ref):
        shifted = jnp.concatenate(
            [
                source[pl.ds(margin + x, STRIP), PAD + s : PAD + s + PAIRS].reshape(
                    STRIP * PAIRS, LANES
                )
                for s in range(-SHIFT, SHIFT + 1)
            ],
            axis=1,
        )
        high = shifted.astype(jnp.bfloat16)
        low = (shifted - high.astype(jnp.float32)).astype(jnp.bfloat16)
        dot = functools.partial(jnp.dot, preferred_element_type=jnp.float32)
        return dot(high, high_ref[...]) + (dot(low, high_ref[...]) + dot(high, low_ref[...]))

    def own(x):
        return source[pl.ds(margin + x, STRIP), PAD : PAD + PAIRS]

    def half(x):
        return filtered[pl.ds(margin + x, STRIP)]

    copies[0].wait()
    copies[1].wait()
    planes = lax.broadcasted_iota(jnp.int32, (STRIP * PAIRS, LANES), 0) // PAIRS
    bounds = bounds_ref[...]
    own_place = lax.broadcasted_iota(jnp.int32, bounds.shape, 1) == position
    bounds = jnp.sum(jnp.where(own_place, bounds, 0), axis=1, keepdims=True)
    begin, end = bounds[0:1], bounds[1:2]
    blocks = STRIP * PAIRS // ROWS
    half_planes = G // 2

    def tiled(strip):
        return strip.reshape(blocks, ROWS, LANES)

    for side, out_ref in ((core, keep_ref), (1 - core, give_ref)):
        for strip in range(0, half_planes, STRIP):
            x = half_planes * side + strip
            inside = (planes + x >= begin) & (planes + x < end)
            orbital = orbital_ref[pl.ds(x, STRIP)].reshape(STRIP * PAIRS, LANES)
            masked = jnp.where(inside, orbital, 0.0).reshape(STRIP, PAIRS, LANES)
            source[pl.ds(margin + x, STRIP), PAD : PAD + PAIRS] = masked
            first = strip * PAIRS // ROWS
            out_ref[first : first + blocks, :ROWS, :] = tiled(masked)

    for copy in copies[2:5]:
        copy.wait()

    @pl.loop(0, G, step=STRIP)
    def _(x):
        cells = pl.ds(pl.multiple_of(x * G, STRIP * G), STRIP * G)
        lines_ref[cells, :] = potential_ref[:, cells].T
        both = product(x, both_high_ref, both_low_ref)
        filtered[pl.ds(margin + x, STRIP)] = both[:, :LANES].reshape(STRIP, PAIRS, LANES)
        kinetic[pl.ds(x, STRIP)] = both[:, LANES:].reshape(STRIP, PAIRS, LANES) + plane_filter(
            own, x, kinetic_taps
        )

    scale = occupation_ref[position] * (1.0 / occupation_ref.shape[0])
    lines = STRIP * G // 2

    @pl.loop(0, G, step=STRIP)
    def _(x):
        realspace = plane_filter(half, x, magic_taps)
        density_ref[pl.ds(x, STRIP)] = scale * realspace * realspace
        potential = jnp.concatenate(
            [lines_ref[pl.ds(x * G + odd, lines, stride=2), :] for odd in range(2)], axis=1
        ).reshape(STRIP, PAIRS, LANES)
        source[pl.ds(margin + x, STRIP), PAD : PAD + PAIRS] = realspace * potential

    density_out = pltpu.make_async_copy(density_ref, density_hbm, out_sems.at[4])
    density_out.start()
    copies[5].wait()
    copies[6].wait()

    @pl.loop(0, G, step=STRIP)
    def _(x):
        filtered[pl.ds(margin + x, STRIP)] = product(x, magic_high_ref, magic_low_ref).reshape(
            STRIP, PAIRS, LANES
        )

    done = [density_out]
    for side, out_ref, out_hbm in ((core, keep_ref, keep_hbm), (1 - core, give_ref, give_hbm)):
        for strip in range(0, half_planes, STRIP):
            x = half_planes * side + strip
            images = plane_filter(half, x, magic_taps) - 0.5 * kinetic[pl.ds(x, STRIP)]
            first = strip * PAIRS // ROWS
            out_ref[first : first + blocks, ROWS:, :] = tiled(images)
            here = pl.ds(first, blocks)
            copy = pltpu.make_async_copy(
                out_ref.at[here], out_hbm.at[here], out_sems.at[len(done) - 1]
            )
            copy.start()
            done.append(copy)
    for copy in done:
        copy.wait()


def vmem():
    return pl.BlockSpec(memory_space=pltpu.VMEM)


def smem():
    return pl.BlockSpec(memory_space=pltpu.SMEM)


def far_away():
    return pl.BlockSpec(memory_space=pltpu.HBM)


def apply_hamiltonian(place, region_bounds, occupation, orbital, potential):
    (both_high, both_low), (magic_high, magic_low) = filter_constants()
    margin = len(kinetic_taps) // 2
    side = jax.ShapeDtypeStruct((G * PAIRS // ROWS // 2, 2 * ROWS, LANES), jnp.float32)
    grid = jax.ShapeDtypeStruct((G, PAIRS, LANES), jnp.float32)
    far = (region_bounds.T, orbital, both_high, both_low, potential.T, magic_high, magic_low)
    far = [jnp.asarray(values) for values in far]
    return pl.pallas_call(
        hamiltonian_kernel,
        out_shape=(side, side, grid),
        in_specs=[smem()] * 2 + [far_away()] * len(far),
        out_specs=(far_away(),) * 3,
        scratch_shapes=[pltpu.VMEM(values.shape, values.dtype) for values in far]
        + [
            pltpu.VMEM((G + 2 * margin, PAIRS + 2 * PAD, LANES), jnp.float32),
            pltpu.VMEM((G + 2 * margin, PAIRS, LANES), jnp.float32),
            pltpu.VMEM((G, PAIRS, LANES), jnp.float32),
            pltpu.VMEM((G * G, G), jnp.float32),
            pltpu.VMEM(side.shape, side.dtype),
            pltpu.VMEM(side.shape, side.dtype),
            pltpu.VMEM(grid.shape, grid.dtype),
            pltpu.SemaphoreType.DMA((len(far),)),
            pltpu.SemaphoreType.DMA((5,)),
        ],
        compiler_params=pltpu.CompilerParams(vmem_limit_bytes=MOST_VMEM),
        cost_estimate=pl.CostEstimate(
            flops=6 * 2048 * 640 * 384, bytes_accessed=5 * 2**20, transcendentals=0
        ),
        name="hamiltonian",
    )(place, occupation, *far)


def transposed_dot(a, b):
    return lax.dot_general(
        a, b, (((1,), (1,)), ((), ())), precision=precise, preferred_element_type=jnp.float32
    )


CORES = 2
PARTS = 4
LINES = 4


def natural_rows(flat_ref, natural_ref, core, gather, part=0, parts=1):
    planes, orbitals, _ = natural_ref.shape
    groups = orbitals // (CORES * LINES * parts)
    stride = CORES * LINES * planes
    for slot in range(CORES):
        for line in range(LINES):
            for plane in range(planes):
                inner = (line * CORES + slot) * planes + plane + part * groups * stride
                inner = pl.ds(inner, groups, stride=stride)
                outer = (slot ^ core) * LINES + line + part * groups * CORES * LINES
                outer = pl.ds(outer, groups, stride=CORES * LINES)
                if gather:
                    natural_ref[plane, outer, :] = flat_ref[inner, :]
                else:
                    flat_ref[inner, :] = natural_ref[plane, outer, :]


def overlap_kernel(
    core_ref, flat_hbm, natural_hbm, packed_ref, flat_ref, natural_ref, in_sems, out_sem
):
    rows = flat_ref.shape[0] // PARTS
    arrivals = []
    for part in range(PARTS):
        here = pl.ds(part * rows, rows)
        copy = pltpu.make_async_copy(flat_hbm.at[here], flat_ref.at[here], in_sems.at[part])
        copy.start()
        arrivals.append(copy)
    for part in range(PARTS):
        arrivals[part].wait()
        for core in range(CORES):

            @pl.when(core_ref[0] == core)
            def _(core=core, part=part):
                natural_rows(flat_ref, natural_ref, core, True, part, PARTS)

    copy = pltpu.make_async_copy(natural_ref, natural_hbm, out_sem)
    copy.start()
    planes, size, _ = natural_ref.shape
    half = planes // 2
    total = None
    for plane in range(0, half, 2):
        psi = jnp.concatenate([natural_ref[plane], natural_ref[plane + 1]], axis=1)
        images = jnp.concatenate(
            [natural_ref[half + plane], natural_ref[half + plane + 1]], axis=1
        )
        term = transposed_dot(psi, jnp.concatenate([psi, images], axis=0))
        total = term if total is None else total + term
    row = lax.broadcasted_iota(jnp.int32, (size, size), 0)
    column = lax.broadcasted_iota(jnp.int32, (size, size), 1)
    hamilton = total[:, size:]
    packed = jnp.where(row <= column, total[:, :size], hamilton)
    diagonal = jnp.sum(jnp.where(row == column, hamilton, 0.0), axis=1, keepdims=True)
    chunks = size // ROWS
    for part in range(size // LANES):
        packed_ref[:, part * ROWS : (part + 1) * ROWS, :] = packed[
            :, part * LANES : (part + 1) * LANES
        ].reshape(chunks, ROWS, LANES)
    packed_ref[:, size // LANES * ROWS :, :] = jnp.broadcast_to(
        diagonal, (size, LANES)
    ).reshape(chunks, ROWS, LANES)
    copy.wait()


def overlap(core, arrived):
    rows, lanes = arrived.shape
    planes = 2 * ROWS
    size = rows // planes
    return pl.pallas_call(
        overlap_kernel,
        out_shape=(
            jax.ShapeDtypeStruct((planes, size, lanes), jnp.float32),
            jax.ShapeDtypeStruct((size // ROWS, (size // LANES + 1) * ROWS, LANES), jnp.float32),
        ),
        in_specs=[smem(), far_away()],
        out_specs=(far_away(), vmem()),
        scratch_shapes=[
            pltpu.VMEM((rows, lanes), jnp.float32),
            pltpu.VMEM((planes, size, lanes), jnp.float32),
            pltpu.SemaphoreType.DMA((PARTS,)),
            pltpu.SemaphoreType.DMA,
        ],
        compiler_params=pltpu.CompilerParams(vmem_limit_bytes=MOST_VMEM),
        cost_estimate=pl.CostEstimate(
            flops=24 * 256 * 256 * 1024, bytes_accessed=4 * 2**20, transcendentals=0
        ),
        name="overlap",
    )(core, arrived)


def eliminate(work):
    size = work.shape[0]
    sub = lax.broadcasted_iota(jnp.int32, (ROWS, LANES), 0)

    def row_of(tile, j):
        return jnp.broadcast_to(tile[j : j + 1, :], tile.shape)

    for start in range(0, size, BLOCK):
        stop = start + BLOCK
        first = start // LANES * LANES
        last = size + (stop + LANES - 1) // LANES * LANES
        lanes = range(first, last, LANES)
        groups = BLOCK // ROWS
        tiles = [
            {c: work[start + g * ROWS : start + (g + 1) * ROWS, c : c + LANES] for c in lanes}
            for g in range(groups)
        ]
        for q in range(groups):
            base = start + q * ROWS
            home, at = base // LANES * LANES, base % LANES
            spread = [
                [
                    jnp.broadcast_to(tiles[g][home][:, at + m : at + m + 1], (ROWS, LANES))
                    for m in range(ROWS)
                ]
                if g >= q
                else None
                for g in range(groups)
            ]
            for j in range(0, ROWS, 2):
                first, second = spread[q][j], spread[q][j + 1]
                pivot, side, corner = row_of(first, j), row_of(first, j + 1), row_of(second, j + 1)
                root = lax.rsqrt(pivot)
                lower = side * root
                root2 = lax.rsqrt(pivot * corner - side * side) * (pivot * root)
                weight, weight2 = {}, {}
                for g in range(q, groups):
                    below, below2 = spread[g][j], spread[g][j + 1]
                    if g == q:
                        below = jnp.where(sub > j + 1, below, 0.0)
                        below2 = jnp.where(sub > j + 1, below2, 0.0)
                    weight[g] = below * root
                    weight2[g] = (below2 - weight[g] * lower) * root2

                def tops(tile):
                    top = row_of(tile, j) * root
                    return top, (row_of(tile, j + 1) - lower * top) * root2

                for m in range(j + 2, ROWS):
                    top, top2 = tops(spread[q][m])
                    for g in range(q, groups):
                        spread[g][m] = spread[g][m] - weight[g] * top - weight2[g] * top2
                for c in lanes:
                    top, top2 = tops(tiles[q][c])
                    for g in range(q, groups):
                        tiles[g][c] = tiles[g][c] - weight[g] * top - weight2[g] * top2
                    here = jnp.where(sub == j + 1, top2, tiles[q][c])
                    tiles[q][c] = jnp.where(sub == j, top, here)
        for g in range(groups):
            for c in lanes:
                work[start + g * ROWS : start + (g + 1) * ROWS, c : c + LANES] = tiles[g][c]
        if stop < size:
            low = stop // LANES * LANES
            done = work[start:stop, :]
            update = lax.dot_general(
                done[:, low:size],
                done[:, low:last],
                (((0,), (0,)), ((), ())),
                precision=precise,
                preferred_element_type=jnp.float32,
            )
            work[stop:, low:last] = work[stop:, low:last] - update[stop - low :, :]


def solve_kernel(
    cells,
    summed_ref,
    natural_hbm,
    flat_hbm,
    subspace_ref,
    work,
    natural_ref,
    mixed,
    flat_ref,
    in_sem,
    out_sems,
):
    arrival = pltpu.make_async_copy(natural_hbm, natural_ref, in_sem)
    arrival.start()

    def dot(a, b):
        return jnp.dot(a, b, precision=precise, preferred_element_type=jnp.float32)

    size = work.shape[0]
    parts = size // LANES
    tiles = [
        summed_ref[:, part * ROWS : (part + 1) * ROWS, :].reshape(size, LANES)
        for part in range(parts + 1)
    ]
    packed = jnp.concatenate(tiles[:parts], axis=1) * (1.0 / cells)
    diagonal = jnp.concatenate(tiles[parts:] * parts, axis=1) * (1.0 / cells)
    row = lax.broadcasted_iota(jnp.int32, (size, size), 0)
    column = lax.broadcasted_iota(jnp.int32, (size, size), 1)
    turned = packed.T
    on_diagonal = jnp.where(row == column, packed, 0.0)
    scale = lax.rsqrt(jnp.sum(on_diagonal, axis=0, keepdims=True))
    scale_down = lax.rsqrt(jnp.sum(on_diagonal, axis=1, keepdims=True))
    work[:, :size] = jnp.where(row <= column, packed, turned) * scale_down * scale
    work[:, size:] = jnp.where(row == column, scale, 0.0)
    hamilton = jnp.where(row > column, packed, jnp.where(row == column, diagonal, turned))
    eliminate(work)
    inverse = jnp.where(row >= column, work[:, size:], 0.0)
    subspace = transposed_dot(dot(inverse, hamilton), inverse)
    subspace_ref[...] = subspace
    planes = natural_ref.shape[0]
    half = planes // 2
    arrival.wait()
    for plane in range(0, half, 2):
        both = [
            dot(
                inverse,
                jnp.concatenate([natural_ref[plane + k], natural_ref[half + plane + k]], axis=1),
            )
            for k in range(2)
        ]
        product = dot(subspace, jnp.concatenate([part[:, :LANES] for part in both], axis=1))
        for k, part in enumerate(both):
            mixed[plane + k] = part[:, :LANES]
            mixed[half + plane + k] = part[:, LANES:] - product[:, k * LANES : (k + 1) * LANES]
    rows = flat_ref.shape[0] // PARTS
    copies = []
    for part in range(PARTS):
        natural_rows(flat_ref, mixed, 0, False, part, PARTS)
        here = pl.ds(part * rows, rows)
        copy = pltpu.make_async_copy(flat_ref.at[here], flat_hbm.at[here], out_sems.at[part])
        copy.start()
        copies.append(copy)
    for copy in copies:
        copy.wait()


def solve(summed, natural, cells):
    planes, size, lanes = natural.shape
    return pl.pallas_call(
        functools.partial(solve_kernel, cells),
        out_shape=(
            jax.ShapeDtypeStruct((planes * size, lanes), jnp.float32),
            jax.ShapeDtypeStruct((size, size), jnp.float32),
        ),
        in_specs=[vmem(), far_away()],
        out_specs=(far_away(), vmem()),
        scratch_shapes=[
            pltpu.VMEM((size, 2 * size), jnp.float32),
            pltpu.VMEM(natural.shape, jnp.float32),
            pltpu.VMEM(natural.shape, jnp.float32),
            pltpu.VMEM((planes * size, lanes), jnp.float32),
            pltpu.SemaphoreType.DMA,
            pltpu.SemaphoreType.DMA((PARTS,)),
        ],
        compiler_params=pltpu.CompilerParams(vmem_limit_bytes=MOST_VMEM),
        cost_estimate=pl.CostEstimate(
            flops=20_000_000_000, bytes_accessed=6 * 2**20, transcendentals=256
        ),
        name="solve",
    )(summed, natural)


def assemble_kernel(core_ref, arrived_ref, received_ref, first_ref, second_ref, staged, sems):
    core = core_ref[0]
    blocks = received_ref.shape[0]
    copies = []
    for which, out_ref in enumerate((first_ref, second_ref)):
        for own in range(2):
            slot = 2 * which + own
            if own:
                staged[slot] = arrived_ref[:, pl.ds((core * 2 + which) * ROWS, ROWS), :]
            else:
                staged[slot] = received_ref[:, which * ROWS : (which + 1) * ROWS, :]
            side = core if own else 1 - core
            copy = pltpu.make_async_copy(
                staged.at[slot], out_ref.at[pl.ds(side * blocks, blocks)], sems.at[slot]
            )
            copy.start()
            copies.append(copy)
    for copy in copies:
        copy.wait()


def assemble(core, arrived, received):
    blocks, _, lanes = received.shape
    out = jax.ShapeDtypeStruct((CORES * blocks, ROWS, lanes), jnp.float32)
    return pl.pallas_call(
        assemble_kernel,
        out_shape=(out, out),
        in_specs=[smem(), vmem(), vmem()],
        out_specs=(far_away(), far_away()),
        scratch_shapes=[
            pltpu.VMEM((4, blocks, ROWS, lanes), jnp.float32),
            pltpu.SemaphoreType.DMA((4,)),
        ],
        compiler_params=pltpu.CompilerParams(vmem_limit_bytes=32 * 2**20),
        cost_estimate=pl.CostEstimate(flops=0, bytes_accessed=4 * 2**20, transcendentals=0),
        name="assemble",
    )(core, arrived, received)


def exchange(blocks, groups, axes=AXES):
    return lax.all_to_all(
        blocks, axes, split_axis=0, concat_axis=0, tiled=True, axis_index_groups=groups
    )


class Layout:
    def __init__(self, orb, grp):
        self.x, self.core, self.y = 4, CORES, grp
        self.z = orb // (self.x * self.core)
        self.total = orb * grp

    def orb(self, z, x, core):
        return ((z % self.z) * self.x + x % self.x) * self.core + core % self.core

    def device(self, z, x, core, y):
        return self.orb(z, x, core) * self.y + y

    def places(self):
        return [
            (z, x, core)
            for z in range(self.z)
            for x in range(self.x)
            for core in range(self.core)
        ]

    def chips(self):
        return [
            [
                self.device(z, x, core, y)
                for z in range(self.z)
                for x in range(self.x)
                for y in range(self.y)
            ]
            for core in range(self.core)
        ]

    def planes(self):
        return [
            [
                self.device(z, x, core, y)
                for x in range(self.x)
                for core in range(self.core)
                for y in range(self.y)
            ]
            for z in range(self.z)
        ]

    def columns(self):
        return [
            [self.orb(z, x, core) for z in range(self.z)]
            for x in range(self.x)
            for core in range(self.core)
        ]

    def swap_cores(self, values):
        pairs = [(self.orb(z, x, c), self.orb(z, x, c + 1)) for z, x, c in self.places()]
        return lax.ppermute(values, "orb", pairs)


def reduce_slab(partial, layout):
    me = lax.axis_index("orb")
    core = me % layout.core
    x = me // layout.core % layout.x
    y = lax.axis_index("grp")

    def stage(values, dim, count, index, axis, pairs):
        total = lax.dynamic_index_in_dim(values, index, dim, keepdims=False)
        arrived = [
            lax.ppermute(
                lax.dynamic_index_in_dim(values, (index + k) % count, dim, keepdims=False),
                axis,
                pairs(k),
            )
            for k in range(1, count)
        ]
        for term in arrived:
            total = total + term
        return total

    def along(dx, dc):
        return lambda k: [
            (layout.orb(a, b, c), layout.orb(a, b + dx * k, c + dc * k))
            for a, b, c in layout.places()
        ]

    def lines(k):
        return [(i, (i + k) % layout.y) for i in range(layout.y)]

    values = partial.reshape(layout.z, layout.x, layout.core, layout.y, -1, LANES)
    values = stage(values, 2, layout.core, core, "orb", along(0, 1))
    values = stage(values, 2, layout.y, y, "grp", lines)
    return stage(values, 1, layout.x, x, "orb", along(1, 0))


def sum_everywhere(chunks, slabs, layout):
    count, rows, lanes = chunks.shape
    part = jnp.sum(exchange(chunks, layout.planes()), axis=0, keepdims=True)
    part = jnp.broadcast_to(part, (layout.z, rows, lanes))
    part = exchange(jnp.concatenate([part, slabs], axis=1), layout.columns(), "orb")
    total = jnp.sum(part, axis=0)
    everywhere = jnp.broadcast_to(total[None, :rows], (count, rows, lanes))
    return exchange(everywhere, layout.planes()), total[rows:]


def on_device(layout, orbitals, potential, occupation, region_bounds):
    cell_total = orbitals.shape[1]
    orb, grp = lax.axis_index("orb"), lax.axis_index("grp")
    position = orb * layout.y + grp
    core = orb % layout.core
    place = jnp.stack([position, core]).astype(jnp.int32)
    core = core.reshape(1).astype(jnp.int32)
    keep, give, density_part = apply_hamiltonian(
        place, region_bounds, occupation, orbitals.reshape(G, PAIRS, LANES), potential
    )
    sent = jnp.concatenate([keep, layout.swap_cores(give)], axis=1)
    slabs = reduce_slab(density_part, layout)
    arrived = exchange(sent, layout.chips())
    arrived, slabs = lax.optimization_barrier((arrived, slabs))
    natural, packed = overlap(core, arrived.reshape(-1, LANES))
    summed, density = sum_everywhere(packed, slabs, layout)
    mixed, subspace = solve(summed, natural, cell_total)
    back = exchange(mixed.reshape(-1, 4 * ROWS, LANES), layout.chips())
    back, density = lax.optimization_barrier((back, density.reshape(-1, G)))
    other = lax.dynamic_slice_in_dim(back, (1 - core[0]) * 2 * ROWS, 2 * ROWS, 1)
    orthonormal, gradient = assemble(core, back, layout.swap_cores(other))
    return (
        orthonormal.reshape(1, cell_total),
        gradient.reshape(1, cell_total),
        subspace,
        density,
    )


def solution(mesh):
    in_specs = (P(AXES, None), P(), P(), P())
    out_specs = (P(AXES, None), P(AXES, None), P(), P(AXES, None))
    step = functools.partial(on_device, Layout(mesh.shape["orb"], mesh.shape["grp"]))
    return jax.shard_map(
        step, mesh=mesh, in_specs=in_specs, out_specs=out_specs, check_vma=False
    )
```

```python
import functools

import jax
import jax.numpy as jnp
import ml_dtypes
import numpy as np
from jax import lax
from jax.experimental import pallas as pl
from jax.experimental.pallas import tpu as pltpu
from jax.sharding import PartitionSpec as P

G = 64
LANES = 128
PAIRS = G * G // LANES
PAD = 8
SHIFT = 2
STRIP = 16
ROWS = 8
BLOCK = 64

magic_taps = (0.0028, -0.0236, 0.1026, 0.8364, 0.1026, -0.0236, 0.0028)
kinetic_taps = (
    -1.0 / 560.0,
    8.0 / 315.0,
    -0.2,
    1.6,
    -205.0 / 72.0,
    1.6,
    -0.2,
    8.0 / 315.0,
    -1.0 / 560.0,
)
precise = lax.Precision.HIGHEST
AXES = ("orb", "grp")


def banded(extent, taps):
    radius = len(taps) // 2
    matrix = np.zeros((extent, extent))
    for position, weight in enumerate(taps):
        matrix += weight * np.eye(extent, k=position - radius)
    return matrix


def shifted_blocks(along_y, along_z):
    radius = len(along_y) // 2
    blocks = np.zeros((2 * SHIFT + 1, 2, G, 2, G))
    for shift in range(-SHIFT, SHIFT + 1):
        for source in range(2):
            for target in range(2):
                offset = 2 * shift + source - target
                if abs(offset) <= radius:
                    blocks[shift + SHIFT, source, :, target, :] = (
                        along_y[offset + radius] * along_z.T
                    )
    return blocks.reshape((2 * SHIFT + 1) * LANES, LANES)


def split_constant(matrix):
    high = matrix.astype(ml_dtypes.bfloat16)
    low = (matrix - high.astype(np.float64)).astype(ml_dtypes.bfloat16)
    return high, low


def filter_constants():
    magic = shifted_blocks(magic_taps, banded(G, magic_taps))
    kinetic = shifted_blocks(kinetic_taps, np.eye(G)) + shifted_blocks(
        (1.0,), banded(G, kinetic_taps)
    )
    return np.concatenate(split_constant(np.concatenate([magic, kinetic], axis=1)), axis=1)


def plane_filter(read, first, taps):
    radius = len(taps) // 2
    total = taps[radius] * read(first)
    for step in range(1, radius + 1):
        total += taps[radius + step] * (read(first + step) + read(first - step))
    return total


def hamiltonian_kernel(
    place_ref,
    occupation_ref,
    bounds_hbm,
    orbital_hbm,
    filters_hbm,
    potential_hbm,
    keep_ref,
    give_ref,
    density_ref,
    bounds_ref,
    orbital_ref,
    filters_ref,
    potential_ref,
    source,
    filtered,
    kinetic,
    lines_ref,
    sems,
):
    margin = len(kinetic_taps) // 2
    position, core = place_ref[0], place_ref[1]
    copies = [
        pltpu.make_async_copy(far, near, sems.at[k])
        for k, (far, near) in enumerate(
            (
                (bounds_hbm, bounds_ref),
                (orbital_hbm, orbital_ref),
                (filters_hbm, filters_ref),
                (potential_hbm, potential_ref),
            )
        )
    ]
    for copy in copies:
        copy.start()

    zeros = jnp.zeros((margin, PAIRS + 2 * PAD, LANES), jnp.float32)
    source[:margin] = zeros
    source[margin + G :] = zeros
    edge = jnp.zeros((G + 2 * margin, PAD, LANES), jnp.float32)
    source[:, :PAD] = edge
    source[:, PAD + PAIRS :] = edge
    zeros = jnp.zeros((margin, PAIRS, LANES), jnp.float32)
    filtered[:margin] = zeros
    filtered[margin + G :] = zeros

    def product(x, width):
        shifted = jnp.concatenate(
            [
                source[pl.ds(margin + x, STRIP), PAD + s : PAD + s + PAIRS].reshape(
                    STRIP * PAIRS, LANES
                )
                for s in range(-SHIFT, SHIFT + 1)
            ],
            axis=1,
        )
        high = shifted.astype(jnp.bfloat16)
        low = (shifted - high.astype(jnp.float32)).astype(jnp.bfloat16)
        dot = functools.partial(jnp.dot, preferred_element_type=jnp.float32)
        high_filter = filters_ref[:, :width]
        low_filter = filters_ref[:, 2 * LANES : 2 * LANES + width]
        return dot(high, high_filter) + (dot(low, high_filter) + dot(high, low_filter))

    def own(x):
        return source[pl.ds(margin + x, STRIP), PAD : PAD + PAIRS]

    def half(x):
        return filtered[pl.ds(margin + x, STRIP)]

    copies[0].wait()
    copies[1].wait()
    planes = lax.broadcasted_iota(jnp.int32, (STRIP * PAIRS, LANES), 0) // PAIRS
    bounds = bounds_ref[...]
    own_place = lax.broadcasted_iota(jnp.int32, bounds.shape, 1) == position
    bounds = jnp.sum(jnp.where(own_place, bounds, 0), axis=1, keepdims=True)
    begin, end = bounds[0:1], bounds[1:2]
    blocks = STRIP * PAIRS // ROWS
    half_planes = G // 2

    def tiled(strip):
        return strip.reshape(blocks, ROWS, LANES)

    for side, out_ref in ((core, keep_ref), (1 - core, give_ref)):
        for strip in range(0, half_planes, STRIP):
            x = half_planes * side + strip
            inside = (planes + x >= begin) & (planes + x < end)
            orbital = orbital_ref[pl.ds(x, STRIP)].reshape(STRIP * PAIRS, LANES)
            masked = jnp.where(inside, orbital, 0.0).reshape(STRIP, PAIRS, LANES)
            source[pl.ds(margin + x, STRIP), PAD : PAD + PAIRS] = masked
            first = strip * PAIRS // ROWS
            out_ref[first : first + blocks, :ROWS, :] = tiled(masked)

    copies[2].wait()
    copies[3].wait()

    @pl.loop(0, G, step=STRIP)
    def _(x):
        cells = pl.ds(pl.multiple_of(x * G, STRIP * G), STRIP * G)
        lines_ref[cells, :] = potential_ref[:, cells].T
        both = product(x, 2 * LANES)
        filtered[pl.ds(margin + x, STRIP)] = both[:, :LANES].reshape(STRIP, PAIRS, LANES)
        kinetic[pl.ds(x, STRIP)] = both[:, LANES:].reshape(STRIP, PAIRS, LANES) + plane_filter(
            own, x, kinetic_taps
        )

    scale = occupation_ref[position] * (1.0 / occupation_ref.shape[0])
    lines = STRIP * G // 2

    @pl.loop(0, G, step=STRIP)
    def _(x):
        realspace = plane_filter(half, x, magic_taps)
        density_ref[pl.ds(x, STRIP)] = scale * realspace * realspace
        potential = jnp.concatenate(
            [lines_ref[pl.ds(x * G + odd, lines, stride=2), :] for odd in range(2)], axis=1
        ).reshape(STRIP, PAIRS, LANES)
        source[pl.ds(margin + x, STRIP), PAD : PAD + PAIRS] = realspace * potential

    @pl.loop(0, G, step=STRIP)
    def _(x):
        filtered[pl.ds(margin + x, STRIP)] = product(x, LANES).reshape(
            STRIP, PAIRS, LANES
        )

    for side, out_ref in ((core, keep_ref), (1 - core, give_ref)):
        for strip in range(0, half_planes, STRIP):
            x = half_planes * side + strip
            images = plane_filter(half, x, magic_taps) - 0.5 * kinetic[pl.ds(x, STRIP)]
            first = strip * PAIRS // ROWS
            out_ref[first : first + blocks, ROWS:, :] = tiled(images)


def vmem():
    return pl.BlockSpec(memory_space=pltpu.VMEM)


def smem():
    return pl.BlockSpec(memory_space=pltpu.SMEM)


def far_away():
    return pl.BlockSpec(memory_space=pltpu.HBM)


def apply_hamiltonian(place, region_bounds, occupation, orbital, potential):
    margin = len(kinetic_taps) // 2
    side = jax.ShapeDtypeStruct((G * PAIRS // ROWS // 2, 2 * ROWS, LANES), jnp.float32)
    grid = jax.ShapeDtypeStruct((G, PAIRS, LANES), jnp.float32)
    far = (region_bounds.T, orbital, filter_constants(), potential.T)
    far = [jnp.asarray(values) for values in far]
    return pl.pallas_call(
        hamiltonian_kernel,
        out_shape=(side, side, grid),
        in_specs=[smem()] * 2 + [far_away()] * len(far),
        out_specs=(vmem(),) * 3,
        scratch_shapes=[pltpu.VMEM(values.shape, values.dtype) for values in far]
        + [
            pltpu.VMEM((G + 2 * margin, PAIRS + 2 * PAD, LANES), jnp.float32),
            pltpu.VMEM((G + 2 * margin, PAIRS, LANES), jnp.float32),
            pltpu.VMEM((G, PAIRS, LANES), jnp.float32),
            pltpu.VMEM((G * G, G), jnp.float32),
            pltpu.SemaphoreType.DMA((len(far),)),
        ],
        compiler_params=pltpu.CompilerParams(vmem_limit_bytes=50 * 2**20),
        cost_estimate=pl.CostEstimate(
            flops=6 * 2048 * 640 * 384, bytes_accessed=5 * 2**20, transcendentals=0
        ),
        name="hamiltonian",
    )(place, occupation, *far)


def transposed_dot(a, b):
    return lax.dot_general(
        a, b, (((1,), (1,)), ((), ())), precision=precise, preferred_element_type=jnp.float32
    )


CORES = 2
LINES = 4


def natural_rows(flat_ref, natural_ref, core, gather):
    planes, orbitals, _ = natural_ref.shape
    groups = orbitals // (CORES * LINES)
    stride = CORES * LINES * planes
    for slot in range(CORES):
        for line in range(LINES):
            for plane in range(planes):
                inner = pl.ds((line * CORES + slot) * planes + plane, groups, stride=stride)
                outer = pl.ds((slot ^ core) * LINES + line, groups, stride=CORES * LINES)
                if gather:
                    natural_ref[plane, outer, :] = flat_ref[inner, :]
                else:
                    flat_ref[inner, :] = natural_ref[plane, outer, :]


def overlap_kernel(core_ref, flat_ref, natural_ref, packed_ref):
    for core in range(CORES):

        @pl.when(core_ref[0] == core)
        def _(core=core):
            natural_rows(flat_ref, natural_ref, core, True)

    planes, size, _ = natural_ref.shape
    half = planes // 2
    total = None
    for plane in range(0, half, 2):
        psi = jnp.concatenate([natural_ref[plane], natural_ref[plane + 1]], axis=1)
        images = jnp.concatenate(
            [natural_ref[half + plane], natural_ref[half + plane + 1]], axis=1
        )
        term = transposed_dot(psi, jnp.concatenate([psi, images], axis=0))
        total = term if total is None else total + term
    row = lax.broadcasted_iota(jnp.int32, (size, size), 0)
    column = lax.broadcasted_iota(jnp.int32, (size, size), 1)
    hamilton = total[:, size:]
    packed = jnp.where(row <= column, total[:, :size], hamilton)
    diagonal = jnp.sum(jnp.where(row == column, hamilton, 0.0), axis=1, keepdims=True)
    chunks = size // ROWS
    for part in range(size // LANES):
        packed_ref[:, part * ROWS : (part + 1) * ROWS, :] = packed[
            :, part * LANES : (part + 1) * LANES
        ].reshape(chunks, ROWS, LANES)
    packed_ref[:, size // LANES * ROWS :, :] = jnp.broadcast_to(
        diagonal, (size, LANES)
    ).reshape(chunks, ROWS, LANES)


def overlap(core, arrived):
    rows, lanes = arrived.shape
    planes = 2 * ROWS
    size = rows // planes
    return pl.pallas_call(
        overlap_kernel,
        out_shape=(
            jax.ShapeDtypeStruct((planes, size, lanes), jnp.float32),
            jax.ShapeDtypeStruct((size // ROWS, (size // LANES + 1) * ROWS, LANES), jnp.float32),
        ),
        in_specs=[smem(), vmem()],
        out_specs=(vmem(), vmem()),
        compiler_params=pltpu.CompilerParams(vmem_limit_bytes=40 * 2**20),
        cost_estimate=pl.CostEstimate(
            flops=24 * 256 * 256 * 1024, bytes_accessed=4 * 2**20, transcendentals=0
        ),
        name="overlap",
    )(core, arrived)


def eliminate(work):
    size = work.shape[0]
    sub = lax.broadcasted_iota(jnp.int32, (ROWS, LANES), 0)

    def row_of(tile, j):
        return jnp.broadcast_to(tile[j : j + 1, :], tile.shape)

    for start in range(0, size, BLOCK):
        stop = start + BLOCK
        first = start // LANES * LANES
        last = size + (stop + LANES - 1) // LANES * LANES
        lanes = range(first, last, LANES)
        groups = BLOCK // ROWS
        tiles = [
            {c: work[start + g * ROWS : start + (g + 1) * ROWS, c : c + LANES] for c in lanes}
            for g in range(groups)
        ]
        for q in range(groups):
            base = start + q * ROWS
            home, at = base // LANES * LANES, base % LANES
            spread = [
                [
                    jnp.broadcast_to(tiles[g][home][:, at + m : at + m + 1], (ROWS, LANES))
                    for m in range(ROWS)
                ]
                if g >= q
                else None
                for g in range(groups)
            ]
            for j in range(0, ROWS, 2):
                first, second = spread[q][j], spread[q][j + 1]
                pivot, side, corner = row_of(first, j), row_of(first, j + 1), row_of(second, j + 1)
                root = lax.rsqrt(pivot)
                lower = side * root
                root2 = lax.rsqrt(pivot * corner - side * side) * (pivot * root)
                weight, weight2 = {}, {}
                for g in range(q, groups):
                    below, below2 = spread[g][j], spread[g][j + 1]
                    if g == q:
                        below = jnp.where(sub > j + 1, below, 0.0)
                        below2 = jnp.where(sub > j + 1, below2, 0.0)
                    weight[g] = below * root
                    weight2[g] = (below2 - weight[g] * lower) * root2

                def tops(tile):
                    top = row_of(tile, j) * root
                    return top, (row_of(tile, j + 1) - lower * top) * root2

                for m in range(j + 2, ROWS):
                    top, top2 = tops(spread[q][m])
                    for g in range(q, groups):
                        spread[g][m] = spread[g][m] - weight[g] * top - weight2[g] * top2
                for c in lanes:
                    top, top2 = tops(tiles[q][c])
                    for g in range(q, groups):
                        tiles[g][c] = tiles[g][c] - weight[g] * top - weight2[g] * top2
                    here = jnp.where(sub == j + 1, top2, tiles[q][c])
                    tiles[q][c] = jnp.where(sub == j, top, here)
        for g in range(groups):
            for c in lanes:
                work[start + g * ROWS : start + (g + 1) * ROWS, c : c + LANES] = tiles[g][c]
        if stop < size:
            low = stop // LANES * LANES
            done = work[start:stop, :]
            update = lax.dot_general(
                done[:, low:size],
                done[:, low:last],
                (((0,), (0,)), ((), ())),
                precision=precise,
                preferred_element_type=jnp.float32,
            )
            work[stop:, low:last] = work[stop:, low:last] - update[stop - low :, :]


def solve_kernel(
    cells,
    summed_ref,
    natural_ref,
    flat_ref,
    subspace_ref,
    work,
    mixed,
):
    def dot(a, b):
        return jnp.dot(a, b, precision=precise, preferred_element_type=jnp.float32)

    size = work.shape[0]
    parts = size // LANES
    tiles = [
        summed_ref[:, part * ROWS : (part + 1) * ROWS, :].reshape(size, LANES)
        for part in range(parts + 1)
    ]
    packed = jnp.concatenate(tiles[:parts], axis=1) * (1.0 / cells)
    diagonal = jnp.concatenate(tiles[parts:] * parts, axis=1) * (1.0 / cells)
    row = lax.broadcasted_iota(jnp.int32, (size, size), 0)
    column = lax.broadcasted_iota(jnp.int32, (size, size), 1)
    turned = packed.T
    on_diagonal = jnp.where(row == column, packed, 0.0)
    scale = lax.rsqrt(jnp.sum(on_diagonal, axis=0, keepdims=True))
    scale_down = lax.rsqrt(jnp.sum(on_diagonal, axis=1, keepdims=True))
    work[:, :size] = jnp.where(row <= column, packed, turned) * scale_down * scale
    work[:, size:] = jnp.where(row == column, scale, 0.0)
    hamilton = jnp.where(row > column, packed, jnp.where(row == column, diagonal, turned))
    eliminate(work)
    inverse = jnp.where(row >= column, work[:, size:], 0.0)
    subspace = transposed_dot(dot(inverse, hamilton), inverse)
    subspace_ref[...] = subspace
    planes = natural_ref.shape[0]
    half = planes // 2
    for plane in range(0, half, 2):
        both = [
            dot(
                inverse,
                jnp.concatenate([natural_ref[plane + k], natural_ref[half + plane + k]], axis=1),
            )
            for k in range(2)
        ]
        product = dot(subspace, jnp.concatenate([part[:, :LANES] for part in both], axis=1))
        for k, part in enumerate(both):
            mixed[plane + k] = part[:, :LANES]
            mixed[half + plane + k] = part[:, LANES:] - product[:, k * LANES : (k + 1) * LANES]
    natural_rows(flat_ref, mixed, 0, False)


def solve(summed, natural, cells):
    planes, size, lanes = natural.shape
    return pl.pallas_call(
        functools.partial(solve_kernel, cells),
        out_shape=(
            jax.ShapeDtypeStruct((planes * size, lanes), jnp.float32),
            jax.ShapeDtypeStruct((size, size), jnp.float32),
        ),
        in_specs=[vmem(), vmem()],
        out_specs=(vmem(), vmem()),
        scratch_shapes=[
            pltpu.VMEM((size, 2 * size), jnp.float32),
            pltpu.VMEM(natural.shape, jnp.float32),
        ],
        compiler_params=pltpu.CompilerParams(vmem_limit_bytes=48 * 2**20),
        cost_estimate=pl.CostEstimate(
            flops=20_000_000_000, bytes_accessed=6 * 2**20, transcendentals=256
        ),
        name="solve",
    )(summed, natural)


def assemble_kernel(core_ref, arrived_ref, received_ref, first_ref, second_ref, staged, sems):
    core = core_ref[0]
    blocks = received_ref.shape[0]
    copies = []
    for which, out_ref in enumerate((first_ref, second_ref)):
        for own in range(2):
            slot = 2 * which + own
            if own:
                staged[slot] = arrived_ref[:, pl.ds((core * 2 + which) * ROWS, ROWS), :]
            else:
                staged[slot] = received_ref[:, which * ROWS : (which + 1) * ROWS, :]
            side = core if own else 1 - core
            copy = pltpu.make_async_copy(
                staged.at[slot], out_ref.at[pl.ds(side * blocks, blocks)], sems.at[slot]
            )
            copy.start()
            copies.append(copy)
    for copy in copies:
        copy.wait()


def assemble(core, arrived, received):
    blocks, _, lanes = received.shape
    out = jax.ShapeDtypeStruct((CORES * blocks, ROWS, lanes), jnp.float32)
    return pl.pallas_call(
        assemble_kernel,
        out_shape=(out, out),
        in_specs=[smem(), vmem(), vmem()],
        out_specs=(far_away(), far_away()),
        scratch_shapes=[
            pltpu.VMEM((4, blocks, ROWS, lanes), jnp.float32),
            pltpu.SemaphoreType.DMA((4,)),
        ],
        compiler_params=pltpu.CompilerParams(vmem_limit_bytes=32 * 2**20),
        cost_estimate=pl.CostEstimate(flops=0, bytes_accessed=4 * 2**20, transcendentals=0),
        name="assemble",
    )(core, arrived, received)


def exchange(blocks, groups, axes=AXES):
    return lax.all_to_all(
        blocks, axes, split_axis=0, concat_axis=0, tiled=True, axis_index_groups=groups
    )


class Layout:
    def __init__(self, orb, grp):
        self.x, self.core, self.y = 4, CORES, grp
        self.z = orb // (self.x * self.core)
        self.total = orb * grp

    def orb(self, z, x, core):
        return ((z % self.z) * self.x + x % self.x) * self.core + core % self.core

    def device(self, z, x, core, y):
        return self.orb(z, x, core) * self.y + y

    def places(self):
        return [
            (z, x, core)
            for z in range(self.z)
            for x in range(self.x)
            for core in range(self.core)
        ]

    def chips(self):
        return [
            [
                self.device(z, x, core, y)
                for z in range(self.z)
                for x in range(self.x)
                for y in range(self.y)
            ]
            for core in range(self.core)
        ]

    def planes(self):
        return [
            [
                self.device(z, x, core, y)
                for x in range(self.x)
                for core in range(self.core)
                for y in range(self.y)
            ]
            for z in range(self.z)
        ]

    def columns(self):
        return [
            [self.orb(z, x, core) for z in range(self.z)]
            for x in range(self.x)
            for core in range(self.core)
        ]

    def swap_cores(self, values):
        pairs = [(self.orb(z, x, c), self.orb(z, x, c + 1)) for z, x, c in self.places()]
        return lax.ppermute(values, "orb", pairs)


def reduce_slab(partial, layout):
    me = lax.axis_index("orb")
    core = me % layout.core
    x = me // layout.core % layout.x
    y = lax.axis_index("grp")

    def stage(values, dim, count, index, axis, pairs):
        total = lax.dynamic_index_in_dim(values, index, dim, keepdims=False)
        arrived = [
            lax.ppermute(
                lax.dynamic_index_in_dim(values, (index + k) % count, dim, keepdims=False),
                axis,
                pairs(k),
            )
            for k in range(1, count)
        ]
        for term in arrived:
            total = total + term
        return total

    def along(dx, dc):
        return lambda k: [
            (layout.orb(a, b, c), layout.orb(a, b + dx * k, c + dc * k))
            for a, b, c in layout.places()
        ]

    def lines(k):
        return [(i, (i + k) % layout.y) for i in range(layout.y)]

    values = partial.reshape(layout.z, layout.x, layout.core, layout.y, -1, LANES)
    values = stage(values, 2, layout.core, core, "orb", along(0, 1))
    values = stage(values, 2, layout.y, y, "grp", lines)
    return stage(values, 1, layout.x, x, "orb", along(1, 0))


def sum_everywhere(chunks, slabs, layout):
    count, rows, lanes = chunks.shape
    part = jnp.sum(exchange(chunks, layout.planes()), axis=0, keepdims=True)
    part = jnp.broadcast_to(part, (layout.z, rows, lanes))
    part = exchange(jnp.concatenate([part, slabs], axis=1), layout.columns(), "orb")
    total = jnp.sum(part, axis=0)
    everywhere = jnp.broadcast_to(total[None, :rows], (count, rows, lanes))
    return exchange(everywhere, layout.planes()), total[rows:]


def on_device(layout, orbitals, potential, occupation, region_bounds):
    cell_total = orbitals.shape[1]
    orb, grp = lax.axis_index("orb"), lax.axis_index("grp")
    position = orb * layout.y + grp
    core = orb % layout.core
    place = jnp.stack([position, core]).astype(jnp.int32)
    core = core.reshape(1).astype(jnp.int32)
    keep, give, density_part = apply_hamiltonian(
        place, region_bounds, occupation, orbitals.reshape(G, PAIRS, LANES), potential
    )
    sent = jnp.concatenate([keep, layout.swap_cores(give)], axis=1)
    slabs = reduce_slab(density_part, layout)
    arrived = exchange(sent, layout.chips())
    arrived, slabs = lax.optimization_barrier((arrived, slabs))
    natural, packed = overlap(core, arrived.reshape(-1, LANES))
    summed, density = sum_everywhere(packed, slabs, layout)
    mixed, subspace = solve(summed, natural, cell_total)
    back = exchange(mixed.reshape(-1, 4 * ROWS, LANES), layout.chips())
    back, density = lax.optimization_barrier((back, density.reshape(-1, G)))
    other = lax.dynamic_slice_in_dim(back, (1 - core[0]) * 2 * ROWS, 2 * ROWS, 1)
    orthonormal, gradient = assemble(core, back, layout.swap_cores(other))
    return (
        orthonormal.reshape(1, cell_total),
        gradient.reshape(1, cell_total),
        subspace,
        density,
    )


def solution(mesh):
    in_specs = (P(AXES, None), P(), P(), P())
    out_specs = (P(AXES, None), P(AXES, None), P(), P(AXES, None))
    step = functools.partial(on_device, Layout(mesh.shape["orb"], mesh.shape["grp"]))
    return jax.shard_map(
        step, mesh=mesh, in_specs=in_specs, out_specs=out_specs, check_vma=False
    )
```

```python
import functools

import jax
import jax.numpy as jnp
import ml_dtypes
import numpy as np
from jax import lax
from jax.experimental import pallas as pl
from jax.experimental.pallas import tpu as pltpu
from jax.sharding import PartitionSpec as P

G = 64
LANES = 128
PAIRS = G * G // LANES
PAD = 8
SHIFT = 2
STRIP = 16
ROWS = 8
BLOCK = 64

magic_taps = (0.0028, -0.0236, 0.1026, 0.8364, 0.1026, -0.0236, 0.0028)
kinetic_taps = (
    -1.0 / 560.0,
    8.0 / 315.0,
    -0.2,
    1.6,
    -205.0 / 72.0,
    1.6,
    -0.2,
    8.0 / 315.0,
    -1.0 / 560.0,
)
precise = lax.Precision.HIGHEST
AXES = ("orb", "grp")


def banded(extent, taps):
    radius = len(taps) // 2
    matrix = np.zeros((extent, extent))
    for position, weight in enumerate(taps):
        matrix += weight * np.eye(extent, k=position - radius)
    return matrix


def shifted_blocks(along_y, along_z):
    radius = len(along_y) // 2
    blocks = np.zeros((2 * SHIFT + 1, 2, G, 2, G))
    for shift in range(-SHIFT, SHIFT + 1):
        for source in range(2):
            for target in range(2):
                offset = 2 * shift + source - target
                if abs(offset) <= radius:
                    blocks[shift + SHIFT, source, :, target, :] = (
                        along_y[offset + radius] * along_z.T
                    )
    return blocks.reshape((2 * SHIFT + 1) * LANES, LANES)


def split_constant(matrix):
    high = matrix.astype(ml_dtypes.bfloat16)
    low = (matrix - high.astype(np.float64)).astype(ml_dtypes.bfloat16)
    return high, low


def filter_constants():
    magic = shifted_blocks(magic_taps, banded(G, magic_taps))
    kinetic = shifted_blocks(kinetic_taps, np.eye(G)) + shifted_blocks(
        (1.0,), banded(G, kinetic_taps)
    )
    return np.concatenate(split_constant(np.concatenate([magic, kinetic], axis=1)), axis=1)


def plane_filter(read, first, taps):
    radius = len(taps) // 2
    total = taps[radius] * read(first)
    for step in range(1, radius + 1):
        total += taps[radius + step] * (read(first + step) + read(first - step))
    return total


def hamiltonian_kernel(
    place_ref,
    bounds_hbm,
    orbital_hbm,
    filters_hbm,
    potential_hbm,
    keep_ref,
    give_ref,
    density_ref,
    bounds_ref,
    orbital_ref,
    filters_ref,
    potential_ref,
    source,
    filtered,
    kinetic,
    lines_ref,
    sems,
):
    margin = len(kinetic_taps) // 2
    position, core = place_ref[0], place_ref[1]
    copies = [
        pltpu.make_async_copy(far, near, sems.at[k])
        for k, (far, near) in enumerate(
            (
                (bounds_hbm, bounds_ref),
                (orbital_hbm, orbital_ref),
                (filters_hbm, filters_ref),
                (potential_hbm, potential_ref),
            )
        )
    ]
    for copy in copies:
        copy.start()

    zeros = jnp.zeros((margin, PAIRS + 2 * PAD, LANES), jnp.float32)
    source[:margin] = zeros
    source[margin + G :] = zeros
    edge = jnp.zeros((G + 2 * margin, PAD, LANES), jnp.float32)
    source[:, :PAD] = edge
    source[:, PAD + PAIRS :] = edge
    zeros = jnp.zeros((margin, PAIRS, LANES), jnp.float32)
    filtered[:margin] = zeros
    filtered[margin + G :] = zeros

    def product(x, width):
        shifted = jnp.concatenate(
            [
                source[pl.ds(margin + x, STRIP), PAD + s : PAD + s + PAIRS].reshape(
                    STRIP * PAIRS, LANES
                )
                for s in range(-SHIFT, SHIFT + 1)
            ],
            axis=1,
        )
        high = shifted.astype(jnp.bfloat16)
        low = (shifted - high.astype(jnp.float32)).astype(jnp.bfloat16)
        dot = functools.partial(jnp.dot, preferred_element_type=jnp.float32)
        high_filter = filters_ref[:, :width]
        low_filter = filters_ref[:, 2 * LANES : 2 * LANES + width]
        return dot(high, high_filter) + (dot(low, high_filter) + dot(high, low_filter))

    def own(x):
        return source[pl.ds(margin + x, STRIP), PAD : PAD + PAIRS]

    def half(x):
        return filtered[pl.ds(margin + x, STRIP)]

    copies[0].wait()
    copies[1].wait()
    planes = lax.broadcasted_iota(jnp.int32, (STRIP * PAIRS, LANES), 0) // PAIRS
    bounds = bounds_ref[...]
    own_place = lax.broadcasted_iota(jnp.int32, bounds.shape, 1) == position
    bounds = jnp.sum(jnp.where(own_place, bounds, 0), axis=1, keepdims=True)
    begin, end = bounds[0:1], bounds[1:2]
    blocks = STRIP * PAIRS // ROWS
    half_planes = G // 2

    def tiled(strip):
        return strip.reshape(blocks, ROWS, LANES)

    for side, out_ref in ((core, keep_ref), (1 - core, give_ref)):
        for strip in range(0, half_planes, STRIP):
            x = half_planes * side + strip
            inside = (planes + x >= begin) & (planes + x < end)
            orbital = orbital_ref[pl.ds(x, STRIP)].reshape(STRIP * PAIRS, LANES)
            masked = jnp.where(inside, orbital, 0.0).reshape(STRIP, PAIRS, LANES)
            source[pl.ds(margin + x, STRIP), PAD : PAD + PAIRS] = masked
            first = strip * PAIRS // ROWS
            out_ref[first : first + blocks, :ROWS, :] = tiled(masked)

    copies[2].wait()
    copies[3].wait()

    @pl.loop(0, G, step=STRIP)
    def _(x):
        cells = pl.ds(pl.multiple_of(x * G, STRIP * G), STRIP * G)
        lines_ref[cells, :] = potential_ref[:, cells].T
        both = product(x, 2 * LANES)
        filtered[pl.ds(margin + x, STRIP)] = both[:, :LANES].reshape(STRIP, PAIRS, LANES)
        kinetic[pl.ds(x, STRIP)] = both[:, LANES:].reshape(STRIP, PAIRS, LANES) + plane_filter(
            own, x, kinetic_taps
        )

    lines = STRIP * G // 2

    @pl.loop(0, G, step=STRIP)
    def _(x):
        realspace = plane_filter(half, x, magic_taps)
        density_ref[pl.ds(x, STRIP)] = realspace * realspace
        potential = jnp.concatenate(
            [lines_ref[pl.ds(x * G + odd, lines, stride=2), :] for odd in range(2)], axis=1
        ).reshape(STRIP, PAIRS, LANES)
        source[pl.ds(margin + x, STRIP), PAD : PAD + PAIRS] = realspace * potential

    @pl.loop(0, G, step=STRIP)
    def _(x):
        filtered[pl.ds(margin + x, STRIP)] = product(x, LANES).reshape(
            STRIP, PAIRS, LANES
        )

    for side, out_ref in ((core, keep_ref), (1 - core, give_ref)):
        for strip in range(0, half_planes, STRIP):
            x = half_planes * side + strip
            images = plane_filter(half, x, magic_taps) - 0.5 * kinetic[pl.ds(x, STRIP)]
            first = strip * PAIRS // ROWS
            out_ref[first : first + blocks, ROWS:, :] = tiled(images)


def vmem():
    return pl.BlockSpec(memory_space=pltpu.VMEM)


def smem():
    return pl.BlockSpec(memory_space=pltpu.SMEM)


def far_away():
    return pl.BlockSpec(memory_space=pltpu.HBM)


def apply_hamiltonian(place, region_bounds, orbital, potential):
    margin = len(kinetic_taps) // 2
    side = jax.ShapeDtypeStruct((G * PAIRS // ROWS // 2, 2 * ROWS, LANES), jnp.float32)
    grid = jax.ShapeDtypeStruct((G, PAIRS, LANES), jnp.float32)
    far = (region_bounds.T, orbital, filter_constants(), potential.T)
    far = [jnp.asarray(values) for values in far]
    return pl.pallas_call(
        hamiltonian_kernel,
        out_shape=(side, side, grid),
        in_specs=[smem()] + [far_away()] * len(far),
        out_specs=(vmem(),) * 3,
        scratch_shapes=[pltpu.VMEM(values.shape, values.dtype) for values in far]
        + [
            pltpu.VMEM((G + 2 * margin, PAIRS + 2 * PAD, LANES), jnp.float32),
            pltpu.VMEM((G + 2 * margin, PAIRS, LANES), jnp.float32),
            pltpu.VMEM((G, PAIRS, LANES), jnp.float32),
            pltpu.VMEM((G * G, G), jnp.float32),
            pltpu.SemaphoreType.DMA((len(far),)),
        ],
        compiler_params=pltpu.CompilerParams(vmem_limit_bytes=50 * 2**20),
        cost_estimate=pl.CostEstimate(
            flops=6 * 2048 * 640 * 384, bytes_accessed=5 * 2**20, transcendentals=0
        ),
        name="hamiltonian",
    )(place, *far)


def transposed_dot(a, b):
    return lax.dot_general(
        a, b, (((1,), (1,)), ((), ())), precision=precise, preferred_element_type=jnp.float32
    )


CORES = 2
LINES = 4


def natural_rows(flat_ref, natural_ref, core, gather):
    planes, orbitals, _ = natural_ref.shape
    groups = orbitals // (CORES * LINES)
    stride = CORES * LINES * planes
    for slot in range(CORES):
        for line in range(LINES):
            for plane in range(planes):
                inner = pl.ds((line * CORES + slot) * planes + plane, groups, stride=stride)
                outer = pl.ds((slot ^ core) * LINES + line, groups, stride=CORES * LINES)
                if gather:
                    natural_ref[plane, outer, :] = flat_ref[inner, :]
                else:
                    flat_ref[inner, :] = natural_ref[plane, outer, :]


def overlap_kernel(core_ref, flat_ref, natural_ref, packed_ref, square):
    for core in range(CORES):

        @pl.when(core_ref[0] == core)
        def _(core=core):
            natural_rows(flat_ref, natural_ref, core, True)

    planes, size, _ = natural_ref.shape
    half = planes // 2
    total = None
    for plane in range(0, half, 2):
        psi = jnp.concatenate([natural_ref[plane], natural_ref[plane + 1]], axis=1)
        images = jnp.concatenate(
            [natural_ref[half + plane], natural_ref[half + plane + 1]], axis=1
        )
        term = transposed_dot(psi, jnp.concatenate([psi, images], axis=0))
        total = term if total is None else total + term
    row = lax.broadcasted_iota(jnp.int32, (size, size), 0)
    column = lax.broadcasted_iota(jnp.int32, (size, size), 1)
    hamilton = total[:, size:]
    packed = jnp.where(row <= column, total[:, :size], hamilton)
    diagonal = jnp.where(row == column, hamilton, 0.0)
    chunks = size // ROWS
    parts = size // LANES
    lane_sum = 0.0
    for part in range(parts):
        lanes = slice(part * LANES, (part + 1) * LANES)
        square[part] = packed[:, lanes]
        lane_sum += diagonal[:, lanes]
        for line in range(ROWS):
            packed_ref[pl.ds(part * ROWS + line, chunks, stride=parts * ROWS + 1), :] = square[
                part, pl.ds(line, chunks, stride=ROWS), :
            ]
    packed_ref[pl.ds(parts * ROWS, chunks, stride=parts * ROWS + 1), :] = jnp.sum(
        lane_sum.reshape(chunks, ROWS, LANES), axis=1
    )


def overlap(core, arrived):
    rows, lanes = arrived.shape
    planes = 2 * ROWS
    size = rows // planes
    return pl.pallas_call(
        overlap_kernel,
        out_shape=(
            jax.ShapeDtypeStruct((planes, size, lanes), jnp.float32),
            jax.ShapeDtypeStruct((size // ROWS * (size // LANES * ROWS + 1), LANES), jnp.float32),
        ),
        in_specs=[smem(), vmem()],
        out_specs=(vmem(), vmem()),
        scratch_shapes=[pltpu.VMEM((size // LANES, size, LANES), jnp.float32)],
        compiler_params=pltpu.CompilerParams(vmem_limit_bytes=40 * 2**20),
        cost_estimate=pl.CostEstimate(
            flops=24 * 256 * 256 * 1024, bytes_accessed=4 * 2**20, transcendentals=0
        ),
        name="overlap",
    )(core, arrived)


def eliminate(work):
    size = work.shape[0]
    sub = lax.broadcasted_iota(jnp.int32, (ROWS, LANES), 0)

    def row_of(tile, j):
        return jnp.broadcast_to(tile[j : j + 1, :], tile.shape)

    for start in range(0, size, BLOCK):
        stop = start + BLOCK
        first = start // LANES * LANES
        last = size + (stop + LANES - 1) // LANES * LANES
        lanes = range(first, last, LANES)
        groups = BLOCK // ROWS
        tiles = [
            {c: work[start + g * ROWS : start + (g + 1) * ROWS, c : c + LANES] for c in lanes}
            for g in range(groups)
        ]
        for q in range(groups):
            base = start + q * ROWS
            home, at = base // LANES * LANES, base % LANES
            spread = [
                [
                    jnp.broadcast_to(tiles[g][home][:, at + m : at + m + 1], (ROWS, LANES))
                    for m in range(ROWS)
                ]
                if g >= q
                else None
                for g in range(groups)
            ]
            for j in range(0, ROWS, 2):
                first, second = spread[q][j], spread[q][j + 1]
                pivot, side, corner = row_of(first, j), row_of(first, j + 1), row_of(second, j + 1)
                root = lax.rsqrt(pivot)
                lower = side * root
                root2 = lax.rsqrt(pivot * corner - side * side) * (pivot * root)
                weight, weight2 = {}, {}
                for g in range(q, groups):
                    below, below2 = spread[g][j], spread[g][j + 1]
                    if g == q:
                        below = jnp.where(sub > j + 1, below, 0.0)
                        below2 = jnp.where(sub > j + 1, below2, 0.0)
                    weight[g] = below * root
                    weight2[g] = (below2 - weight[g] * lower) * root2

                def tops(tile):
                    top = row_of(tile, j) * root
                    return top, (row_of(tile, j + 1) - lower * top) * root2

                for m in range(j + 2, ROWS):
                    top, top2 = tops(spread[q][m])
                    for g in range(q, groups):
                        spread[g][m] = spread[g][m] - weight[g] * top - weight2[g] * top2
                for c in lanes:
                    top, top2 = tops(tiles[q][c])
                    for g in range(q, groups):
                        tiles[g][c] = tiles[g][c] - weight[g] * top - weight2[g] * top2
                    here = jnp.where(sub == j + 1, top2, tiles[q][c])
                    tiles[q][c] = jnp.where(sub == j, top, here)
        for g in range(groups):
            for c in lanes:
                work[start + g * ROWS : start + (g + 1) * ROWS, c : c + LANES] = tiles[g][c]
        if stop < size:
            low = stop // LANES * LANES
            done = work[start:stop, :]
            update = lax.dot_general(
                done[:, low:size],
                done[:, low:last],
                (((0,), (0,)), ((), ())),
                precision=precise,
                preferred_element_type=jnp.float32,
            )
            work[stop:, low:last] = work[stop:, low:last] - update[stop - low :, :]


def solve_kernel(
    cells,
    summed_ref,
    natural_ref,
    flat_ref,
    subspace_ref,
    work,
    mixed,
    square,
):
    def dot(a, b):
        return jnp.dot(a, b, precision=precise, preferred_element_type=jnp.float32)

    size = work.shape[0]
    parts = size // LANES
    chunks = size // ROWS
    stride = parts * ROWS + 1
    for part in range(parts):
        for line in range(ROWS):
            square[part, pl.ds(line, chunks, stride=ROWS), :] = summed_ref[
                pl.ds(part * ROWS + line, chunks, stride=stride), :
            ]
    diagonal = summed_ref[pl.ds(parts * ROWS, chunks, stride=stride), :]
    diagonal = jnp.broadcast_to(diagonal[:, None, :], (chunks, ROWS, LANES)).reshape(size, LANES)
    diagonal = jnp.concatenate([diagonal] * parts, axis=1) * (1.0 / cells)
    packed = jnp.concatenate([square[part] for part in range(parts)], axis=1) * (1.0 / cells)
    row = lax.broadcasted_iota(jnp.int32, (size, size), 0)
    column = lax.broadcasted_iota(jnp.int32, (size, size), 1)
    turned = packed.T
    on_diagonal = jnp.where(row == column, packed, 0.0)
    scale = lax.rsqrt(jnp.sum(on_diagonal, axis=0, keepdims=True))
    scale_down = lax.rsqrt(jnp.sum(on_diagonal, axis=1, keepdims=True))
    work[:, :size] = jnp.where(row <= column, packed, turned) * scale_down * scale
    work[:, size:] = jnp.where(row == column, scale, 0.0)
    hamilton = jnp.where(row > column, packed, jnp.where(row == column, diagonal, turned))
    eliminate(work)
    inverse = jnp.where(row >= column, work[:, size:], 0.0)
    subspace = transposed_dot(dot(inverse, hamilton), inverse)
    subspace_ref[...] = subspace
    planes = natural_ref.shape[0]
    half = planes // 2
    for plane in range(0, half, 2):
        both = [
            dot(
                inverse,
                jnp.concatenate([natural_ref[plane + k], natural_ref[half + plane + k]], axis=1),
            )
            for k in range(2)
        ]
        product = dot(subspace, jnp.concatenate([part[:, :LANES] for part in both], axis=1))
        for k, part in enumerate(both):
            mixed[plane + k] = part[:, :LANES]
            mixed[half + plane + k] = part[:, LANES:] - product[:, k * LANES : (k + 1) * LANES]
    natural_rows(flat_ref, mixed, 0, False)


def solve(summed, natural, cells):
    planes, size, lanes = natural.shape
    return pl.pallas_call(
        functools.partial(solve_kernel, cells),
        out_shape=(
            jax.ShapeDtypeStruct((planes * size, lanes), jnp.float32),
            jax.ShapeDtypeStruct((size, size), jnp.float32),
        ),
        in_specs=[vmem(), vmem()],
        out_specs=(vmem(), vmem()),
        scratch_shapes=[
            pltpu.VMEM((size, 2 * size), jnp.float32),
            pltpu.VMEM(natural.shape, jnp.float32),
            pltpu.VMEM((size // LANES, size, LANES), jnp.float32),
        ],
        compiler_params=pltpu.CompilerParams(vmem_limit_bytes=48 * 2**20),
        cost_estimate=pl.CostEstimate(
            flops=20_000_000_000, bytes_accessed=6 * 2**20, transcendentals=256
        ),
        name="solve",
    )(summed, natural)


def assemble_kernel(core_ref, arrived_ref, received_ref, first_ref, second_ref, staged, sems):
    core = core_ref[0]
    blocks = received_ref.shape[0]
    copies = []
    for which, out_ref in enumerate((first_ref, second_ref)):
        for own in range(2):
            slot = 2 * which + own
            if own:
                staged[slot] = arrived_ref[:, pl.ds((core * 2 + which) * ROWS, ROWS), :]
            else:
                staged[slot] = received_ref[:, which * ROWS : (which + 1) * ROWS, :]
            side = core if own else 1 - core
            copy = pltpu.make_async_copy(
                staged.at[slot], out_ref.at[pl.ds(side * blocks, blocks)], sems.at[slot]
            )
            copy.start()
            copies.append(copy)
    for copy in copies:
        copy.wait()


def assemble(core, arrived, received):
    blocks, _, lanes = received.shape
    out = jax.ShapeDtypeStruct((CORES * blocks, ROWS, lanes), jnp.float32)
    return pl.pallas_call(
        assemble_kernel,
        out_shape=(out, out),
        in_specs=[smem(), vmem(), vmem()],
        out_specs=(far_away(), far_away()),
        scratch_shapes=[
            pltpu.VMEM((4, blocks, ROWS, lanes), jnp.float32),
            pltpu.SemaphoreType.DMA((4,)),
        ],
        compiler_params=pltpu.CompilerParams(vmem_limit_bytes=32 * 2**20),
        cost_estimate=pl.CostEstimate(flops=0, bytes_accessed=4 * 2**20, transcendentals=0),
        name="assemble",
    )(core, arrived, received)


def exchange(blocks, groups, axes=AXES):
    return lax.all_to_all(
        blocks, axes, split_axis=0, concat_axis=0, tiled=True, axis_index_groups=groups
    )


class Layout:
    def __init__(self, orb, grp):
        self.x, self.core, self.y = 4, CORES, grp
        self.z = orb // (self.x * self.core)
        self.total = orb * grp

    def orb(self, z, x, core):
        return ((z % self.z) * self.x + x % self.x) * self.core + core % self.core

    def device(self, z, x, core, y):
        return self.orb(z, x, core) * self.y + y

    def places(self):
        return [
            (z, x, core)
            for z in range(self.z)
            for x in range(self.x)
            for core in range(self.core)
        ]

    def chips(self):
        return [
            [
                self.device(z, x, core, y)
                for z in range(self.z)
                for x in range(self.x)
                for y in range(self.y)
            ]
            for core in range(self.core)
        ]

    def planes(self):
        return [
            [
                self.device(z, x, core, y)
                for x in range(self.x)
                for core in range(self.core)
                for y in range(self.y)
            ]
            for z in range(self.z)
        ]

    def columns(self):
        return [
            [self.orb(z, x, core) for z in range(self.z)]
            for x in range(self.x)
            for core in range(self.core)
        ]

    def swap_cores(self, values):
        pairs = [(self.orb(z, x, c), self.orb(z, x, c + 1)) for z, x, c in self.places()]
        return lax.ppermute(values, "orb", pairs)


def reduce_slab(partial, layout):
    me = lax.axis_index("orb")
    core = me % layout.core
    x = me // layout.core % layout.x
    y = lax.axis_index("grp")

    def stage(values, dim, count, index, axis, pairs):
        total = lax.dynamic_index_in_dim(values, index, dim, keepdims=False)
        arrived = [
            lax.ppermute(
                lax.dynamic_index_in_dim(values, (index + k) % count, dim, keepdims=False),
                axis,
                pairs(k),
            )
            for k in range(1, count)
        ]
        for term in arrived:
            total = total + term
        return total

    def along(dx, dc):
        return lambda k: [
            (layout.orb(a, b, c), layout.orb(a, b + dx * k, c + dc * k))
            for a, b, c in layout.places()
        ]

    def lines(k):
        return [(i, (i + k) % layout.y) for i in range(layout.y)]

    values = partial.reshape(layout.z, layout.x, layout.core, layout.y, -1, LANES)
    values = stage(values, 2, layout.core, core, "orb", along(0, 1))
    values = stage(values, 2, layout.y, y, "grp", lines)
    return stage(values, 1, layout.x, x, "orb", along(1, 0))


def sum_everywhere(chunks, slabs, layout):
    count = layout.total // layout.z
    flat = chunks.reshape(count, 1, -1)
    length = flat.shape[2]
    part = jnp.sum(exchange(flat, layout.planes()), axis=0, keepdims=True)
    part = jnp.broadcast_to(part, (layout.z, 1, length))
    slabs = slabs.reshape(layout.z, 1, -1)
    part = exchange(jnp.concatenate([part, slabs], axis=2), layout.columns(), "orb")
    total = jnp.sum(part, axis=0)
    everywhere = jnp.broadcast_to(total[None, :, :length], (count, 1, length))
    return exchange(everywhere, layout.planes()).reshape(chunks.shape), total[:, length:]


def on_device(layout, orbitals, potential, occupation, region_bounds):
    cell_total = orbitals.shape[1]
    orb, grp = lax.axis_index("orb"), lax.axis_index("grp")
    position = orb * layout.y + grp
    core = orb % layout.core
    place = jnp.stack([position, core]).astype(jnp.int32)
    core = core.reshape(1).astype(jnp.int32)
    keep, give, density_part = apply_hamiltonian(
        place, region_bounds, orbitals.reshape(G, PAIRS, LANES), potential
    )
    scale = lax.dynamic_slice_in_dim(occupation, position, 1, 0) / layout.total
    sent = jnp.concatenate([keep, layout.swap_cores(give)], axis=1)
    slabs = reduce_slab(scale * density_part, layout)
    arrived = exchange(sent, layout.chips())
    arrived, slabs = lax.optimization_barrier((arrived, slabs))
    natural, packed = overlap(core, arrived.reshape(-1, LANES))
    summed, density = sum_everywhere(packed, slabs, layout)
    mixed, subspace = solve(summed, natural, cell_total)
    back = exchange(mixed.reshape(-1, 4 * ROWS, LANES), layout.chips())
    back, density = lax.optimization_barrier((back, density.reshape(-1, G)))
    other = lax.dynamic_slice_in_dim(back, (1 - core[0]) * 2 * ROWS, 2 * ROWS, 1)
    orthonormal, gradient = assemble(core, back, layout.swap_cores(other))
    return (
        orthonormal.reshape(1, cell_total),
        gradient.reshape(1, cell_total),
        subspace,
        density,
    )


def solution(mesh):
    in_specs = (P(AXES, None), P(), P(), P())
    out_specs = (P(AXES, None), P(AXES, None), P(), P(AXES, None))
    step = functools.partial(on_device, Layout(mesh.shape["orb"], mesh.shape["grp"]))
    return jax.shard_map(
        step, mesh=mesh, in_specs=in_specs, out_specs=out_specs, check_vma=False
    )
```

```python
import functools

import jax
import jax.numpy as jnp
import ml_dtypes
import numpy as np
from jax import lax
from jax.experimental import pallas as pl
from jax.experimental.pallas import tpu as pltpu
from jax.sharding import PartitionSpec as P

G = 64
LANES = 128
PAIRS = G * G // LANES
PAD = 8
SHIFT = 2
WINDOW = 2 * SHIFT + 2
STRIP = 16
ROWS = 8
BLOCK = 64

magic_taps = (0.0028, -0.0236, 0.1026, 0.8364, 0.1026, -0.0236, 0.0028)
kinetic_taps = (
    -1.0 / 560.0,
    8.0 / 315.0,
    -0.2,
    1.6,
    -205.0 / 72.0,
    1.6,
    -0.2,
    8.0 / 315.0,
    -1.0 / 560.0,
)
precise = lax.Precision.HIGHEST
AXES = ("orb", "grp")


def banded(extent, taps):
    radius = len(taps) // 2
    matrix = np.zeros((extent, extent))
    for position, weight in enumerate(taps):
        matrix += weight * np.eye(extent, k=position - radius)
    return matrix


def shifted_blocks(along_y, along_z):
    radius = len(along_y) // 2
    blocks = np.zeros((2 * SHIFT + 1, 2, G, 2, G))
    for shift in range(-SHIFT, SHIFT + 1):
        for source in range(2):
            for target in range(2):
                offset = 2 * shift + source - target
                if abs(offset) <= radius:
                    blocks[shift + SHIFT, source, :, target, :] = (
                        along_y[offset + radius] * along_z.T
                    )
    return blocks.reshape((2 * SHIFT + 1) * LANES, LANES)


def split_constant(matrix):
    high = matrix.astype(ml_dtypes.bfloat16)
    low = (matrix - high.astype(np.float64)).astype(ml_dtypes.bfloat16)
    return high, low


def paired(matrix):
    blocks = matrix.reshape(2 * SHIFT + 1, LANES, LANES)
    both = np.zeros((WINDOW, LANES, 2, LANES))
    for shift in range(2 * SHIFT + 1):
        for row in range(2):
            both[shift + row, :, row, :] = blocks[shift]
    return both.reshape(WINDOW * LANES, 2 * LANES)


def filter_constants():
    magic = shifted_blocks(magic_taps, banded(G, magic_taps))
    kinetic = shifted_blocks(kinetic_taps, np.eye(G)) + shifted_blocks(
        (1.0,), banded(G, kinetic_taps)
    )
    return np.concatenate(
        split_constant(np.concatenate([paired(magic), paired(kinetic)], axis=1)), axis=1
    )


def plane_filter(read, first, taps):
    radius = len(taps) // 2
    total = taps[radius] * read(first)
    for step in range(1, radius + 1):
        total += taps[radius + step] * (read(first + step) + read(first - step))
    return total


def hamiltonian_kernel(
    place_ref,
    bounds_hbm,
    orbital_hbm,
    filters_hbm,
    potential_hbm,
    keep_ref,
    give_ref,
    density_ref,
    bounds_ref,
    orbital_ref,
    filters_ref,
    potential_ref,
    source,
    filtered,
    kinetic,
    lines_ref,
    sems,
):
    margin = len(kinetic_taps) // 2
    position, core = place_ref[0], place_ref[1]
    copies = [
        pltpu.make_async_copy(far, near, sems.at[k])
        for k, (far, near) in enumerate(
            (
                (bounds_hbm, bounds_ref),
                (orbital_hbm, orbital_ref),
                (filters_hbm, filters_ref),
                (potential_hbm, potential_ref),
            )
        )
    ]
    for copy in copies:
        copy.start()

    zeros = jnp.zeros((margin, PAIRS + 2 * PAD, LANES), jnp.float32)
    source[:margin] = zeros
    source[margin + G :] = zeros
    edge = jnp.zeros((G + 2 * margin, PAD, LANES), jnp.float32)
    source[:, :PAD] = edge
    source[:, PAD + PAIRS :] = edge
    zeros = jnp.zeros((margin, PAIRS, LANES), jnp.float32)
    filtered[:margin] = zeros
    filtered[margin + G :] = zeros

    def product(x, kinds):
        shifted = jnp.concatenate(
            [
                source[
                    pl.ds(margin + x, STRIP), pl.ds(PAD + s, PAIRS // 2, stride=2), :
                ].reshape(STRIP * PAIRS // 2, LANES)
                for s in range(-SHIFT, WINDOW - SHIFT)
            ],
            axis=1,
        )
        high = shifted.astype(jnp.bfloat16)
        low = (shifted - high.astype(jnp.float32)).astype(jnp.bfloat16)
        dot = functools.partial(jnp.dot, preferred_element_type=jnp.float32)
        width = 2 * kinds * LANES
        high_filter = filters_ref[:, :width]
        low_filter = filters_ref[:, 4 * LANES : 4 * LANES + width]
        out = dot(high, high_filter) + (dot(low, high_filter) + dot(high, low_filter))
        return [
            [
                out[:, (2 * kind + odd) * LANES : (2 * kind + odd + 1) * LANES].reshape(
                    STRIP, PAIRS // 2, LANES
                )
                for odd in range(2)
            ]
            for kind in range(kinds)
        ]

    def every_second(odd):
        return pl.ds(odd, PAIRS // 2, stride=2)

    def own(x):
        return source[pl.ds(margin + x, STRIP), PAD : PAD + PAIRS]

    def half(x):
        return filtered[pl.ds(margin + x, STRIP)]

    copies[0].wait()
    copies[1].wait()
    planes = lax.broadcasted_iota(jnp.int32, (STRIP * PAIRS, LANES), 0) // PAIRS
    bounds = bounds_ref[...]
    own_place = lax.broadcasted_iota(jnp.int32, bounds.shape, 1) == position
    bounds = jnp.sum(jnp.where(own_place, bounds, 0), axis=1, keepdims=True)
    begin, end = bounds[0:1], bounds[1:2]
    blocks = STRIP * PAIRS // ROWS
    half_planes = G // 2

    def tiled(strip):
        return strip.reshape(blocks, ROWS, LANES)

    for side, out_ref in ((core, keep_ref), (1 - core, give_ref)):
        for strip in range(0, half_planes, STRIP):
            x = half_planes * side + strip
            inside = (planes + x >= begin) & (planes + x < end)
            orbital = orbital_ref[pl.ds(x, STRIP)].reshape(STRIP * PAIRS, LANES)
            masked = jnp.where(inside, orbital, 0.0).reshape(STRIP, PAIRS, LANES)
            source[pl.ds(margin + x, STRIP), PAD : PAD + PAIRS] = masked
            first = strip * PAIRS // ROWS
            out_ref[first : first + blocks, :ROWS, :] = tiled(masked)

    copies[2].wait()
    copies[3].wait()

    @pl.loop(0, G, step=STRIP)
    def _(x):
        cells = pl.ds(pl.multiple_of(x * G, STRIP * G), STRIP * G)
        lines_ref[cells, :] = potential_ref[:, cells].T
        kinetic[pl.ds(x, STRIP)] = plane_filter(own, x, kinetic_taps)
        magic_rows, kinetic_rows = product(x, 2)
        for odd in range(2):
            filtered[pl.ds(margin + x, STRIP), every_second(odd), :] = magic_rows[odd]
            kinetic[pl.ds(x, STRIP), every_second(odd), :] += kinetic_rows[odd]

    lines = STRIP * G // 2

    @pl.loop(0, G, step=STRIP)
    def _(x):
        realspace = plane_filter(half, x, magic_taps)
        density_ref[pl.ds(x, STRIP)] = realspace * realspace
        potential = jnp.concatenate(
            [lines_ref[pl.ds(x * G + odd, lines, stride=2), :] for odd in range(2)], axis=1
        ).reshape(STRIP, PAIRS, LANES)
        source[pl.ds(margin + x, STRIP), PAD : PAD + PAIRS] = realspace * potential

    @pl.loop(0, G, step=STRIP)
    def _(x):
        (magic_rows,) = product(x, 1)
        for odd in range(2):
            filtered[pl.ds(margin + x, STRIP), every_second(odd), :] = magic_rows[odd]

    for side, out_ref in ((core, keep_ref), (1 - core, give_ref)):
        for strip in range(0, half_planes, STRIP):
            x = half_planes * side + strip
            images = plane_filter(half, x, magic_taps) - 0.5 * kinetic[pl.ds(x, STRIP)]
            first = strip * PAIRS // ROWS
            out_ref[first : first + blocks, ROWS:, :] = tiled(images)


def vmem():
    return pl.BlockSpec(memory_space=pltpu.VMEM)


def smem():
    return pl.BlockSpec(memory_space=pltpu.SMEM)


def far_away():
    return pl.BlockSpec(memory_space=pltpu.HBM)


def apply_hamiltonian(place, region_bounds, orbital, potential):
    margin = len(kinetic_taps) // 2
    side = jax.ShapeDtypeStruct((G * PAIRS // ROWS // 2, 2 * ROWS, LANES), jnp.float32)
    grid = jax.ShapeDtypeStruct((G, PAIRS, LANES), jnp.float32)
    far = (region_bounds.T, orbital, filter_constants(), potential.T)
    far = [jnp.asarray(values) for values in far]
    return pl.pallas_call(
        hamiltonian_kernel,
        out_shape=(side, side, grid),
        in_specs=[smem()] + [far_away()] * len(far),
        out_specs=(vmem(),) * 3,
        scratch_shapes=[pltpu.VMEM(values.shape, values.dtype) for values in far]
        + [
            pltpu.VMEM((G + 2 * margin, PAIRS + 2 * PAD, LANES), jnp.float32),
            pltpu.VMEM((G + 2 * margin, PAIRS, LANES), jnp.float32),
            pltpu.VMEM((G, PAIRS, LANES), jnp.float32),
            pltpu.VMEM((G * G, G), jnp.float32),
            pltpu.SemaphoreType.DMA((len(far),)),
        ],
        compiler_params=pltpu.CompilerParams(vmem_limit_bytes=50 * 2**20),
        cost_estimate=pl.CostEstimate(
            flops=6 * 2048 * 640 * 384, bytes_accessed=5 * 2**20, transcendentals=0
        ),
        name="hamiltonian",
    )(place, *far)


def transposed_dot(a, b):
    return lax.dot_general(
        a, b, (((1,), (1,)), ((), ())), precision=precise, preferred_element_type=jnp.float32
    )


CORES = 2
LINES = 4


def natural_rows(flat_ref, natural_ref, core, gather):
    planes, orbitals, _ = natural_ref.shape
    groups = orbitals // (CORES * LINES)
    stride = CORES * LINES * planes
    for slot in range(CORES):
        for line in range(LINES):
            for plane in range(planes):
                inner = pl.ds((line * CORES + slot) * planes + plane, groups, stride=stride)
                outer = pl.ds((slot ^ core) * LINES + line, groups, stride=CORES * LINES)
                if gather:
                    natural_ref[plane, outer, :] = flat_ref[inner, :]
                else:
                    flat_ref[inner, :] = natural_ref[plane, outer, :]


def overlap_kernel(core_ref, flat_ref, natural_ref, packed_ref, square):
    for core in range(CORES):

        @pl.when(core_ref[0] == core)
        def _(core=core):
            natural_rows(flat_ref, natural_ref, core, True)

    planes, size, _ = natural_ref.shape
    half = planes // 2
    total = None
    for plane in range(0, half, 2):
        psi = jnp.concatenate([natural_ref[plane], natural_ref[plane + 1]], axis=1)
        images = jnp.concatenate(
            [natural_ref[half + plane], natural_ref[half + plane + 1]], axis=1
        )
        term = transposed_dot(psi, jnp.concatenate([psi, images], axis=0))
        total = term if total is None else total + term
    row = lax.broadcasted_iota(jnp.int32, (size, size), 0)
    column = lax.broadcasted_iota(jnp.int32, (size, size), 1)
    hamilton = total[:, size:]
    packed = jnp.where(row <= column, total[:, :size], hamilton)
    diagonal = jnp.where(row == column, hamilton, 0.0)
    chunks = size // ROWS
    parts = size // LANES
    lane_sum = 0.0
    for part in range(parts):
        lanes = slice(part * LANES, (part + 1) * LANES)
        square[part] = packed[:, lanes]
        lane_sum += diagonal[:, lanes]
        for line in range(ROWS):
            packed_ref[pl.ds(part * ROWS + line, chunks, stride=parts * ROWS + 1), :] = square[
                part, pl.ds(line, chunks, stride=ROWS), :
            ]
    packed_ref[pl.ds(parts * ROWS, chunks, stride=parts * ROWS + 1), :] = jnp.sum(
        lane_sum.reshape(chunks, ROWS, LANES), axis=1
    )


def overlap(core, arrived):
    rows, lanes = arrived.shape
    planes = 2 * ROWS
    size = rows // planes
    return pl.pallas_call(
        overlap_kernel,
        out_shape=(
            jax.ShapeDtypeStruct((planes, size, lanes), jnp.float32),
            jax.ShapeDtypeStruct((size // ROWS * (size // LANES * ROWS + 1), LANES), jnp.float32),
        ),
        in_specs=[smem(), vmem()],
        out_specs=(vmem(), vmem()),
        scratch_shapes=[pltpu.VMEM((size // LANES, size, LANES), jnp.float32)],
        compiler_params=pltpu.CompilerParams(vmem_limit_bytes=40 * 2**20),
        cost_estimate=pl.CostEstimate(
            flops=24 * 256 * 256 * 1024, bytes_accessed=4 * 2**20, transcendentals=0
        ),
        name="overlap",
    )(core, arrived)


def eliminate(work):
    size = work.shape[0]
    sub = lax.broadcasted_iota(jnp.int32, (ROWS, LANES), 0)

    def row_of(tile, j):
        return jnp.broadcast_to(tile[j : j + 1, :], tile.shape)

    for start in range(0, size, BLOCK):
        stop = start + BLOCK
        first = start // LANES * LANES
        last = size + (stop + LANES - 1) // LANES * LANES
        lanes = range(first, last, LANES)
        groups = BLOCK // ROWS
        tiles = [
            {c: work[start + g * ROWS : start + (g + 1) * ROWS, c : c + LANES] for c in lanes}
            for g in range(groups)
        ]
        for q in range(groups):
            base = start + q * ROWS
            home, at = base // LANES * LANES, base % LANES
            spread = [
                [
                    jnp.broadcast_to(tiles[g][home][:, at + m : at + m + 1], (ROWS, LANES))
                    for m in range(ROWS)
                ]
                if g >= q
                else None
                for g in range(groups)
            ]
            for j in range(0, ROWS, 2):
                first, second = spread[q][j], spread[q][j + 1]
                pivot, side, corner = row_of(first, j), row_of(first, j + 1), row_of(second, j + 1)
                root = lax.rsqrt(pivot)
                lower = side * root
                root2 = lax.rsqrt(pivot * corner - side * side) * (pivot * root)
                weight, weight2 = {}, {}
                for g in range(q, groups):
                    below, below2 = spread[g][j], spread[g][j + 1]
                    if g == q:
                        below = jnp.where(sub > j + 1, below, 0.0)
                        below2 = jnp.where(sub > j + 1, below2, 0.0)
                    weight[g] = below * root
                    weight2[g] = (below2 - weight[g] * lower) * root2

                def tops(tile):
                    top = row_of(tile, j) * root
                    return top, (row_of(tile, j + 1) - lower * top) * root2

                for m in range(j + 2, ROWS):
                    top, top2 = tops(spread[q][m])
                    for g in range(q, groups):
                        spread[g][m] = spread[g][m] - weight[g] * top - weight2[g] * top2
                for c in lanes:
                    top, top2 = tops(tiles[q][c])
                    for g in range(q, groups):
                        tiles[g][c] = tiles[g][c] - weight[g] * top - weight2[g] * top2
                    here = jnp.where(sub == j + 1, top2, tiles[q][c])
                    tiles[q][c] = jnp.where(sub == j, top, here)
        for g in range(groups):
            for c in lanes:
                work[start + g * ROWS : start + (g + 1) * ROWS, c : c + LANES] = tiles[g][c]
        if stop < size:
            low = stop // LANES * LANES
            done = work[start:stop, :]
            update = lax.dot_general(
                done[:, low:size],
                done[:, low:last],
                (((0,), (0,)), ((), ())),
                precision=precise,
                preferred_element_type=jnp.float32,
            )
            work[stop:, low:last] = work[stop:, low:last] - update[stop - low :, :]


def solve_kernel(
    cells,
    summed_ref,
    natural_ref,
    flat_ref,
    subspace_ref,
    work,
    mixed,
    square,
):
    def dot(a, b):
        return jnp.dot(a, b, precision=precise, preferred_element_type=jnp.float32)

    size = work.shape[0]
    parts = size // LANES
    chunks = size // ROWS
    stride = parts * ROWS + 1
    for part in range(parts):
        for line in range(ROWS):
            square[part, pl.ds(line, chunks, stride=ROWS), :] = summed_ref[
                pl.ds(part * ROWS + line, chunks, stride=stride), :
            ]
    diagonal = summed_ref[pl.ds(parts * ROWS, chunks, stride=stride), :]
    diagonal = jnp.broadcast_to(diagonal[:, None, :], (chunks, ROWS, LANES)).reshape(size, LANES)
    diagonal = jnp.concatenate([diagonal] * parts, axis=1) * (1.0 / cells)
    packed = jnp.concatenate([square[part] for part in range(parts)], axis=1) * (1.0 / cells)
    row = lax.broadcasted_iota(jnp.int32, (size, size), 0)
    column = lax.broadcasted_iota(jnp.int32, (size, size), 1)
    turned = packed.T
    on_diagonal = jnp.where(row == column, packed, 0.0)
    scale = lax.rsqrt(jnp.sum(on_diagonal, axis=0, keepdims=True))
    scale_down = lax.rsqrt(jnp.sum(on_diagonal, axis=1, keepdims=True))
    work[:, :size] = jnp.where(row <= column, packed, turned) * scale_down * scale
    work[:, size:] = jnp.where(row == column, scale, 0.0)
    hamilton = jnp.where(row > column, packed, jnp.where(row == column, diagonal, turned))
    eliminate(work)
    inverse = jnp.where(row >= column, work[:, size:], 0.0)
    subspace = transposed_dot(dot(inverse, hamilton), inverse)
    subspace_ref[...] = subspace
    planes = natural_ref.shape[0]
    half = planes // 2
    for plane in range(0, half, 2):
        both = [
            dot(
                inverse,
                jnp.concatenate([natural_ref[plane + k], natural_ref[half + plane + k]], axis=1),
            )
            for k in range(2)
        ]
        product = dot(subspace, jnp.concatenate([part[:, :LANES] for part in both], axis=1))
        for k, part in enumerate(both):
            mixed[plane + k] = part[:, :LANES]
            mixed[half + plane + k] = part[:, LANES:] - product[:, k * LANES : (k + 1) * LANES]
    natural_rows(flat_ref, mixed, 0, False)


def solve(summed, natural, cells):
    planes, size, lanes = natural.shape
    return pl.pallas_call(
        functools.partial(solve_kernel, cells),
        out_shape=(
            jax.ShapeDtypeStruct((planes * size, lanes), jnp.float32),
            jax.ShapeDtypeStruct((size, size), jnp.float32),
        ),
        in_specs=[vmem(), vmem()],
        out_specs=(vmem(), vmem()),
        scratch_shapes=[
            pltpu.VMEM((size, 2 * size), jnp.float32),
            pltpu.VMEM(natural.shape, jnp.float32),
            pltpu.VMEM((size // LANES, size, LANES), jnp.float32),
        ],
        compiler_params=pltpu.CompilerParams(vmem_limit_bytes=48 * 2**20),
        cost_estimate=pl.CostEstimate(
            flops=20_000_000_000, bytes_accessed=6 * 2**20, transcendentals=256
        ),
        name="solve",
    )(summed, natural)


def assemble_kernel(core_ref, arrived_ref, received_ref, first_ref, second_ref, staged, sems):
    core = core_ref[0]
    blocks = received_ref.shape[0]
    copies = []
    for which, out_ref in enumerate((first_ref, second_ref)):
        for own in range(2):
            slot = 2 * which + own
            if own:
                staged[slot] = arrived_ref[:, pl.ds((core * 2 + which) * ROWS, ROWS), :]
            else:
                staged[slot] = received_ref[:, which * ROWS : (which + 1) * ROWS, :]
            side = core if own else 1 - core
            copy = pltpu.make_async_copy(
                staged.at[slot], out_ref.at[pl.ds(side * blocks, blocks)], sems.at[slot]
            )
            copy.start()
            copies.append(copy)
    for copy in copies:
        copy.wait()


def assemble(core, arrived, received):
    blocks, _, lanes = received.shape
    out = jax.ShapeDtypeStruct((CORES * blocks, ROWS, lanes), jnp.float32)
    return pl.pallas_call(
        assemble_kernel,
        out_shape=(out, out),
        in_specs=[smem(), vmem(), vmem()],
        out_specs=(far_away(), far_away()),
        scratch_shapes=[
            pltpu.VMEM((4, blocks, ROWS, lanes), jnp.float32),
            pltpu.SemaphoreType.DMA((4,)),
        ],
        compiler_params=pltpu.CompilerParams(vmem_limit_bytes=32 * 2**20),
        cost_estimate=pl.CostEstimate(flops=0, bytes_accessed=4 * 2**20, transcendentals=0),
        name="assemble",
    )(core, arrived, received)


def exchange(blocks, groups, axes=AXES):
    return lax.all_to_all(
        blocks, axes, split_axis=0, concat_axis=0, tiled=True, axis_index_groups=groups
    )


class Layout:
    def __init__(self, orb, grp):
        self.x, self.core, self.y = 4, CORES, grp
        self.z = orb // (self.x * self.core)
        self.total = orb * grp

    def orb(self, z, x, core):
        return ((z % self.z) * self.x + x % self.x) * self.core + core % self.core

    def device(self, z, x, core, y):
        return self.orb(z, x, core) * self.y + y

    def places(self):
        return [
            (z, x, core)
            for z in range(self.z)
            for x in range(self.x)
            for core in range(self.core)
        ]

    def chips(self):
        return [
            [
                self.device(z, x, core, y)
                for z in range(self.z)
                for x in range(self.x)
                for y in range(self.y)
            ]
            for core in range(self.core)
        ]

    def planes(self):
        return [
            [
                self.device(z, x, core, y)
                for x in range(self.x)
                for core in range(self.core)
                for y in range(self.y)
            ]
            for z in range(self.z)
        ]

    def columns(self):
        return [
            [self.orb(z, x, core) for z in range(self.z)]
            for x in range(self.x)
            for core in range(self.core)
        ]

    def swap_cores(self, values):
        pairs = [(self.orb(z, x, c), self.orb(z, x, c + 1)) for z, x, c in self.places()]
        return lax.ppermute(values, "orb", pairs)


def reduce_slab(partial, layout):
    me = lax.axis_index("orb")
    core = me % layout.core
    x = me // layout.core % layout.x
    y = lax.axis_index("grp")

    def stage(values, dim, count, index, axis, pairs):
        total = lax.dynamic_index_in_dim(values, index, dim, keepdims=False)
        arrived = [
            lax.ppermute(
                lax.dynamic_index_in_dim(values, (index + k) % count, dim, keepdims=False),
                axis,
                pairs(k),
            )
            for k in range(1, count)
        ]
        for term in arrived:
            total = total + term
        return total

    def along(dx, dc):
        return lambda k: [
            (layout.orb(a, b, c), layout.orb(a, b + dx * k, c + dc * k))
            for a, b, c in layout.places()
        ]

    def lines(k):
        return [(i, (i + k) % layout.y) for i in range(layout.y)]

    values = partial.reshape(layout.z, layout.x, layout.core, layout.y, -1, LANES)
    values = stage(values, 2, layout.core, core, "orb", along(0, 1))
    values = stage(values, 2, layout.y, y, "grp", lines)
    return stage(values, 1, layout.x, x, "orb", along(1, 0))


def sum_everywhere(chunks, slabs, layout):
    count = layout.total // layout.z
    flat = chunks.reshape(count, 1, -1)
    length = flat.shape[2]
    part = jnp.sum(exchange(flat, layout.planes()), axis=0, keepdims=True)
    part = jnp.broadcast_to(part, (layout.z, 1, length))
    slabs = slabs.reshape(layout.z, 1, -1)
    part = exchange(jnp.concatenate([part, slabs], axis=2), layout.columns(), "orb")
    total = jnp.sum(part, axis=0)
    everywhere = jnp.broadcast_to(total[None, :, :length], (count, 1, length))
    return exchange(everywhere, layout.planes()).reshape(chunks.shape), total[:, length:]


def on_device(layout, orbitals, potential, occupation, region_bounds):
    cell_total = orbitals.shape[1]
    orb, grp = lax.axis_index("orb"), lax.axis_index("grp")
    position = orb * layout.y + grp
    core = orb % layout.core
    place = jnp.stack([position, core]).astype(jnp.int32)
    core = core.reshape(1).astype(jnp.int32)
    keep, give, density_part = apply_hamiltonian(
        place, region_bounds, orbitals.reshape(G, PAIRS, LANES), potential
    )
    scale = lax.dynamic_slice_in_dim(occupation, position, 1, 0) / layout.total
    sent = jnp.concatenate([keep, layout.swap_cores(give)], axis=1)
    slabs = reduce_slab(scale * density_part, layout)
    arrived = exchange(sent, layout.chips())
    arrived, slabs = lax.optimization_barrier((arrived, slabs))
    natural, packed = overlap(core, arrived.reshape(-1, LANES))
    summed, density = sum_everywhere(packed, slabs, layout)
    mixed, subspace = solve(summed, natural, cell_total)
    back = exchange(mixed.reshape(-1, 4 * ROWS, LANES), layout.chips())
    back, density = lax.optimization_barrier((back, density.reshape(-1, G)))
    other = lax.dynamic_slice_in_dim(back, (1 - core[0]) * 2 * ROWS, 2 * ROWS, 1)
    orthonormal, gradient = assemble(core, back, layout.swap_cores(other))
    return (
        orthonormal.reshape(1, cell_total),
        gradient.reshape(1, cell_total),
        subspace,
        density,
    )


def solution(mesh):
    in_specs = (P(AXES, None), P(), P(), P())
    out_specs = (P(AXES, None), P(AXES, None), P(), P(AXES, None))
    step = functools.partial(on_device, Layout(mesh.shape["orb"], mesh.shape["grp"]))
    return jax.shard_map(
        step, mesh=mesh, in_specs=in_specs, out_specs=out_specs, check_vma=False
    )
```

```python
import functools

import jax
import jax.numpy as jnp
import ml_dtypes
import numpy as np
from jax import lax
from jax.experimental import pallas as pl
from jax.experimental.pallas import tpu as pltpu
from jax.sharding import PartitionSpec as P

G = 64
LANES = 128
PAIRS = G * G // LANES
PAD = 8
SHIFT = 2
WINDOW = 2 * SHIFT + 2
STRIP = 32
ROWS = 8
BLOCK = 64

magic_taps = (0.0028, -0.0236, 0.1026, 0.8364, 0.1026, -0.0236, 0.0028)
kinetic_taps = (
    -1.0 / 560.0,
    8.0 / 315.0,
    -0.2,
    1.6,
    -205.0 / 72.0,
    1.6,
    -0.2,
    8.0 / 315.0,
    -1.0 / 560.0,
)
precise = lax.Precision.HIGHEST
AXES = ("orb", "grp")


def banded(extent, taps):
    radius = len(taps) // 2
    matrix = np.zeros((extent, extent))
    for position, weight in enumerate(taps):
        matrix += weight * np.eye(extent, k=position - radius)
    return matrix


def shifted_blocks(along_y, along_z):
    radius = len(along_y) // 2
    blocks = np.zeros((2 * SHIFT + 1, 2, G, 2, G))
    for shift in range(-SHIFT, SHIFT + 1):
        for source in range(2):
            for target in range(2):
                offset = 2 * shift + source - target
                if abs(offset) <= radius:
                    blocks[shift + SHIFT, source, :, target, :] = (
                        along_y[offset + radius] * along_z.T
                    )
    return blocks.reshape((2 * SHIFT + 1) * LANES, LANES)


def split_constant(matrix):
    high = matrix.astype(ml_dtypes.bfloat16)
    low = (matrix - high.astype(np.float64)).astype(ml_dtypes.bfloat16)
    return high, low


def paired(matrix):
    blocks = matrix.reshape(2 * SHIFT + 1, LANES, LANES)
    both = np.zeros((WINDOW, LANES, 2, LANES))
    for shift in range(2 * SHIFT + 1):
        for row in range(2):
            both[shift + row, :, row, :] = blocks[shift]
    return both.reshape(WINDOW * LANES, 2 * LANES)


def filter_constants():
    magic = shifted_blocks(magic_taps, banded(G, magic_taps))
    kinetic = shifted_blocks(kinetic_taps, np.eye(G)) + shifted_blocks(
        (1.0,), banded(G, kinetic_taps)
    )
    return np.concatenate(
        split_constant(np.concatenate([paired(magic), paired(kinetic)], axis=1)), axis=1
    )


def plane_filter(read, first, taps):
    radius = len(taps) // 2
    total = taps[radius] * read(first)
    for step in range(1, radius + 1):
        total += taps[radius + step] * (read(first + step) + read(first - step))
    return total


def hamiltonian_kernel(
    place_ref,
    bounds_hbm,
    orbital_hbm,
    filters_hbm,
    potential_hbm,
    keep_ref,
    give_ref,
    density_ref,
    bounds_ref,
    orbital_ref,
    filters_ref,
    potential_ref,
    source,
    filtered,
    kinetic,
    lines_ref,
    sems,
):
    margin = len(kinetic_taps) // 2
    position, core = place_ref[0], place_ref[1]
    copies = [
        pltpu.make_async_copy(far, near, sems.at[k])
        for k, (far, near) in enumerate(
            (
                (bounds_hbm, bounds_ref),
                (orbital_hbm, orbital_ref),
                (filters_hbm, filters_ref),
                (potential_hbm, potential_ref),
            )
        )
    ]
    for copy in copies:
        copy.start()

    zeros = jnp.zeros((margin, PAIRS + 2 * PAD, LANES), jnp.float32)
    source[:margin] = zeros
    source[margin + G :] = zeros
    edge = jnp.zeros((G + 2 * margin, PAD, LANES), jnp.float32)
    source[:, :PAD] = edge
    source[:, PAD + PAIRS :] = edge
    zeros = jnp.zeros((margin, PAIRS, LANES), jnp.float32)
    filtered[:margin] = zeros
    filtered[margin + G :] = zeros

    def product(x, kinds):
        shifted = jnp.concatenate(
            [
                source[
                    pl.ds(margin + x, STRIP), pl.ds(PAD + s, PAIRS // 2, stride=2), :
                ].reshape(STRIP * PAIRS // 2, LANES)
                for s in range(-SHIFT, WINDOW - SHIFT)
            ],
            axis=1,
        )
        high = shifted.astype(jnp.bfloat16)
        low = (shifted - high.astype(jnp.float32)).astype(jnp.bfloat16)
        dot = functools.partial(jnp.dot, preferred_element_type=jnp.float32)
        width = 2 * kinds * LANES
        high_filter = filters_ref[:, :width]
        low_filter = filters_ref[:, 4 * LANES : 4 * LANES + width]
        out = dot(high, high_filter) + (dot(low, high_filter) + dot(high, low_filter))
        return [
            [
                out[:, (2 * kind + odd) * LANES : (2 * kind + odd + 1) * LANES].reshape(
                    STRIP, PAIRS // 2, LANES
                )
                for odd in range(2)
            ]
            for kind in range(kinds)
        ]

    def every_second(odd):
        return pl.ds(odd, PAIRS // 2, stride=2)

    def own(x):
        return source[pl.ds(margin + x, STRIP), PAD : PAD + PAIRS]

    def half(x):
        return filtered[pl.ds(margin + x, STRIP)]

    copies[0].wait()
    copies[1].wait()
    planes = lax.broadcasted_iota(jnp.int32, (STRIP * PAIRS, LANES), 0) // PAIRS
    bounds = bounds_ref[...]
    own_place = lax.broadcasted_iota(jnp.int32, bounds.shape, 1) == position
    bounds = jnp.sum(jnp.where(own_place, bounds, 0), axis=1, keepdims=True)
    begin, end = bounds[0:1], bounds[1:2]
    blocks = STRIP * PAIRS // ROWS
    half_planes = G // 2

    def tiled(strip):
        return strip.reshape(blocks, ROWS, LANES)

    for side, out_ref in ((core, keep_ref), (1 - core, give_ref)):
        for strip in range(0, half_planes, STRIP):
            x = half_planes * side + strip
            inside = (planes + x >= begin) & (planes + x < end)
            orbital = orbital_ref[pl.ds(x, STRIP)].reshape(STRIP * PAIRS, LANES)
            masked = jnp.where(inside, orbital, 0.0).reshape(STRIP, PAIRS, LANES)
            source[pl.ds(margin + x, STRIP), PAD : PAD + PAIRS] = masked
            first = strip * PAIRS // ROWS
            out_ref[first : first + blocks, :ROWS, :] = tiled(masked)

    copies[2].wait()
    copies[3].wait()

    @pl.loop(0, G, step=STRIP)
    def _(x):
        cells = pl.ds(pl.multiple_of(x * G, STRIP * G), STRIP * G)
        lines_ref[cells, :] = potential_ref[:, cells].T
        kinetic[pl.ds(x, STRIP)] = plane_filter(own, x, kinetic_taps)
        magic_rows, kinetic_rows = product(x, 2)
        for odd in range(2):
            filtered[pl.ds(margin + x, STRIP), every_second(odd), :] = magic_rows[odd]
            kinetic[pl.ds(x, STRIP), every_second(odd), :] += kinetic_rows[odd]

    lines = STRIP * G // 2

    @pl.loop(0, G, step=STRIP)
    def _(x):
        realspace = plane_filter(half, x, magic_taps)
        density_ref[pl.ds(x, STRIP)] = realspace * realspace
        potential = jnp.concatenate(
            [lines_ref[pl.ds(x * G + odd, lines, stride=2), :] for odd in range(2)], axis=1
        ).reshape(STRIP, PAIRS, LANES)
        source[pl.ds(margin + x, STRIP), PAD : PAD + PAIRS] = realspace * potential

    @pl.loop(0, G, step=STRIP)
    def _(x):
        (magic_rows,) = product(x, 1)
        for odd in range(2):
            filtered[pl.ds(margin + x, STRIP), every_second(odd), :] = magic_rows[odd]

    for side, out_ref in ((core, keep_ref), (1 - core, give_ref)):
        for strip in range(0, half_planes, STRIP):
            x = half_planes * side + strip
            images = plane_filter(half, x, magic_taps) - 0.5 * kinetic[pl.ds(x, STRIP)]
            first = strip * PAIRS // ROWS
            out_ref[first : first + blocks, ROWS:, :] = tiled(images)


def vmem():
    return pl.BlockSpec(memory_space=pltpu.VMEM)


def smem():
    return pl.BlockSpec(memory_space=pltpu.SMEM)


def far_away():
    return pl.BlockSpec(memory_space=pltpu.HBM)


def apply_hamiltonian(place, region_bounds, orbital, potential):
    margin = len(kinetic_taps) // 2
    side = jax.ShapeDtypeStruct((G * PAIRS // ROWS // 2, 2 * ROWS, LANES), jnp.float32)
    grid = jax.ShapeDtypeStruct((G, PAIRS, LANES), jnp.float32)
    far = (region_bounds.T, orbital, filter_constants(), potential.T)
    far = [jnp.asarray(values) for values in far]
    return pl.pallas_call(
        hamiltonian_kernel,
        out_shape=(side, side, grid),
        in_specs=[smem()] + [far_away()] * len(far),
        out_specs=(vmem(),) * 3,
        scratch_shapes=[pltpu.VMEM(values.shape, values.dtype) for values in far]
        + [
            pltpu.VMEM((G + 2 * margin, PAIRS + 2 * PAD, LANES), jnp.float32),
            pltpu.VMEM((G + 2 * margin, PAIRS, LANES), jnp.float32),
            pltpu.VMEM((G, PAIRS, LANES), jnp.float32),
            pltpu.VMEM((G * G, G), jnp.float32),
            pltpu.SemaphoreType.DMA((len(far),)),
        ],
        compiler_params=pltpu.CompilerParams(vmem_limit_bytes=50 * 2**20),
        cost_estimate=pl.CostEstimate(
            flops=6 * 2048 * 640 * 384, bytes_accessed=5 * 2**20, transcendentals=0
        ),
        name="hamiltonian",
    )(place, *far)


def transposed_dot(a, b):
    return lax.dot_general(
        a, b, (((1,), (1,)), ((), ())), precision=precise, preferred_element_type=jnp.float32
    )


CORES = 2
LINES = 4


def natural_rows(flat_ref, natural_ref, core, gather):
    planes, orbitals, _ = natural_ref.shape
    groups = orbitals // (CORES * LINES)
    stride = CORES * LINES * planes
    for slot in range(CORES):
        for line in range(LINES):
            for plane in range(planes):
                inner = pl.ds((line * CORES + slot) * planes + plane, groups, stride=stride)
                outer = pl.ds((slot ^ core) * LINES + line, groups, stride=CORES * LINES)
                if gather:
                    natural_ref[plane, outer, :] = flat_ref[inner, :]
                else:
                    flat_ref[inner, :] = natural_ref[plane, outer, :]


def overlap_kernel(core_ref, flat_ref, natural_ref, packed_ref, square):
    for core in range(CORES):

        @pl.when(core_ref[0] == core)
        def _(core=core):
            natural_rows(flat_ref, natural_ref, core, True)

    planes, size, _ = natural_ref.shape
    half = planes // 2
    total = None
    for plane in range(0, half, 2):
        psi = jnp.concatenate([natural_ref[plane], natural_ref[plane + 1]], axis=1)
        images = jnp.concatenate(
            [natural_ref[half + plane], natural_ref[half + plane + 1]], axis=1
        )
        term = transposed_dot(psi, jnp.concatenate([psi, images], axis=0))
        total = term if total is None else total + term
    row = lax.broadcasted_iota(jnp.int32, (size, size), 0)
    column = lax.broadcasted_iota(jnp.int32, (size, size), 1)
    hamilton = total[:, size:]
    packed = jnp.where(row <= column, total[:, :size], hamilton)
    diagonal = jnp.where(row == column, hamilton, 0.0)
    chunks = size // ROWS
    parts = size // LANES
    lane_sum = 0.0
    for part in range(parts):
        lanes = slice(part * LANES, (part + 1) * LANES)
        square[part] = packed[:, lanes]
        lane_sum += diagonal[:, lanes]
        for line in range(ROWS):
            packed_ref[pl.ds(part * ROWS + line, chunks, stride=parts * ROWS + 1), :] = square[
                part, pl.ds(line, chunks, stride=ROWS), :
            ]
    packed_ref[pl.ds(parts * ROWS, chunks, stride=parts * ROWS + 1), :] = jnp.sum(
        lane_sum.reshape(chunks, ROWS, LANES), axis=1
    )


def overlap(core, arrived):
    rows, lanes = arrived.shape
    planes = 2 * ROWS
    size = rows // planes
    return pl.pallas_call(
        overlap_kernel,
        out_shape=(
            jax.ShapeDtypeStruct((planes, size, lanes), jnp.float32),
            jax.ShapeDtypeStruct((size // ROWS * (size // LANES * ROWS + 1), LANES), jnp.float32),
        ),
        in_specs=[smem(), vmem()],
        out_specs=(vmem(), vmem()),
        scratch_shapes=[pltpu.VMEM((size // LANES, size, LANES), jnp.float32)],
        compiler_params=pltpu.CompilerParams(vmem_limit_bytes=40 * 2**20),
        cost_estimate=pl.CostEstimate(
            flops=24 * 256 * 256 * 1024, bytes_accessed=4 * 2**20, transcendentals=0
        ),
        name="overlap",
    )(core, arrived)


def eliminate(work):
    size = work.shape[0]
    sub = lax.broadcasted_iota(jnp.int32, (ROWS, LANES), 0)

    def row_of(tile, j):
        return jnp.broadcast_to(tile[j : j + 1, :], tile.shape)

    for start in range(0, size, BLOCK):
        stop = start + BLOCK
        first = start // LANES * LANES
        last = size + (stop + LANES - 1) // LANES * LANES
        lanes = range(first, last, LANES)
        groups = BLOCK // ROWS
        tiles = [
            {c: work[start + g * ROWS : start + (g + 1) * ROWS, c : c + LANES] for c in lanes}
            for g in range(groups)
        ]
        for q in range(groups):
            base = start + q * ROWS
            home, at = base // LANES * LANES, base % LANES
            spread = [
                [
                    jnp.broadcast_to(tiles[g][home][:, at + m : at + m + 1], (ROWS, LANES))
                    for m in range(ROWS)
                ]
                if g >= q
                else None
                for g in range(groups)
            ]
            for j in range(0, ROWS, 2):
                first, second = spread[q][j], spread[q][j + 1]
                pivot, side, corner = row_of(first, j), row_of(first, j + 1), row_of(second, j + 1)
                root = lax.rsqrt(pivot)
                lower = side * root
                root2 = lax.rsqrt(pivot * corner - side * side) * (pivot * root)
                weight, weight2 = {}, {}
                for g in range(q, groups):
                    below, below2 = spread[g][j], spread[g][j + 1]
                    if g == q:
                        below = jnp.where(sub > j + 1, below, 0.0)
                        below2 = jnp.where(sub > j + 1, below2, 0.0)
                    weight[g] = below * root
                    weight2[g] = (below2 - weight[g] * lower) * root2

                def tops(tile):
                    top = row_of(tile, j) * root
                    return top, (row_of(tile, j + 1) - lower * top) * root2

                for m in range(j + 2, ROWS):
                    top, top2 = tops(spread[q][m])
                    for g in range(q, groups):
                        spread[g][m] = spread[g][m] - weight[g] * top - weight2[g] * top2
                for c in lanes:
                    top, top2 = tops(tiles[q][c])
                    for g in range(q, groups):
                        tiles[g][c] = tiles[g][c] - weight[g] * top - weight2[g] * top2
                    here = jnp.where(sub == j + 1, top2, tiles[q][c])
                    tiles[q][c] = jnp.where(sub == j, top, here)
        for g in range(groups):
            for c in lanes:
                work[start + g * ROWS : start + (g + 1) * ROWS, c : c + LANES] = tiles[g][c]
        if stop < size:
            low = stop // LANES * LANES
            done = work[start:stop, :]
            update = lax.dot_general(
                done[:, low:size],
                done[:, low:last],
                (((0,), (0,)), ((), ())),
                precision=precise,
                preferred_element_type=jnp.float32,
            )
            work[stop:, low:last] = work[stop:, low:last] - update[stop - low :, :]


def solve_kernel(
    cells,
    summed_ref,
    natural_ref,
    flat_ref,
    subspace_ref,
    work,
    mixed,
    square,
):
    def dot(a, b):
        return jnp.dot(a, b, precision=precise, preferred_element_type=jnp.float32)

    size = work.shape[0]
    parts = size // LANES
    chunks = size // ROWS
    stride = parts * ROWS + 1
    for part in range(parts):
        for line in range(ROWS):
            square[part, pl.ds(line, chunks, stride=ROWS), :] = summed_ref[
                pl.ds(part * ROWS + line, chunks, stride=stride), :
            ]
    diagonal = summed_ref[pl.ds(parts * ROWS, chunks, stride=stride), :]
    diagonal = jnp.broadcast_to(diagonal[:, None, :], (chunks, ROWS, LANES)).reshape(size, LANES)
    diagonal = jnp.concatenate([diagonal] * parts, axis=1) * (1.0 / cells)
    packed = jnp.concatenate([square[part] for part in range(parts)], axis=1) * (1.0 / cells)
    row = lax.broadcasted_iota(jnp.int32, (size, size), 0)
    column = lax.broadcasted_iota(jnp.int32, (size, size), 1)
    turned = packed.T
    on_diagonal = jnp.where(row == column, packed, 0.0)
    scale = lax.rsqrt(jnp.sum(on_diagonal, axis=0, keepdims=True))
    scale_down = lax.rsqrt(jnp.sum(on_diagonal, axis=1, keepdims=True))
    work[:, :size] = jnp.where(row <= column, packed, turned) * scale_down * scale
    work[:, size:] = jnp.where(row == column, scale, 0.0)
    hamilton = jnp.where(row > column, packed, jnp.where(row == column, diagonal, turned))
    eliminate(work)
    inverse = jnp.where(row >= column, work[:, size:], 0.0)
    subspace = transposed_dot(dot(inverse, hamilton), inverse)
    subspace_ref[...] = subspace
    planes = natural_ref.shape[0]
    half = planes // 2
    for plane in range(0, half, 2):
        both = [
            dot(
                inverse,
                jnp.concatenate([natural_ref[plane + k], natural_ref[half + plane + k]], axis=1),
            )
            for k in range(2)
        ]
        product = dot(subspace, jnp.concatenate([part[:, :LANES] for part in both], axis=1))
        for k, part in enumerate(both):
            mixed[plane + k] = part[:, :LANES]
            mixed[half + plane + k] = part[:, LANES:] - product[:, k * LANES : (k + 1) * LANES]
    natural_rows(flat_ref, mixed, 0, False)


def solve(summed, natural, cells):
    planes, size, lanes = natural.shape
    return pl.pallas_call(
        functools.partial(solve_kernel, cells),
        out_shape=(
            jax.ShapeDtypeStruct((planes * size, lanes), jnp.float32),
            jax.ShapeDtypeStruct((size, size), jnp.float32),
        ),
        in_specs=[vmem(), vmem()],
        out_specs=(vmem(), vmem()),
        scratch_shapes=[
            pltpu.VMEM((size, 2 * size), jnp.float32),
            pltpu.VMEM(natural.shape, jnp.float32),
            pltpu.VMEM((size // LANES, size, LANES), jnp.float32),
        ],
        compiler_params=pltpu.CompilerParams(vmem_limit_bytes=48 * 2**20),
        cost_estimate=pl.CostEstimate(
            flops=20_000_000_000, bytes_accessed=6 * 2**20, transcendentals=256
        ),
        name="solve",
    )(summed, natural)


def assemble_kernel(core_ref, arrived_ref, received_ref, first_ref, second_ref, staged, sems):
    core = core_ref[0]
    blocks = received_ref.shape[0]
    copies = []
    for which, out_ref in enumerate((first_ref, second_ref)):
        for own in range(2):
            slot = 2 * which + own
            if own:
                staged[slot] = arrived_ref[:, pl.ds((core * 2 + which) * ROWS, ROWS), :]
            else:
                staged[slot] = received_ref[:, which * ROWS : (which + 1) * ROWS, :]
            side = core if own else 1 - core
            copy = pltpu.make_async_copy(
                staged.at[slot], out_ref.at[pl.ds(side * blocks, blocks)], sems.at[slot]
            )
            copy.start()
            copies.append(copy)
    for copy in copies:
        copy.wait()


def assemble(core, arrived, received):
    blocks, _, lanes = received.shape
    out = jax.ShapeDtypeStruct((CORES * blocks, ROWS, lanes), jnp.float32)
    return pl.pallas_call(
        assemble_kernel,
        out_shape=(out, out),
        in_specs=[smem(), vmem(), vmem()],
        out_specs=(far_away(), far_away()),
        scratch_shapes=[
            pltpu.VMEM((4, blocks, ROWS, lanes), jnp.float32),
            pltpu.SemaphoreType.DMA((4,)),
        ],
        compiler_params=pltpu.CompilerParams(vmem_limit_bytes=32 * 2**20),
        cost_estimate=pl.CostEstimate(flops=0, bytes_accessed=4 * 2**20, transcendentals=0),
        name="assemble",
    )(core, arrived, received)


def exchange(blocks, groups, axes=AXES):
    return lax.all_to_all(
        blocks, axes, split_axis=0, concat_axis=0, tiled=True, axis_index_groups=groups
    )


class Layout:
    def __init__(self, orb, grp):
        self.x, self.core, self.y = 4, CORES, grp
        self.z = orb // (self.x * self.core)
        self.total = orb * grp

    def orb(self, z, x, core):
        return ((z % self.z) * self.x + x % self.x) * self.core + core % self.core

    def device(self, z, x, core, y):
        return self.orb(z, x, core) * self.y + y

    def places(self):
        return [
            (z, x, core)
            for z in range(self.z)
            for x in range(self.x)
            for core in range(self.core)
        ]

    def chips(self):
        return [
            [
                self.device(z, x, core, y)
                for z in range(self.z)
                for x in range(self.x)
                for y in range(self.y)
            ]
            for core in range(self.core)
        ]

    def planes(self):
        return [
            [
                self.device(z, x, core, y)
                for x in range(self.x)
                for core in range(self.core)
                for y in range(self.y)
            ]
            for z in range(self.z)
        ]

    def columns(self):
        return [
            [self.orb(z, x, core) for z in range(self.z)]
            for x in range(self.x)
            for core in range(self.core)
        ]

    def swap_cores(self, values):
        pairs = [(self.orb(z, x, c), self.orb(z, x, c + 1)) for z, x, c in self.places()]
        return lax.ppermute(values, "orb", pairs)


def reduce_slab(partial, layout):
    me = lax.axis_index("orb")
    core = me % layout.core
    x = me // layout.core % layout.x
    y = lax.axis_index("grp")

    def stage(values, dim, count, index, axis, pairs):
        total = lax.dynamic_index_in_dim(values, index, dim, keepdims=False)
        arrived = [
            lax.ppermute(
                lax.dynamic_index_in_dim(values, (index + k) % count, dim, keepdims=False),
                axis,
                pairs(k),
            )
            for k in range(1, count)
        ]
        for term in arrived:
            total = total + term
        return total

    def along(dx, dc):
        return lambda k: [
            (layout.orb(a, b, c), layout.orb(a, b + dx * k, c + dc * k))
            for a, b, c in layout.places()
        ]

    def lines(k):
        return [(i, (i + k) % layout.y) for i in range(layout.y)]

    values = partial.reshape(layout.z, layout.x, layout.core, layout.y, -1, LANES)
    values = stage(values, 2, layout.core, core, "orb", along(0, 1))
    values = stage(values, 2, layout.y, y, "grp", lines)
    return stage(values, 1, layout.x, x, "orb", along(1, 0))


def sum_everywhere(chunks, slabs, layout):
    count = layout.total // layout.z
    flat = chunks.reshape(count, 1, -1)
    length = flat.shape[2]
    part = jnp.sum(exchange(flat, layout.planes()), axis=0, keepdims=True)
    part = jnp.broadcast_to(part, (layout.z, 1, length))
    slabs = slabs.reshape(layout.z, 1, -1)
    part = exchange(jnp.concatenate([part, slabs], axis=2), layout.columns(), "orb")
    total = jnp.sum(part, axis=0)
    everywhere = jnp.broadcast_to(total[None, :, :length], (count, 1, length))
    return exchange(everywhere, layout.planes()).reshape(chunks.shape), total[:, length:]


def on_device(layout, orbitals, potential, occupation, region_bounds):
    cell_total = orbitals.shape[1]
    orb, grp = lax.axis_index("orb"), lax.axis_index("grp")
    position = orb * layout.y + grp
    core = orb % layout.core
    place = jnp.stack([position, core]).astype(jnp.int32)
    core = core.reshape(1).astype(jnp.int32)
    keep, give, density_part = apply_hamiltonian(
        place, region_bounds, orbitals.reshape(G, PAIRS, LANES), potential
    )
    scale = lax.dynamic_slice_in_dim(occupation, position, 1, 0) / layout.total
    sent = jnp.concatenate([keep, layout.swap_cores(give)], axis=1)
    slabs = reduce_slab(scale * density_part, layout)
    arrived = exchange(sent, layout.chips())
    arrived, slabs = lax.optimization_barrier((arrived, slabs))
    natural, packed = overlap(core, arrived.reshape(-1, LANES))
    summed, density = sum_everywhere(packed, slabs, layout)
    mixed, subspace = solve(summed, natural, cell_total)
    back = exchange(mixed.reshape(-1, 4 * ROWS, LANES), layout.chips())
    back, density = lax.optimization_barrier((back, density.reshape(-1, G)))
    other = lax.dynamic_slice_in_dim(back, (1 - core[0]) * 2 * ROWS, 2 * ROWS, 1)
    orthonormal, gradient = assemble(core, back, layout.swap_cores(other))
    return (
        orthonormal.reshape(1, cell_total),
        gradient.reshape(1, cell_total),
        subspace,
        density,
    )


def solution(mesh):
    in_specs = (P(AXES, None), P(), P(), P())
    out_specs = (P(AXES, None), P(AXES, None), P(), P(AXES, None))
    step = functools.partial(on_device, Layout(mesh.shape["orb"], mesh.shape["grp"]))
    return jax.shard_map(
        step, mesh=mesh, in_specs=in_specs, out_specs=out_specs, check_vma=False
    )
```
